32 devices in a mesh: dp: 8 (over z, x), shard: 4 (over y, core).
Axes of the slice: x: 2, y: 2, z: 4, core: 2. Of those that a mesh axis runs over, the one named last changes fastest.
Arguments:
- tokens: bfloat16 [32768, 1024], P(('dp', 'shard')), may hold values from -6 to 6
- cotangent: bfloat16 [32768, 1024], P(('dp', 'shard')), may hold values from -6 to 6
- segment_ids: int32 [32768], P(('dp', 'shard')), may hold values from 0 to 5, as said below
- group_counts: int32 [8], replicated, may hold values from 50 to 400
- master_qkv: float32 [1024, 3072], P('dp', 'shard'), may hold values from -0.1875 to 0.1875
- master_out: float32 [1024, 1024], P('dp', 'shard'), may hold values from -1 to 1
- master_up: float32 [1024, 4096], P('dp', 'shard'), may hold values from -0.1875 to 0.1875
- master_down: float32 [4096, 1024], P('dp', 'shard'), may hold values from -0.09375 to 0.09375
- moment_qkv: float32 [1024, 3072], P('dp', 'shard')
- moment_out: float32 [1024, 1024], P('dp', 'shard')
- moment_up: float32 [1024, 4096], P('dp', 'shard')
- moment_down: float32 [4096, 1024], P('dp', 'shard')
- square_qkv: float32 [1024, 3072], P('dp', 'shard'), as said below
- square_out: float32 [1024, 1024], P('dp', 'shard'), as said below
- square_up: float32 [1024, 4096], P('dp', 'shard'), as said below
- square_down: float32 [4096, 1024], P('dp', 'shard'), as said below
- norm_params: float32 [4, 1024], replicated, as said below
- norm_moment: float32 [4, 1024], replicated
- norm_square: float32 [4, 1024], replicated, as said below
Outputs:
- block_out: bfloat16 [32768, 1024], P(('dp', 'shard'))
- input_grad: float32 [32768, 1024], P(('dp', 'shard'))
- grad_qkv: float32 [1024, 3072], P('dp', 'shard')
- grad_out: float32 [1024, 1024], P('dp', 'shard')
- grad_up: float32 [1024, 4096], P('dp', 'shard')
- grad_down: float32 [4096, 1024], P('dp', 'shard')
- new_qkv: float32 [1024, 3072], P('dp', 'shard')
- new_out: float32 [1024, 1024], P('dp', 'shard')
- new_up: float32 [1024, 4096], P('dp', 'shard')
- new_down: float32 [4096, 1024], P('dp', 'shard')
- new_moment_qkv: float32 [1024, 3072], P('dp', 'shard')
- new_moment_out: float32 [1024, 1024], P('dp', 'shard')
- new_moment_up: float32 [1024, 4096], P('dp', 'shard')
- new_moment_down: float32 [4096, 1024], P('dp', 'shard')
- new_square_qkv: float32 [1024, 3072], P('dp', 'shard')
- new_square_out: float32 [1024, 1024], P('dp', 'shard')
- new_square_up: float32 [1024, 4096], P('dp', 'shard')
- new_square_down: float32 [4096, 1024], P('dp', 'shard')
- copy_qkv: bfloat16 [1024, 3072], P('dp', 'shard')
- copy_out: bfloat16 [1024, 1024], P('dp', 'shard')
- copy_up: bfloat16 [1024, 4096], P('dp', 'shard')
- copy_down: bfloat16 [4096, 1024], P('dp', 'shard')
- norm_grad: float32 [4, 1024], replicated
- new_norm: float32 [4, 1024], replicated
- new_norm_moment: float32 [4, 1024], replicated
- new_norm_square: float32 [4, 1024], replicated
The draws below stay inside these ranges and needn't reach their ends.
Inputs may be any that keep to these rules, and one draw needn't show every extreme that they name: `segment_ids`: in each packed row of 256 tokens the ids number whole images in order, with the padding tokens as one more id placed before, between or after whole images; every row of one group holds images of 50 tokens or every row holds images of 145 tokens, and both kinds of group occur. `norm_params`: gains near one, shifts near zero. `norm_square`: every entry positive. `square_qkv`: every entry positive. `square_out`: every entry positive. `square_up`: every entry positive. `square_down`: every entry positive.
All inputs are finite; a program needn't handle non-finite values.
Results may differ from the reference program's by a relative error of at most 0.012.
Values may be sent and summed in bfloat16 or wider, within the bound.
No kernel may reach another device: no remote copies, remote signals or barrier semaphores. Data moves between devices by JAX's collectives and lax.ppermute only.
A program may use at most 256 MiB of HBM per device.

```python
import math
import jax
import jax.numpy as jnp
from jax import lax

D = 1024
FF = 4096
HEADS = 16
HD = 64
SEQ = 256
IMG_SMALL = 50
IMG_LARGE = 145
STEP = 3
GROUP_TOK = 4096
GROUPS = 8
TOKENS = 32768


def typical_moment(key, extent, typical):
    return jax.random.normal(key, extent, jnp.float32) * (typical * math.sqrt(TOKENS))


def typical_square(key, extent, typical):
    spread = jax.random.uniform(key, extent, jnp.float32, math.log(0.5), math.log(4.0))
    return jnp.exp(spread) * (typical * typical * TOKENS)


def norm_levels():
    return jnp.array([2.8, 2.8, 0.7, 0.7], jnp.float32)[:, None]


def draw_segment_ids(key, part):
    key_label = jax.random.fold_in(key, 101)
    key_pick = jax.random.fold_in(key, 102)
    key_slot = jax.random.fold_in(key, 103)
    labels = jax.random.randint(key_label, (GROUPS,), 0, 2)
    chosen = jax.random.randint(key_pick, (), 0, GROUPS)
    group_index = jnp.arange(GROUPS)
    labels = jnp.where(group_index == chosen, 0, labels)
    labels = jnp.where(group_index == (chosen + 1) % GROUPS, 1, labels)
    rows_all = TOKENS // SEQ
    row_group = jnp.arange(rows_all) // (GROUP_TOK // SEQ)
    row_label = labels[row_group]
    length = jnp.where(row_label == 1, IMG_LARGE, IMG_SMALL)[:, None]
    images = SEQ // length
    padding = SEQ - images * length
    slot = jax.random.randint(key_slot, (rows_all, 1), 0, images + 1)
    positions = jnp.arange(SEQ)[None, :]
    pad_start = slot * length
    numbered = jnp.where(positions < pad_start, positions // length, jnp.where(positions < pad_start + padding, images, (positions - padding) // length))
    return numbered.astype(jnp.int32).reshape(TOKENS)


def draw_norm_params(key, part):
    gains = jax.random.uniform(jax.random.fold_in(key, 201), (4, D), jnp.float32, 0.6, 1.4)
    shifts = 0.1 * jax.random.normal(jax.random.fold_in(key, 202), (4, D), jnp.float32)
    row_index = jnp.arange(4)[:, None]
    return jnp.where(row_index % 2 == 0, gains, shifts)


def draw_norm_moment(key, part):
    return jax.random.normal(jax.random.fold_in(key, 211), (4, D), jnp.float32) * (norm_levels() * math.sqrt(TOKENS))


def draw_norm_square(key, part):
    spread = jax.random.uniform(jax.random.fold_in(key, 212), (4, D), jnp.float32, math.log(0.5), math.log(4.0))
    return jnp.exp(spread) * (norm_levels() * norm_levels() * TOKENS)


def draw_moment_qkv(key, part):
    return typical_moment(jax.random.fold_in(key, 301), (D, 3 * D), 1.6)


def draw_moment_out(key, part):
    return typical_moment(jax.random.fold_in(key, 302), (D, D), 0.28)


def draw_moment_up(key, part):
    return typical_moment(jax.random.fold_in(key, 303), (D, FF), 0.33)


def draw_moment_down(key, part):
    return typical_moment(jax.random.fold_in(key, 304), (FF, D), 0.65)


def draw_square_qkv(key, part):
    return typical_square(jax.random.fold_in(key, 401), (D, 3 * D), 1.6)


def draw_square_out(key, part):
    return typical_square(jax.random.fold_in(key, 402), (D, D), 0.28)


def draw_square_up(key, part):
    return typical_square(jax.random.fold_in(key, 403), (D, FF), 0.33)


def draw_square_down(key, part):
    return typical_square(jax.random.fold_in(key, 404), (FF, D), 0.65)


def plant(entries, own_key, least, top_value):
    longest = entries.shape.index(max(entries.shape))
    spots = []
    for shift in (0, 1):
        where = [jax.random.randint(jax.random.fold_in(own_key, axis), (), 0, length) for axis, length in enumerate(entries.shape)]
        where[longest] = (where[longest] + shift) % entries.shape[longest]
        spots.append(tuple(where))
    return entries.at[spots[0]].set(least).at[spots[1]].set(top_value)


def block_scale(key, shape, pieces, low, top_value):
    loudness, own = 1.0, jax.random.fold_in(key, 6)
    for dim, parts in pieces:
        heights = jnp.exp(jax.random.uniform(jax.random.fold_in(own, dim), (parts,), jnp.float32, low / len(pieces), top_value / len(pieces)))
        loudness = loudness * jnp.repeat(heights, shape[dim] // parts).reshape([-1 if axis == dim else 1 for axis in range(len(shape))])
    return loudness


def bell_draw(rng, shape, width, limit, cuts=(), dtype=jnp.bfloat16):
    level = block_scale(rng, shape, cuts, -0.22, 0.18) if cuts else 1.0
    values = jax.random.normal(rng, shape, jnp.float32) * width * level
    return jnp.minimum(jnp.maximum(values, -limit), limit).astype(dtype)


def setup_inputs(seed: int = 0) -> dict:
    seeds = jax.random.split(jax.random.key(seed), 20)
    tokens = bell_draw(seeds[0], (TOKENS, D), 1.0, 6.0, ((0, 32),))
    cotangent = bell_draw(seeds[1], (TOKENS, D), 1.0, 6.0, ((0, 32),))
    segment_ids = draw_segment_ids(jax.random.fold_in(seeds[19], 71), 0)
    group_counts = plant(jax.random.randint(seeds[3], (GROUPS,), 50, 401), jax.random.fold_in(seeds[3], 1), 50, 400).astype(jnp.int32)
    master_qkv = bell_draw(seeds[4], (D, 3 * D), D ** -0.5, 0.1875, ((0, 8), (1, 4)), jnp.float32)
    master_out = bell_draw(seeds[5], (D, D), (D // 32) ** -0.5, 1.0, ((0, 8), (1, 4)), jnp.float32)
    master_up = bell_draw(seeds[6], (D, FF), D ** -0.5, 0.1875, ((0, 8), (1, 4)), jnp.float32)
    master_down = bell_draw(seeds[7], (FF, D), FF ** -0.5, 0.09375, ((0, 8), (1, 4)), jnp.float32)
    moment_qkv = draw_moment_qkv(jax.random.fold_in(seeds[19], 71), 0)
    moment_out = draw_moment_out(jax.random.fold_in(seeds[19], 71), 0)
    moment_up = draw_moment_up(jax.random.fold_in(seeds[19], 71), 0)
    moment_down = draw_moment_down(jax.random.fold_in(seeds[19], 71), 0)
    square_qkv = draw_square_qkv(jax.random.fold_in(seeds[19], 71), 0)
    square_out = draw_square_out(jax.random.fold_in(seeds[19], 71), 0)
    square_up = draw_square_up(jax.random.fold_in(seeds[19], 71), 0)
    square_down = draw_square_down(jax.random.fold_in(seeds[19], 71), 0)
    norm_params = draw_norm_params(jax.random.fold_in(seeds[19], 71), 0)
    norm_moment = draw_norm_moment(jax.random.fold_in(seeds[19], 71), 0)
    norm_square = draw_norm_square(jax.random.fold_in(seeds[19], 71), 0)
    return {"tokens": tokens, "cotangent": cotangent, "segment_ids": segment_ids, "group_counts": group_counts, "master_qkv": master_qkv, "master_out": master_out, "master_up": master_up, "master_down": master_down, "moment_qkv": moment_qkv, "moment_out": moment_out, "moment_up": moment_up, "moment_down": moment_down, "square_qkv": square_qkv, "square_out": square_out, "square_up": square_up, "square_down": square_down, "norm_params": norm_params, "norm_moment": norm_moment, "norm_square": norm_square}


NORM_EPSILON = 1e-06
BETA_FIRST = 0.5
BETA_SECOND = 0.5
ADAM_EPSILON = 1e-08
RATE_MATRIX = 0.02
RATE_OUTPUT = 0.1
RATE_NORMS = 0.3
WEIGHT_DECAY = 0.01
MASK_FILL = -1000000000.0

@jax.custom_vjp
def low(v):
    return lax.optimization_barrier(v.astype(jnp.bfloat16)).astype(jnp.float32)

@jax.custom_vjp
def low_back(v):
    return v

def low_keep(v):
    return (low(v), None)

def low_pass(kept, grad):
    return (grad,)

def back_keep(v):
    return (v, None)

def back_low(kept, grad):
    return (low(grad),)
low.defvjp(low_keep, low_pass)
low_back.defvjp(back_keep, back_low)

def dense(first_op, second_op):
    return jnp.dot(first_op, second_op, precision=lax.Precision.HIGHEST)

def layer_norm(values, scales, shifts):
    centred = values - lax.optimization_barrier(jnp.mean(values, axis=-1, keepdims=True))
    variance = lax.optimization_barrier(jnp.mean(centred * centred, axis=-1, keepdims=True))
    return centred * lax.rsqrt(variance + NORM_EPSILON) * scales + shifts

def block_forward(values_in, weight_qkv, weight_out, weight_up, weight_down, params, segment):
    packed = values_in.shape[0] // SEQ
    scaling = 1.0 / math.sqrt(HD)
    first_in = low(layer_norm(values_in, params[0], params[1]))
    joined = low(low_back(dense(first_in, weight_qkv)))
    joined = joined.reshape(packed, SEQ, 3, HEADS, HD)
    query_rows = joined[:, :, 0]
    key_rows = joined[:, :, 1]
    value_rows = joined[:, :, 2]
    scores = low_back(scaling * jnp.einsum('rqhd,rkhd->rhqk', query_rows, key_rows, precision=lax.Precision.HIGHEST))
    segments = segment.reshape(packed, SEQ)
    same_image = (segments[:, :, None] == segments[:, None, :])[:, None]
    masked = jnp.where(same_image, scores, MASK_FILL)
    attn_probs = jax.nn.softmax(masked, axis=-1)
    mixed_heads = jnp.einsum('rhqk,rkhd->rqhd', low(attn_probs), value_rows, precision=lax.Precision.HIGHEST)
    mixed_heads = low(low_back(mixed_heads.reshape(packed * SEQ, HEADS * HD)))
    attention = low_back(dense(mixed_heads, weight_out))
    residual = values_in + attention
    second_in = low(layer_norm(residual, params[2], params[3]))
    upward = low_back(dense(second_in, weight_up))
    hidden = low(jax.nn.gelu(upward, approximate=False))
    return residual + dense(hidden, weight_down)

def adam_update(master, moment, square, gradient, rate):
    new_moment = BETA_FIRST * moment + (1.0 - BETA_FIRST) * gradient
    new_square = BETA_SECOND * square + (1.0 - BETA_SECOND) * gradient * gradient
    bias_first = 1.0 - BETA_FIRST ** STEP
    bias_second = 1.0 - BETA_SECOND ** STEP
    update = new_moment / bias_first / (jnp.sqrt(new_square / bias_second) + ADAM_EPSILON)
    new_master = master - rate * (update + WEIGHT_DECAY * master)
    return (new_master, new_moment, new_square)

def reference(tokens, cotangent, segment_ids, group_counts, master_qkv, master_out, master_up, master_down, moment_qkv, moment_out, moment_up, moment_down, square_qkv, square_out, square_up, square_down, norm_params, norm_moment, norm_square):
    rounded = (low(master_qkv), low(master_out), low(master_up), low(master_down))
    counts = group_counts.astype(jnp.float32)
    factors = counts * GROUPS / jnp.sum(counts)
    inputs_all = tokens.astype(jnp.float32).reshape(GROUPS, GROUP_TOK, D)
    cotangent_all = cotangent.astype(jnp.float32).reshape(GROUPS, GROUP_TOK, D)
    segments_all = segment_ids.reshape(GROUPS, GROUP_TOK)

    def group_step(running, slices):
        inputs, cotangent_rows, segment, factor = slices

        def forward(values_in, weight_qkv, weight_out, weight_up, weight_down, params):
            return block_forward(values_in, weight_qkv, weight_out, weight_up, weight_down, params, segment)
        outputs, pullback = jax.vjp(forward, inputs, rounded[0], rounded[1], rounded[2], rounded[3], norm_params)
        gradients = pullback(cotangent_rows)
        running = (running[0] + factor * gradients[1], running[1] + factor * gradients[2], running[2] + factor * gradients[3], running[3] + factor * gradients[4], running[4] + factor * gradients[5])
        return (running, (outputs.astype(jnp.bfloat16), gradients[0]))
    initial = (jnp.zeros((D, 3 * D), jnp.float32), jnp.zeros((D, D), jnp.float32), jnp.zeros((D, FF), jnp.float32), jnp.zeros((FF, D), jnp.float32), jnp.zeros((4, D), jnp.float32))
    totals, (outputs, input_grads) = lax.scan(group_step, initial, (inputs_all, cotangent_all, segments_all, factors))
    block_out = outputs.reshape(TOKENS, D)
    input_grad = input_grads.reshape(TOKENS, D)
    grad_qkv, grad_out, grad_up, grad_down, norm_grad = totals
    new_qkv, new_moment_qkv, new_square_qkv = adam_update(master_qkv, moment_qkv, square_qkv, grad_qkv, RATE_MATRIX)
    new_out, new_moment_out, new_square_out = adam_update(master_out, moment_out, square_out, grad_out, RATE_OUTPUT)
    new_up, new_moment_up, new_square_up = adam_update(master_up, moment_up, square_up, grad_up, RATE_MATRIX)
    new_down, new_moment_down, new_square_down = adam_update(master_down, moment_down, square_down, grad_down, RATE_MATRIX)
    new_norm, new_norm_moment, new_norm_square = adam_update(norm_params, norm_moment, norm_square, norm_grad, RATE_NORMS)
    return (block_out, input_grad, grad_qkv, grad_out, grad_up, grad_down, new_qkv, new_out, new_up, new_down, new_moment_qkv, new_moment_out, new_moment_up, new_moment_down, new_square_qkv, new_square_out, new_square_up, new_square_down, new_qkv.astype(jnp.bfloat16), new_out.astype(jnp.bfloat16), new_up.astype(jnp.bfloat16), new_down.astype(jnp.bfloat16), norm_grad, new_norm, new_norm_moment, new_norm_square)
```

```python
import functools
import math

import jax
import jax.numpy as jnp
from jax import lax
from jax.experimental import pallas as pl
from jax.experimental.pallas import tpu as pltpu
from jax.sharding import PartitionSpec as P

D = 1024
HEADS = 16
HD = 64
SEQ = 256
STEP = 3


NORM_EPSILON = 1e-06
BETA_FIRST = 0.5
BETA_SECOND = 0.5
ADAM_EPSILON = 1e-08
RATE_MATRIX = 0.02
RATE_OUTPUT = 0.1
RATE_NORMS = 0.3
WEIGHT_DECAY = 0.01
MASK_FILL = -1000000000.0
TRANSPOSED = (((1,), (1,)), ((), ()))
LEADING = (((0,), (0,)), ((), ()))


def layer_norm(values, scales, shifts):
    centred = values - jnp.mean(values, axis=-1, keepdims=True)
    variance = jnp.mean(centred * centred, axis=-1, keepdims=True)
    return centred * lax.rsqrt(variance + NORM_EPSILON) * scales + shifts


def gelu_exact(values):
    return jax.nn.gelu(values, approximate=False)


def adam_update(master, moment, square, gradient, rate):
    new_moment = BETA_FIRST * moment + (1.0 - BETA_FIRST) * gradient
    new_square = BETA_SECOND * square + (1.0 - BETA_SECOND) * gradient * gradient
    bias_first = 1.0 - BETA_FIRST**STEP
    bias_second = 1.0 - BETA_SECOND**STEP
    update = new_moment / bias_first / (jnp.sqrt(new_square / bias_second) + ADAM_EPSILON)
    new_master = master - rate * (update + WEIGHT_DECAY * master)
    return (new_master, new_moment, new_square)


def coordinates(index_dp, index_shard):
    return index_dp // 2, index_dp % 2, index_shard // 2, index_shard % 2


def links(dp, shard):
    depth = dp // 2
    x_pairs = [(i, i ^ 1) for i in range(dp)]
    y_pairs = [(i, i ^ 2) for i in range(shard)]
    c_pairs = [(i, i ^ 1) for i in range(shard)]

    def pull(k):
        return [((i // 2 + k) % depth * 2 + i % 2, i) for i in range(dp)]

    def push(k):
        return [(i, j) for j, i in pull(k)]

    return depth, x_pairs, y_pairs, c_pairs, pull, push


def gather_pieces(piece, dp, shard):
    depth, x_pairs, y_pairs, c_pairs, pull, _ = links(dp, shard)
    half = depth // 2
    near = jnp.stack([piece] + [lax.ppermute(piece, "dp", pull(k)) for k in range(1, depth)])
    over_x = lax.ppermute(near, "dp", x_pairs)
    over_y = lax.ppermute(near, "shard", y_pairs)
    far_a = lax.ppermute(over_x[:half], "shard", y_pairs)
    far_b = lax.ppermute(over_y[half:], "dp", x_pairs)
    mine = [near, over_x, over_y, far_a, far_b]
    return mine + [lax.ppermute(v, "shard", c_pairs) for v in mine]


def piece_places(depth):
    half = depth // 2
    places = []
    for core in (0, 1):
        base = core * 5
        places += [(base, k, k, 0, 0, core) for k in range(depth)]
        places += [(base + 1, k, k, 1, 0, core) for k in range(depth)]
        places += [(base + 2, k, k, 0, 1, core) for k in range(depth)]
        places += [(base + 3, k, k, 1, 1, core) for k in range(half)]
        places += [(base + 4, k - half, k, 1, 1, core) for k in range(half, depth)]
    return places


def assemble(pieces, dp, shard):
    depth = dp // 2
    rows, columns = pieces[0].shape[1:]
    places = piece_places(depth)

    def kernel(*refs):
        ins, out, sems = refs[:10], refs[10], refs[11]
        z, x, y, c = coordinates(lax.axis_index("dp"), lax.axis_index("shard"))
        copies = []
        for n, (i, j, dz, dx, dy, dc) in enumerate(places):
            row = (lax.rem(z + dz, depth) * 2 + lax.rem(x + dx, 2)) * rows
            column = (lax.rem(y + dy, 2) * 2 + lax.rem(c + dc, 2)) * columns
            target = out.at[pl.ds(pl.multiple_of(row, rows), rows), pl.ds(pl.multiple_of(column, columns), columns)]
            copies.append(pltpu.make_async_copy(ins[i].at[j], target, sems.at[n]))
        for copy in copies:
            copy.start()
        for copy in copies:
            copy.wait()

    return pl.pallas_call(
        kernel,
        out_shape=jax.ShapeDtypeStruct((rows * dp, columns * shard), pieces[0].dtype),
        in_specs=[pl.BlockSpec(memory_space=pl.ANY)] * 10,
        out_specs=pl.BlockSpec(memory_space=pltpu.VMEM),
        scratch_shapes=[pltpu.SemaphoreType.DMA((len(places),))],
        compiler_params=pltpu.CompilerParams(vmem_limit_bytes=32 * 2**20),
    )(*pieces)


def spread(whole, dp, shard):
    depth = dp // 2
    rows, columns = whole.shape[0] // dp, whole.shape[1] // shard
    shape = jax.ShapeDtypeStruct((2, 2, depth, rows, columns), whole.dtype)

    def kernel(source, near, far, sems):
        z, x, y, c = coordinates(lax.axis_index("dp"), lax.axis_index("shard"))
        copies = []
        for dc, out in enumerate((near, far)):
            for dy in range(2):
                for dx in range(2):
                    for dz in range(depth):
                        row = (lax.rem(z + dz, depth) * 2 + lax.rem(x + dx, 2)) * rows
                        column = (lax.rem(y + dy, 2) * 2 + lax.rem(c + dc, 2)) * columns
                        block = source.at[pl.ds(pl.multiple_of(row, rows), rows), pl.ds(pl.multiple_of(column, columns), columns)]
                        copies.append(pltpu.make_async_copy(block, out.at[dy, dx, dz], sems.at[len(copies)]))
        for copy in copies:
            copy.start()
        for copy in copies:
            copy.wait()

    return pl.pallas_call(
        kernel,
        out_shape=(shape, shape),
        in_specs=[pl.BlockSpec(memory_space=pltpu.VMEM)],
        out_specs=(pl.BlockSpec(memory_space=pl.ANY),) * 2,
        scratch_shapes=[pltpu.SemaphoreType.DMA((dp * shard,))],
        compiler_params=pltpu.CompilerParams(vmem_limit_bytes=32 * 2**20),
    )(whole)


def scatter_pieces(near, far, dp, shard):
    depth, x_pairs, y_pairs, c_pairs, _, push = links(dp, shard)
    half = depth // 2

    def wide(v):
        return v.astype(jnp.float32)

    def thin(v):
        return v.astype(jnp.bfloat16)

    both = wide(near) + wide(lax.ppermute(far, "shard", c_pairs))
    far_a = lax.ppermute(thin(both[1, 1, :half]), "shard", y_pairs)
    far_b = lax.ppermute(thin(both[1, 1, half:]), "dp", x_pairs)
    for_x = jnp.concatenate([both[0, 1, :half] + wide(far_a), both[0, 1, half:]])
    for_y = jnp.concatenate([both[1, 0, :half], both[1, 0, half:] + wide(far_b)])
    here = both[0, 0] + wide(lax.ppermute(thin(for_x), "dp", x_pairs)) + wide(lax.ppermute(thin(for_y), "shard", y_pairs))
    total = here[0]
    for k in range(1, depth):
        total = total + wide(lax.ppermute(thin(here[k]), "dp", push(k)))
    return total


def local(
    dp,
    shard,
    tokens,
    cotangent,
    segment_ids,
    group_counts,
    master_qkv,
    master_out,
    master_up,
    master_down,
    moment_qkv,
    moment_out,
    moment_up,
    moment_down,
    square_qkv,
    square_out,
    square_up,
    square_down,
    norm_params,
    norm_moment,
    norm_square,
):
    published = [
        assemble(gather_pieces(w.astype(jnp.bfloat16), dp, shard), dp, shard)
        for w in (master_qkv, master_out, master_up, master_down)
    ]

    def project(activations, position):
        return jnp.dot(activations, published[position], preferred_element_type=jnp.float32)

    def project_back(gradient, position):
        return lax.dot_general(
            gradient, published[position], TRANSPOSED, preferred_element_type=jnp.float32
        )

    scaling = 1.0 / math.sqrt(HD)
    inputs = tokens.astype(jnp.float32)
    token_count = inputs.shape[0]
    packed = token_count // SEQ
    normed_one, norm_one_pull = jax.vjp(layer_norm, inputs, norm_params[0], norm_params[1])
    first_in = normed_one.astype(jnp.bfloat16)
    joined = project(first_in, 0).astype(jnp.bfloat16).reshape(packed, SEQ, 3, HEADS, HD)
    query_rows = joined[:, :, 0]
    key_rows = joined[:, :, 1]
    value_rows = joined[:, :, 2]
    segments = segment_ids.reshape(packed, SEQ)
    same_image = (segments[:, :, None] == segments[:, None, :])[:, None]

    def masked_scores():
        raw_scores = (
            jnp.einsum("rqhd,rkhd->rhqk", query_rows, key_rows, preferred_element_type=jnp.float32)
            * scaling
        )
        return jnp.where(same_image, raw_scores, MASK_FILL)

    scores = masked_scores()
    row_max = jnp.max(scores, axis=-1, keepdims=True)
    log_total = row_max + jnp.log(jnp.sum(jnp.exp(scores - row_max), axis=-1, keepdims=True))
    attn_probs = jnp.exp(scores - log_total)
    mixed_heads = jnp.einsum(
        "rhqk,rkhd->rqhd",
        attn_probs.astype(jnp.bfloat16),
        value_rows,
        preferred_element_type=jnp.float32,
    )
    mixed_heads = mixed_heads.reshape(token_count, HEADS * HD).astype(jnp.bfloat16)
    attention = project(mixed_heads, 1)
    residual = inputs + attention
    normed_two, norm_two_pull = jax.vjp(layer_norm, residual, norm_params[2], norm_params[3])
    second_in = normed_two.astype(jnp.bfloat16)
    upward = project(second_in, 2)
    hidden_full, gelu_pull = jax.vjp(gelu_exact, upward)
    hidden = hidden_full.astype(jnp.bfloat16)
    block_out = (residual + project(hidden, 3)).astype(jnp.bfloat16)
    grad_hidden = project_back(cotangent, 3)
    grad_upward = gelu_pull(grad_hidden)[0].astype(jnp.bfloat16)
    grad_second = project_back(grad_upward, 2)
    grad_resid_part, grad_gain_two, grad_shift_two = norm_two_pull(grad_second)
    grad_residual = cotangent.astype(jnp.float32) + grad_resid_part
    grad_attention = grad_residual.astype(jnp.bfloat16)
    grad_mixed = (
        project_back(grad_attention, 1).astype(jnp.bfloat16).reshape(packed, SEQ, HEADS, HD)
    )
    probs_again = jnp.exp(masked_scores() - log_total)
    grad_probs = jnp.einsum(
        "rqhd,rkhd->rhqk", grad_mixed, value_rows, preferred_element_type=jnp.float32
    )
    row_delta = jnp.sum(probs_again * grad_probs, axis=-1, keepdims=True)
    grad_scores = (probs_again * (grad_probs - row_delta)).astype(jnp.bfloat16)
    grad_query = (
        jnp.einsum("rhqk,rkhd->rqhd", grad_scores, key_rows, preferred_element_type=jnp.float32)
        * scaling
    )
    grad_key = (
        jnp.einsum("rhqk,rqhd->rkhd", grad_scores, query_rows, preferred_element_type=jnp.float32)
        * scaling
    )
    grad_value = jnp.einsum(
        "rhqk,rqhd->rkhd",
        probs_again.astype(jnp.bfloat16),
        grad_mixed,
        preferred_element_type=jnp.float32,
    )
    grad_joined = jnp.stack([grad_query, grad_key, grad_value], axis=2).reshape(token_count, 3 * D)
    grad_joined = grad_joined.astype(jnp.bfloat16)
    grad_first = project_back(grad_joined, 0)
    grad_in_part, grad_gain_one, grad_shift_one = norm_one_pull(grad_first)
    input_grad = grad_residual + grad_in_part
    counts = group_counts.astype(jnp.float32)
    own_count = jnp.sum(jnp.where(jnp.arange(counts.shape[0]) == lax.axis_index("dp"), counts, 0.0))
    factor = own_count * counts.shape[0] / jnp.sum(counts)

    def reduce_whole(activations, gradient):
        partial = factor * lax.dot_general(
            activations, gradient, LEADING, preferred_element_type=jnp.float32
        )
        return scatter_pieces(*spread(partial.astype(jnp.bfloat16), dp, shard), dp, shard)

    owned = (
        reduce_whole(first_in, grad_joined),
        reduce_whole(mixed_heads, grad_attention),
        reduce_whole(second_in, grad_upward),
        reduce_whole(hidden, cotangent),
    )
    grad_qkv = owned[0]
    grad_out = owned[1]
    grad_up = owned[2]
    grad_down = owned[3]
    norm_terms = jnp.stack([grad_gain_one, grad_shift_one, grad_gain_two, grad_shift_two]) * factor
    norm_grad = lax.psum(norm_terms, ("dp", "shard"))
    new_qkv, new_moment_qkv, new_square_qkv = adam_update(
        master_qkv, moment_qkv, square_qkv, grad_qkv, RATE_MATRIX
    )
    new_out, new_moment_out, new_square_out = adam_update(
        master_out, moment_out, square_out, grad_out, RATE_OUTPUT
    )
    new_up, new_moment_up, new_square_up = adam_update(
        master_up, moment_up, square_up, grad_up, RATE_MATRIX
    )
    new_down, new_moment_down, new_square_down = adam_update(
        master_down, moment_down, square_down, grad_down, RATE_MATRIX
    )
    new_norm, new_norm_moment, new_norm_square = adam_update(
        norm_params, norm_moment, norm_square, norm_grad, RATE_NORMS
    )
    return (
        block_out,
        input_grad,
        grad_qkv,
        grad_out,
        grad_up,
        grad_down,
        new_qkv,
        new_out,
        new_up,
        new_down,
        new_moment_qkv,
        new_moment_out,
        new_moment_up,
        new_moment_down,
        new_square_qkv,
        new_square_out,
        new_square_up,
        new_square_down,
        new_qkv.astype(jnp.bfloat16),
        new_out.astype(jnp.bfloat16),
        new_up.astype(jnp.bfloat16),
        new_down.astype(jnp.bfloat16),
        norm_grad,
        new_norm,
        new_norm_moment,
        new_norm_square,
    )


def solution(mesh):
    in_specs = (
        P(("dp", "shard"), None),
        P(("dp", "shard"), None),
        P(("dp", "shard")),
        P(),
        P("dp", "shard"),
        P("dp", "shard"),
        P("dp", "shard"),
        P("dp", "shard"),
        P("dp", "shard"),
        P("dp", "shard"),
        P("dp", "shard"),
        P("dp", "shard"),
        P("dp", "shard"),
        P("dp", "shard"),
        P("dp", "shard"),
        P("dp", "shard"),
        P(),
        P(),
        P(),
    )
    out_specs = (
        P(("dp", "shard"), None),
        P(("dp", "shard"), None),
        P("dp", "shard"),
        P("dp", "shard"),
        P("dp", "shard"),
        P("dp", "shard"),
        P("dp", "shard"),
        P("dp", "shard"),
        P("dp", "shard"),
        P("dp", "shard"),
        P("dp", "shard"),
        P("dp", "shard"),
        P("dp", "shard"),
        P("dp", "shard"),
        P("dp", "shard"),
        P("dp", "shard"),
        P("dp", "shard"),
        P("dp", "shard"),
        P("dp", "shard"),
        P("dp", "shard"),
        P("dp", "shard"),
        P("dp", "shard"),
        P(),
        P(),
        P(),
        P(),
    )
    local_step = functools.partial(local, mesh.shape["dp"], mesh.shape["shard"])
    return jax.shard_map(local_step, mesh=mesh, in_specs=in_specs, out_specs=out_specs, check_vma=False)
```

```python
import functools
import math

import jax
import jax.numpy as jnp
from jax import lax
from jax.experimental import pallas as pl
from jax.experimental.pallas import tpu as pltpu
from jax.sharding import PartitionSpec as P

HEADS = 16
HD = 64
SEQ = 256
STEP = 3

NORM_EPSILON = 1e-06
BETA_FIRST = 0.5
BETA_SECOND = 0.5
ADAM_EPSILON = 1e-08
RATE_MATRIX = 0.02
RATE_OUTPUT = 0.1
RATE_NORMS = 0.3
WEIGHT_DECAY = 0.01
MASK_FILL = -1000000000.0
SCALING = 1.0 / math.sqrt(HD)
PLAIN = (((1,), (0,)), ((), ()))
TRANSPOSED = (((1,), (1,)), ((), ()))
LEADING = (((0,), (0,)), ((), ()))

F32 = jnp.float32
BF16 = jnp.bfloat16
MIB = 2**20


def dot(left, right, dims=PLAIN):
    return lax.dot_general(left, right, dims, preferred_element_type=F32)


def wide(values):
    return values.astype(F32)


def thin(values):
    return values.astype(BF16)


def shape_of(dims, dtype):
    return jax.ShapeDtypeStruct(dims, dtype)


def limits(mib):
    return pltpu.CompilerParams(vmem_limit_bytes=mib * MIB)


def cost(flops, moved, transcendentals=0):
    return pl.CostEstimate(flops=flops, bytes_accessed=moved, transcendentals=transcendentals)


def entire(array):
    return pl.BlockSpec(array.shape, lambda *_: (0,) * array.ndim)


class Grid:
    def __init__(self, dp, shard):
        self.dp, self.shard, self.depth = dp, shard, dp // 2

    def core_swap(self, values):
        return lax.ppermute(values, "shard", [(i, i ^ 1) for i in range(self.shard)])

    def cross(self, values, turned):
        pairs = []
        for d in range(self.dp):
            for s in range(self.shard):
                along_x = (s % 2 == 0) != turned
                other = (d ^ 1, s) if along_x else (d, s ^ 2)
                pairs.append((d * self.shard + s, other[0] * self.shard + other[1]))
        return lax.ppermute(values, ("dp", "shard"), pairs)

    def z_exchange(self, values):
        groups = [[z * 2 + x for z in range(self.depth)] for x in range(2)]
        return lax.all_to_all(values, "dp", 0, 0, axis_index_groups=groups, tiled=True)

    def total(self, values):
        for axis, size in (("shard", self.shard), ("dp", self.dp)):
            for bit in range((size - 1).bit_length()):
                pairs = [(i, i ^ (1 << bit)) for i in range(size)]
                values = values + lax.ppermute(values, axis, pairs)
        return values


    def copies(self, piece):
        return jnp.broadcast_to(piece, (self.depth, *piece.shape))

    def both(self, near):
        return near, self.core_swap(near)

    def gather_xy(self, near):
        return self.cross(jnp.stack(near), False)

    def gather_far(self, over):
        return self.cross(over[0], True)

    def gather_end(self, near, over, far):
        return [*near, over, self.core_swap(over), far, self.core_swap(far)]

    def owner(self, z, dx, dy, dc):
        index_dp, index_shard = lax.axis_index("dp"), lax.axis_index("shard")
        x, y, c = index_dp % 2, index_shard // 2, index_shard % 2
        row = z * 2 + lax.rem(x + dx, 2)
        column = lax.rem(y + dy, 2) * 2 + lax.rem(c + dc, 2)
        return row, column

    def gathered_places(self):
        core = lax.rem(lax.axis_index("shard"), 2)
        places = []
        for k in range(self.depth):
            places.append((0, (k,), self.owner(k, 0, 0, 0)))
            places.append((1, (k,), self.owner(k, 0, 0, 1)))
            for side in range(2):
                places.append((2, (side, k), self.owner(k, 1 - core, core, side)))
                places.append((3, (side, k), self.owner(k, core, 1 - core, 1 - side)))
            places.append((4, (k,), self.owner(k, 1, 1, 0)))
            places.append((5, (k,), self.owner(k, 1, 1, 1)))
        return places

    def region(self, other):
        core = lax.rem(lax.axis_index("shard"), 2)
        role = 1 - core if other else core
        flip = 1 if other else 0
        depth = range(self.depth)
        blocks = [self.owner(k, 1 - role, role, (flip + side) % 2) for side in range(2) for k in depth]
        blocks += [self.owner(k, 1, 1, flip) for k in depth]
        return blocks + [self.owner(k, 0, 0, flip) for k in depth]


    def scatter_core(self, far):
        return self.core_swap(far)

    def scatter_far(self, near, other):
        corner = slice(2 * self.depth, 3 * self.depth)
        return self.cross(thin(wide(near[corner]) + wide(other[corner])), True)

    def scatter_xy(self, near, other, far):
        d = self.depth
        first = wide(near[:d]) + wide(other[:d]) + wide(far)
        second = wide(near[d : 2 * d]) + wide(other[d : 2 * d])
        return self.cross(thin(jnp.concatenate([first, second])), False)

    def scatter_home(self, over):
        return self.core_swap(over[self.depth :])

    def scatter_z(self, near, other, over, passed):
        d = self.depth
        home = slice(3 * d, 4 * d)
        here = wide(near[home]) + wide(other[home]) + wide(over[:d]) + wide(passed)
        return self.z_exchange(thin(here))

    def scatter_end(self, sent):
        return jnp.sum(wide(sent), axis=0)


def tie(*values):
    return lax.optimization_barrier(values)


def block(ref, row, rows, column, columns):
    return ref.at[
        pl.ds(pl.multiple_of(row, rows), rows), pl.ds(pl.multiple_of(column, columns), columns)
    ]


def start_copies(pairs, sems):
    copies = [pltpu.make_async_copy(a, b, sems.at[n]) for n, (a, b) in enumerate(pairs)]
    for copy in copies:
        copy.start()
    return copies


def run_copies(pairs, sems):
    for copy in start_copies(pairs, sems):
        copy.wait()


def piece_loads(grid, refs, lane, target, lanes, across, offset):
    rows = target.shape[0] // grid.dp
    pairs = []
    for i, place, (row, column) in grid.gathered_places():
        source = refs[i].at[(*place, slice(None), pl.ds(lane, lanes))]
        pairs.append((source, block(target, row * rows, rows, column * across + offset, lanes)))
    return pairs


def block_stores(grid, source, lanes, near, far, lane):
    rows = source.shape[0] // grid.dp
    pairs = []
    for other in (1, 0):
        for n, (row, column) in enumerate(grid.region(other)):
            taken = block(source, row * rows, rows, column * lanes, lanes)
            pairs.append((taken, (near, far)[other].at[n, :, pl.ds(lane, lanes)]))
    return pairs


ANYWHERE = pl.BlockSpec(memory_space=pl.ANY)
SCALAR = pl.BlockSpec(memory_space=pltpu.SMEM)
HELD = pl.BlockSpec(memory_space=pltpu.VMEM)


def standardised(values):
    centred = values - jnp.mean(values, axis=-1, keepdims=True)
    inverse = lax.rsqrt(jnp.mean(centred * centred, axis=-1, keepdims=True) + NORM_EPSILON)
    return centred * inverse, inverse


def norm_back(grad, values, gain):
    n, inverse = standardised(values)
    scaled = grad * gain
    mean_scaled = jnp.mean(scaled, axis=-1, keepdims=True)
    mean_product = jnp.mean(scaled * n, axis=-1, keepdims=True)
    grad_values = inverse * (scaled - mean_scaled - n * mean_product)
    return (
        grad_values,
        jnp.sum(grad * n, axis=0, keepdims=True),
        jnp.sum(grad, axis=0, keepdims=True),
    )


def first_projection(grid, sets, cuts, tokens, norms):
    count, width = tokens.shape
    halves = len(sets)
    each = len(sets[0])
    across = sum(cuts)
    columns = across * grid.shard
    owners = grid.dp * grid.shard
    tile = width

    def kernel(x_ref, p_ref, *refs):
        sources, rest = refs[: halves * each], refs[halves * each :]
        turned_ref, joined_hbm, weight_hbm, weight, first, joined, sems, out_sems = rest
        pairs = []
        for n in range(halves):
            pieces = sources[n * each : (n + 1) * each]
            pairs += piece_loads(grid, pieces, 0, weight, cuts[n], across, sum(cuts[:n]))
        loads = start_copies(pairs, sems)

        @pl.loop(0, count, step=SEQ)
        def _(i):
            rows = pl.ds(pl.multiple_of(i, SEQ), SEQ)
            n, _ = standardised(wide(x_ref[rows, :]))
            value = thin(n * p_ref[0:1, :] + p_ref[1:2, :])
            first[rows, :] = value
            turned_ref[:, rows] = value.T

        for load in loads:
            load.wait()
        leaving = start_copies([(weight, weight_hbm)], out_sems)
        for n in range(columns // tile):
            own = slice(n * tile, (n + 1) * tile)
            joined[:, own] = thin(dot(first[...], weight[:, own]))
            pair = (joined.at[:, own], joined_hbm.at[:, own])
            leaving += start_copies([pair], out_sems.at[pl.ds(1 + n, 1)])
        for copy in leaving:
            copy.wait()

    return pl.pallas_call(
        kernel,
        out_shape=(
            shape_of((width, count), BF16),
            shape_of((count, columns), BF16),
            shape_of((width, columns), BF16),
        ),
        in_specs=[HELD, HELD] + [ANYWHERE] * (halves * each),
        out_specs=(HELD, ANYWHERE, ANYWHERE),
        scratch_shapes=[
            pltpu.VMEM((width, columns), BF16),
            pltpu.VMEM((count, width), BF16),
            pltpu.VMEM((count, columns), BF16),
            pltpu.SemaphoreType.DMA((halves * owners,)),
            pltpu.SemaphoreType.DMA((1 + columns // tile,)),
        ],
        compiler_params=limits(60),
        cost_estimate=cost(2 * count * width * columns, 4 * (width + count) * columns),
    )(tokens, norms, *[array for pieces in sets for array in pieces])


def attention(grid, pieces, lane, joined, seg_column, seg_row, tokens, norms):
    count, width = tokens.shape

    def kernel(
        j_ref, sc_ref, sr_ref, x_ref, p_ref, *refs,
    ):
        sources, rest = refs[: len(pieces)], refs[len(pieces) :]
        turned_ref, log_ref, res_ref, second_ref, second_turned_ref, mixed, weight, sems = rest
        lanes = width // grid.shard
        step = pl.program_id(0)

        @pl.when(step == 0)
        def _():
            start_copies(piece_loads(grid, sources, lane, weight, lanes, lanes, 0), sems)

        same = sc_ref[...] == sr_ref[0]
        for head in range(HEADS):
            own = slice(head * HD, (head + 1) * HD)
            query = j_ref[:, own]
            key = j_ref[:, width + head * HD : width + (head + 1) * HD]
            value = j_ref[:, 2 * width + head * HD : 2 * width + (head + 1) * HD]
            scores = jnp.where(same, dot(key, query, TRANSPOSED) * SCALING, MASK_FILL)
            top = jnp.max(scores, axis=0, keepdims=True)
            raised = jnp.exp(scores - top)
            total = jnp.sum(raised, axis=0, keepdims=True)
            log_ref[0, head : head + 1, :] = top + jnp.log(total)
            probs = thin(raised * (1.0 / total))
            mixed[:, own] = thin(dot(probs, value, LEADING))
        turned_ref[...] = mixed[...].T

        @pl.when(step == 0)
        def _():
            for n, (a, b) in enumerate(piece_loads(grid, sources, lane, weight, lanes, lanes, 0)):
                pltpu.make_async_copy(a, b, sems.at[n]).wait()

        residual = wide(x_ref[...]) + dot(mixed[...], weight[...])
        res_ref[...] = residual
        n, _ = standardised(residual)
        second = thin(n * p_ref[2:3, :] + p_ref[3:4, :])
        second_ref[...] = second
        second_turned_ref[...] = second.T

    blocks = count // SEQ

    def rows(columns):
        return pl.BlockSpec((SEQ, columns), lambda r: (r, 0))

    turned = pl.BlockSpec((width, SEQ), lambda r: (0, r))
    return pl.pallas_call(
        kernel,
        grid=(blocks,),
        out_shape=(
            shape_of((width, count), BF16),
            shape_of((blocks, HEADS, SEQ), F32),
            shape_of((count, width), F32),
            shape_of((count, width), BF16),
            shape_of((width, count), BF16),
        ),
        in_specs=[
            rows(3 * width),
            rows(1),
            pl.BlockSpec((1, 1, SEQ), lambda r: (r, 0, 0)),
            rows(width),
            entire(norms),
        ]
        + [ANYWHERE] * len(pieces),
        out_specs=(
            turned,
            pl.BlockSpec((1, HEADS, SEQ), lambda r: (r, 0, 0)),
            rows(width),
            rows(width),
            turned,
        ),
        scratch_shapes=[
            pltpu.VMEM((SEQ, width), BF16),
            pltpu.VMEM((width, width), BF16),
            pltpu.SemaphoreType.DMA((grid.dp * grid.shard,)),
        ],
        compiler_params=limits(60),
        cost_estimate=cost(
            4 * count * width * width + 16 * count * SEQ * width,
            20 * count * width,
            count * SEQ * HEADS,
        ),
    )(joined, seg_column, seg_row, tokens, norms, *pieces)


def gelu_and_slope(values):
    below = 0.5 * (1.0 + lax.erf(values * (1.0 / math.sqrt(2.0))))
    density = jnp.exp(-0.5 * values * values) * (1.0 / math.sqrt(2.0 * math.pi))
    return values * below, below + values * density


def feed_forward(grid, pieces, lane, second, second_turned, cotangent, factor, sums, regions,
                 region_lane, region_lanes, up_lanes, down_lanes):
    count, width = second.shape
    columns = up_lanes * grid.shard
    rows = width // grid.dp
    owners = grid.dp * grid.shard
    region = shape_of((4 * grid.depth, rows, region_lanes), BF16)
    used = len(pieces)

    def kernel(f_ref, s_ref, st_ref, c_ref, *refs):
        sources, rest = refs[:used], refs[used:]
        if sums:
            out_in, back_in = rest[:2]
        (
            out_hbm, back_hbm, near, far, up, down, out_sum, back_sum, hidden, grads, gu, gd, sems, sum_sems,
        ) = rest[len(sums) + len(regions) :]
        up_sems, down_sems = sems.at[pl.ds(0, owners)], sems.at[pl.ds(owners, owners)]
        up_loads = start_copies(piece_loads(grid, sources, lane, up, up_lanes, up_lanes, 0), up_sems)
        down_loads = start_copies(
            piece_loads(grid, sources, lane + up_lanes, down, down_lanes, down_lanes, 0), down_sems
        )
        if sums:
            arriving = start_copies([(out_in, out_sum), (back_in, back_sum)], sum_sems)
        for load in up_loads:
            load.wait()
        value, slope = gelu_and_slope(dot(s_ref[...], up[...]))
        for load in down_loads:
            load.wait()
        hidden[...] = thin(value)
        grads[...] = thin(dot(c_ref[...], down[...], TRANSPOSED) * slope)
        if sums:
            for copy in arriving:
                copy.wait()
            out_sum[...] += dot(hidden[...], down[...])
            back_sum[...] += dot(grads[...], up[...], TRANSPOSED)
        else:
            out_sum[...] = dot(hidden[...], down[...])
            back_sum[...] = dot(grads[...], up[...], TRANSPOSED)
        leaving = start_copies([(out_sum, out_hbm), (back_sum, back_hbm)], sum_sems)
        gu[...] = thin(dot(st_ref[...], grads[...]) * f_ref[0, 0])
        leaving += start_copies(block_stores(grid, gu, up_lanes, near, far, region_lane), up_sems)
        gd[...] = thin(dot(hidden[...], c_ref[...], LEADING) * f_ref[0, 0])
        leaving += start_copies(
            block_stores(grid, gd, down_lanes, near, far, region_lane + up_lanes), down_sems
        )
        for copy in leaving:
            copy.wait()

    aliases = {4 + used + n: n for n in range(len(sums))}
    aliases |= {4 + used + len(sums) + n: 2 + n for n in range(len(regions))}
    return pl.pallas_call(
        kernel,
        out_shape=(shape_of((count, width), F32),) * 2 + (region, region),
        in_specs=[SCALAR] + [HELD] * 3 + [ANYWHERE] * (used + len(sums) + len(regions)),
        out_specs=(ANYWHERE,) * 4,
        scratch_shapes=[
            pltpu.VMEM((width, columns), BF16),
            pltpu.VMEM((columns, width), BF16),
            pltpu.VMEM((count, width), F32),
            pltpu.VMEM((count, width), F32),
            pltpu.VMEM((count, columns), BF16),
            pltpu.VMEM((count, columns), BF16),
            pltpu.VMEM((width, columns), BF16),
            pltpu.VMEM((columns, width), BF16),
            pltpu.SemaphoreType.DMA((2 * owners,)),
            pltpu.SemaphoreType.DMA((2,)),
        ],
        input_output_aliases=aliases,
        compiler_params=limits(60),
        cost_estimate=cost(
            12 * count * width * columns,
            8 * width * columns + 22 * count * width,
            2 * count * columns,
        ),
    )(factor, second, second_turned, cotangent, *pieces, *sums, *regions)


def second_norm_back(grid, pieces, lane, sums, residual, cotangent, norms):
    out_sum, back_sum = sums
    count, width = residual.shape

    def kernel(o_ref, b_ref, res_ref, c_ref, p_ref, *refs):
        sources, rest = refs[: len(pieces)], refs[len(pieces) :]
        out_ref, grad_ref, ga_ref, gm_ref, terms_ref, weight, sems = rest
        lanes = width // grid.shard

        @pl.when(pl.program_id(0) == 0)
        def _():
            terms_ref[...] = jnp.zeros_like(terms_ref)
            run_copies(piece_loads(grid, sources, lane, weight, lanes, lanes, 0), sems)

        residual = res_ref[...]
        out_ref[...] = thin(residual + o_ref[...])
        part, gain, shift = norm_back(b_ref[...], residual, p_ref[2:3, :])
        terms_ref[0:1, :] += gain
        terms_ref[1:2, :] += shift
        grad = wide(c_ref[...]) + part
        grad_ref[...] = grad
        ga_ref[...] = thin(grad)
        gm_ref[...] = thin(dot(ga_ref[...], weight[...], TRANSPOSED))

    rows = pl.BlockSpec((SEQ, width), lambda r: (r, 0))
    return pl.pallas_call(
        kernel,
        grid=(count // SEQ,),
        out_shape=(
            shape_of((count, width), BF16),
            shape_of((count, width), F32),
            shape_of((count, width), BF16),
            shape_of((count, width), BF16),
            shape_of((2, width), F32),
        ),
        in_specs=[rows, rows, rows, rows, entire(norms)] + [ANYWHERE] * len(pieces),
        out_specs=(rows, rows, rows, rows, pl.BlockSpec((2, width), lambda r: (0, 0))),
        scratch_shapes=[
            pltpu.VMEM((width, width), BF16),
            pltpu.SemaphoreType.DMA((grid.dp * grid.shard,)),
        ],
        compiler_params=limits(60),
        cost_estimate=cost(2 * count * width * width, 24 * count * width),
    )(out_sum, back_sum, residual, cotangent, norms, *pieces)


def attention_back(first, blocks, joined, grad_mixed, logs, seg_column, seg_row):
    width = grad_mixed.shape[1]
    count = blocks * SEQ

    def kernel(j_ref, gm_ref, log_ref, sc_ref, sr_ref, gj_ref):
        same = sc_ref[...] == sr_ref[0]
        for head in range(HEADS):
            a, b = head * HD, (head + 1) * HD
            query, key = j_ref[:, a:b], j_ref[:, width + a : width + b]
            value, grad = j_ref[:, 2 * width + a : 2 * width + b], gm_ref[:, a:b]
            scores = jnp.where(same, dot(key, query, TRANSPOSED) * SCALING, MASK_FILL)
            probs = jnp.exp(scores - log_ref[0, head : head + 1, :])
            grad_probs = dot(value, grad, TRANSPOSED)
            delta = jnp.sum(probs * grad_probs, axis=0, keepdims=True)
            grad_scores = thin(probs * (grad_probs - delta))
            gj_ref[:, a:b] = thin(dot(grad_scores, key, LEADING) * SCALING)
            gj_ref[:, width + a : width + b] = thin(dot(grad_scores, query) * SCALING)
            gj_ref[:, 2 * width + a : 2 * width + b] = thin(dot(thin(probs), grad))

    def rows(columns):
        return pl.BlockSpec((SEQ, columns), lambda r: (r + first, 0))

    return pl.pallas_call(
        kernel,
        grid=(blocks,),
        out_shape=shape_of((count, 3 * width), BF16),
        in_specs=[
            rows(3 * width),
            rows(width),
            pl.BlockSpec((1, HEADS, SEQ), lambda r: (r + first, 0, 0)),
            rows(1),
            pl.BlockSpec((1, 1, SEQ), lambda r: (r + first, 0, 0)),
        ],
        out_specs=pl.BlockSpec((SEQ, 3 * width), lambda r: (r, 0)),
        compiler_params=limits(60),
        cost_estimate=cost(40 * count * SEQ * width, 14 * count * width, count * SEQ * HEADS),
    )(joined, grad_mixed, logs, seg_column, seg_row)


def first_norm_back(first, grad_joined, grad_residual, tokens, norms, weight, before):
    count, width = tokens.shape
    here = grad_joined.shape[0]

    def kernel(gj_ref, g_ref, x_ref, p_ref, w_ref, *refs):
        out_ref, terms_ref = refs[-2:]

        @pl.when(pl.program_id(0) == 0)
        def _():
            terms_ref[...] = jnp.zeros_like(terms_ref)

        grad_first = dot(gj_ref[...], w_ref[...], TRANSPOSED)
        part, gain, shift = norm_back(grad_first, wide(x_ref[...]), p_ref[0:1, :])
        terms_ref[0:1, :] += gain
        terms_ref[1:2, :] += shift
        out_ref[...] = g_ref[...] + part

    rows = pl.BlockSpec((SEQ, width), lambda r: (r + first, 0))
    return pl.pallas_call(
        kernel,
        grid=(here // SEQ,),
        out_shape=(shape_of((count, width), F32), shape_of((2, width), F32)),
        in_specs=[
            pl.BlockSpec((SEQ, 3 * width), lambda r: (r, 0)),
            rows,
            rows,
            entire(norms),
            entire(weight),
        ]
        + [ANYWHERE] * len(before),
        out_specs=(rows, pl.BlockSpec((2, width), lambda r: (0, 0))),
        input_output_aliases={5: 0} if before else {},
        compiler_params=limits(60),
        cost_estimate=cost(6 * here * width * width, 16 * here * width + 6 * width * width),
    )(grad_joined, grad_residual, tokens, norms, weight, *before)


def weight_grad(grid, turned, grads, factor, lanes, across, offset, regions, region_lane, region_lanes):
    width, count = turned.shape
    parts = len(grads)
    share = count // parts
    columns = lanes * grid.shard
    region = shape_of((4 * grid.depth, width // grid.dp, region_lanes), BF16)

    def kernel(f_ref, t_ref, *refs):
        near, far, grad, whole, sems, load_sems = refs[parts + len(regions) :]
        pairs = []
        for n in range(parts):
            for s in range(grid.shard):
                source = refs[n].at[:, pl.ds(s * across + offset, lanes)]
                rows = pl.ds(n * share, share)
                pairs.append((source, grad.at[rows, pl.ds(s * lanes, lanes)]))
        run_copies(pairs, load_sems)
        whole[...] = thin(dot(t_ref[...], grad[...]) * f_ref[0, 0])
        run_copies(block_stores(grid, whole, lanes, near, far, region_lane), sems)

    return pl.pallas_call(
        kernel,
        out_shape=(region, region),
        in_specs=[SCALAR, HELD] + [ANYWHERE] * (parts + len(regions)),
        out_specs=(ANYWHERE,) * 2,
        scratch_shapes=[
            pltpu.VMEM((count, columns), BF16),
            pltpu.VMEM((width, columns), BF16),
            pltpu.SemaphoreType.DMA((grid.dp * grid.shard,)),
            pltpu.SemaphoreType.DMA((parts * grid.shard,)),
        ],
        input_output_aliases={2 + parts + n: n for n in range(len(regions))},
        compiler_params=limits(60),
        cost_estimate=cost(
            2 * count * width * columns, 2 * (width * count + (width + count) * columns)
        ),
    )(factor, turned, *grads, *regions)


def adam_update(master, moment, square, gradient, rate):
    new_moment = BETA_FIRST * moment + (1.0 - BETA_FIRST) * gradient
    new_square = BETA_SECOND * square + (1.0 - BETA_SECOND) * gradient * gradient
    bias_first = 1.0 - BETA_FIRST**STEP
    bias_second = 1.0 - BETA_SECOND**STEP
    update = new_moment / bias_first / (jnp.sqrt(new_square / bias_second) + ADAM_EPSILON)
    new_master = master - rate * (update + WEIGHT_DECAY * master)
    return (new_master, new_moment, new_square)


def local(
    grid,
    tokens,
    cotangent,
    segment_ids,
    group_counts,
    master_qkv,
    master_out,
    master_up,
    master_down,
    moment_qkv,
    moment_out,
    moment_up,
    moment_down,
    square_qkv,
    square_out,
    square_up,
    square_down,
    norm_params,
    norm_moment,
    norm_square,
):
    rows, out_lanes = master_up.shape[0], master_out.shape[1]
    qkv_lanes = master_qkv.shape[1]
    chunks = master_down.shape[0] // rows
    up_lanes = master_up.shape[1] // chunks
    down_lanes = master_down.shape[1]
    per_shard = grid.dp // grid.shard
    blocks = tokens.shape[0] // SEQ
    both_lanes = up_lanes + down_lanes

    up_cut = thin(master_up).reshape(rows, per_shard, chunks, up_lanes // per_shard)
    down_cut = thin(master_down).reshape(chunks, rows, down_lanes)
    cuts = (qkv_lanes - out_lanes, out_lanes)

    def large(*members):
        parts = []
        for n in members:
            parts += [up_cut[:, :, n].reshape(rows, up_lanes), down_cut[n]]
        return jnp.concatenate(parts, axis=1)

    counts = group_counts.astype(F32)
    own_count = jnp.sum(jnp.where(jnp.arange(counts.shape[0]) == lax.axis_index("dp"), counts, 0.0))
    factor = own_count * counts.shape[0] / jnp.sum(counts)
    factor_cell = factor.reshape(1, 1)
    seg_column = segment_ids[:, None]
    seg_row = segment_ids.reshape(blocks, 1, SEQ)

    piece = jnp.concatenate([thin(master_qkv[:, cuts[0] :]), thin(master_out)], axis=1)
    q0 = grid.z_exchange(grid.copies(thin(master_qkv[:, : cuts[0]])))
    q0, piece = tie(grid.both(q0), piece)
    q0_over = grid.gather_xy(q0)
    q1 = grid.z_exchange(grid.copies(piece))
    q0_over, q1, piece = tie(q0_over, grid.both(q1), large(0))
    q0_far = grid.gather_far(q0_over)
    q1_over = grid.gather_xy(q1)
    q1_over, q0_far, piece = tie(q1_over, q0_far, piece)
    q0_pieces = grid.gather_end(q0, q0_over, q0_far)
    q1_far = grid.gather_far(q1_over)
    m0 = grid.z_exchange(grid.copies(piece))
    q1_far, m0 = tie(q1_far, m0)
    q1_pieces = grid.gather_end(q1, q1_over, q1_far)
    m0 = grid.both(m0)

    q0_pieces, q1_pieces, m0, piece = tie(q0_pieces, q1_pieces, m0, large(1))
    first_turned, joined, qkv_weight = first_projection(
        grid, [q0_pieces, q1_pieces], cuts, tokens, norm_params
    )
    m0_over = grid.gather_xy(m0)
    m1 = grid.z_exchange(grid.copies(piece))

    joined, m0_over, m1, piece = tie(joined, m0_over, m1, large(2, 3))
    m1 = grid.both(m1)
    joined, m1 = tie(joined, m1)
    mixed_turned, logs, residual, second, second_turned = attention(
        grid, q1_pieces, cuts[1], joined, seg_column, seg_row, tokens, norm_params
    )
    m0_far = grid.gather_far(m0_over)
    m1_over = grid.gather_xy(m1)
    m2 = grid.z_exchange(grid.copies(piece))
    second, m0_far, m2 = tie(second, m0_far, m2)
    m0_pieces = grid.gather_end(m0, m0_over, m0_far)
    m2 = grid.both(m2)

    def chunk(weights, lane, sums, regions, place):
        out_sum, back_sum, near, far = feed_forward(
            grid, weights, lane, second, second_turned, cotangent, factor_cell, sums, regions,
            place * both_lanes, 2 * both_lanes, up_lanes, down_lanes,
        )
        return (out_sum, back_sum), (near, far)

    second, m0_pieces, m1_over, m2 = tie(second, m0_pieces, m1_over, m2)
    sums, r0 = chunk(m0_pieces, 0, (), (), 0)
    m1_far = grid.gather_far(m1_over)
    m2_over = grid.gather_xy(m2)
    sums, m1_far = tie(sums, m1_far)
    m1_pieces = grid.gather_end(m1, m1_over, m1_far)

    sums, m1_pieces, m2_over = tie(sums, m1_pieces, m2_over)
    sums, r0 = chunk(m1_pieces, 0, sums, r0, 1)
    m2_far = grid.gather_far(m2_over)
    sums, m2_far = tie(sums, m2_far)
    m2_pieces = grid.gather_end(m2, m2_over, m2_far)

    sums, m2_pieces, r0 = tie(sums, m2_pieces, r0)
    sums, r1 = chunk(m2_pieces, 0, sums, (), 0)
    r0_other = grid.scatter_core(r0[1])

    sums, r0_other = tie(sums, r0_other)
    sums, r1 = chunk(m2_pieces, both_lanes, sums, r1, 1)
    r0_far = grid.scatter_far(r0[0], r0_other)

    sums, r0_far, r1 = tie(sums, r0_far, r1)
    block_out, grad_residual, grad_attention, grad_mixed, second_terms = second_norm_back(
        grid, q1_pieces, cuts[1], sums, residual, cotangent, norm_params
    )
    r0_over = grid.scatter_xy(r0[0], r0_other, r0_far)
    r1_other = grid.scatter_core(r1[1])
    q1 = weight_grad(
        grid, mixed_turned, [grad_attention], factor_cell, out_lanes, out_lanes, 0,
        (), cuts[1], cuts[1] + out_lanes,
    )

    grad_mixed, r0_over, r1_other, q1 = tie(grad_mixed, r0_over, r1_other, q1)
    grad_joined = [attention_back(0, blocks // 2, joined, grad_mixed, logs, seg_column, seg_row)]
    r1_far = grid.scatter_far(r1[0], r1_other)
    r0_passed = grid.scatter_home(r0_over)
    grad_mixed, grad_joined, r1_far, r0_passed = tie(grad_mixed, grad_joined, r1_far, r0_passed)
    grad_joined.append(
        attention_back(blocks // 2, blocks // 2, joined, grad_mixed, logs, seg_column, seg_row)
    )
    r1_over = grid.scatter_xy(r1[0], r1_other, r1_far)
    r0_sent = grid.scatter_z(r0[0], r0_other, r0_over, r0_passed)
    grad_joined, r0_sent = tie(grad_joined, r0_sent)
    q0 = weight_grad(
        grid, first_turned, grad_joined, factor_cell, cuts[0], qkv_lanes, 0, (), 0, cuts[0]
    )
    grad_joined, q0, r1_over = tie(grad_joined, q0, r1_over)
    q0_other = grid.scatter_core(q0[1])
    r1_passed = grid.scatter_home(r1_over)
    q1 = weight_grad(
        grid, first_turned, grad_joined, factor_cell, cuts[1], qkv_lanes, cuts[0],
        q1, 0, cuts[1] + out_lanes,
    )

    grad_joined, q0_other, q1, r1_passed = tie(grad_joined, q0_other, q1, r1_passed)
    q0_far = grid.scatter_far(q0[0], q0_other)
    q1_other = grid.scatter_core(q1[1])
    r1_sent = grid.scatter_z(r1[0], r1_other, r1_over, r1_passed)
    input_grad, first_terms = first_norm_back(
        0, grad_joined[0], grad_residual, tokens, norm_params, qkv_weight, ()
    )
    input_grad, q0_far, q1_other = tie(input_grad, q0_far, q1_other)
    q0_over = grid.scatter_xy(q0[0], q0_other, q0_far)
    q1_far = grid.scatter_far(q1[0], q1_other)
    input_grad, more_terms = first_norm_back(
        blocks // 2, grad_joined[1], grad_residual, tokens, norm_params, qkv_weight, (input_grad,)
    )
    more_terms, q0_over, q1_far, r1_sent = tie(more_terms, q0_over, q1_far, r1_sent)
    q0_passed = grid.scatter_home(q0_over)
    q1_over = grid.scatter_xy(q1[0], q1_other, q1_far)
    q0_sent = grid.scatter_z(q0[0], q0_other, q0_over, q0_passed)
    norm_grad = grid.total(jnp.concatenate([first_terms + more_terms, second_terms]) * factor)
    q0_sent, q1_over, norm_grad = tie(q0_sent, q1_over, norm_grad)
    q1_sent = grid.scatter_z(q1[0], q1_other, q1_over, grid.scatter_home(q1_over))
    q0_total, q1_total = grid.scatter_end(q0_sent), grid.scatter_end(q1_sent)
    grad_qkv = jnp.concatenate([q0_total, q1_total[:, : cuts[1]]], axis=1)
    grad_out = q1_total[:, cuts[1] :]
    totals = [grid.scatter_end(r0_sent), grid.scatter_end(r1_sent)]

    def pieces_of(first, lanes):
        return [
            t[:, i * both_lanes + first : i * both_lanes + first + lanes]
            for t in totals
            for i in range(chunks // 2)
        ]

    grad_up = jnp.stack(
        [piece.reshape(rows, per_shard, -1) for piece in pieces_of(0, up_lanes)], axis=2
    ).reshape(master_up.shape)
    grad_down = jnp.concatenate(pieces_of(up_lanes, down_lanes))
    new_qkv, new_moment_qkv, new_square_qkv = adam_update(
        master_qkv, moment_qkv, square_qkv, grad_qkv, RATE_MATRIX
    )
    new_out, new_moment_out, new_square_out = adam_update(
        master_out, moment_out, square_out, grad_out, RATE_OUTPUT
    )
    new_up, new_moment_up, new_square_up = adam_update(
        master_up, moment_up, square_up, grad_up, RATE_MATRIX
    )
    new_down, new_moment_down, new_square_down = adam_update(
        master_down, moment_down, square_down, grad_down, RATE_MATRIX
    )
    new_norm, new_norm_moment, new_norm_square = adam_update(
        norm_params, norm_moment, norm_square, norm_grad, RATE_NORMS
    )
    return (
        block_out,
        input_grad,
        grad_qkv,
        grad_out,
        grad_up,
        grad_down,
        new_qkv,
        new_out,
        new_up,
        new_down,
        new_moment_qkv,
        new_moment_out,
        new_moment_up,
        new_moment_down,
        new_square_qkv,
        new_square_out,
        new_square_up,
        new_square_down,
        thin(new_qkv),
        thin(new_out),
        thin(new_up),
        thin(new_down),
        norm_grad,
        new_norm,
        new_norm_moment,
        new_norm_square,
    )


def solution(mesh):
    rows = P(("dp", "shard"), None)
    owned = P("dp", "shard")
    in_specs = (rows, rows, P(("dp", "shard")), P()) + (owned,) * 12 + (P(),) * 3
    out_specs = (rows, rows) + (owned,) * 20 + (P(),) * 4
    step = functools.partial(local, Grid(mesh.shape["dp"], mesh.shape["shard"]))
    return jax.shard_map(step, mesh=mesh, in_specs=in_specs, out_specs=out_specs, check_vma=False)
```

```python
import functools
import math

import jax
import jax.numpy as jnp
from jax import lax
from jax.experimental import pallas as pl
from jax.experimental.pallas import tpu as pltpu
from jax.sharding import PartitionSpec as P

HEADS = 16
HD = 64
SEQ = 256
STEP = 3

NORM_EPSILON = 1e-06
BETA_FIRST = 0.5
BETA_SECOND = 0.5
ADAM_EPSILON = 1e-08
RATE_MATRIX = 0.02
RATE_OUTPUT = 0.1
RATE_NORMS = 0.3
WEIGHT_DECAY = 0.01
MASK_FILL = -1000000000.0
SCALING = 1.0 / math.sqrt(HD)
PLAIN = (((1,), (0,)), ((), ()))
TRANSPOSED = (((1,), (1,)), ((), ()))
LEADING = (((0,), (0,)), ((), ()))

F32 = jnp.float32
BF16 = jnp.bfloat16
MIB = 2**20


def dot(left, right, dims=PLAIN):
    return lax.dot_general(left, right, dims, preferred_element_type=F32)


def wide(values):
    return values.astype(F32)


def thin(values):
    return values.astype(BF16)


def shape_of(dims, dtype):
    return jax.ShapeDtypeStruct(dims, dtype)


def limits(mib):
    return pltpu.CompilerParams(vmem_limit_bytes=mib * MIB)


def cost(flops, moved, transcendentals=0):
    return pl.CostEstimate(flops=flops, bytes_accessed=moved, transcendentals=transcendentals)


def entire(array):
    return pl.BlockSpec(array.shape, lambda *_: (0,) * array.ndim)


class Grid:
    def __init__(self, dp, shard):
        self.dp, self.shard, self.depth = dp, shard, dp // 2

    def core_swap(self, values):
        return lax.ppermute(values, "shard", [(i, i ^ 1) for i in range(self.shard)])

    def cross(self, values, turned):
        pairs = []
        for d in range(self.dp):
            for s in range(self.shard):
                along_x = (s % 2 == 0) != turned
                other = (d ^ 1, s) if along_x else (d, s ^ 2)
                pairs.append((d * self.shard + s, other[0] * self.shard + other[1]))
        return lax.ppermute(values, ("dp", "shard"), pairs)

    def z_exchange(self, values):
        groups = [[z * 2 + x for z in range(self.depth)] for x in range(2)]
        return lax.all_to_all(values, "dp", 0, 0, axis_index_groups=groups, tiled=True)

    def total(self, values, axis):
        size = self.shard if axis == "shard" else self.dp
        for bit in range((size - 1).bit_length()):
            pairs = [(i, i ^ (1 << bit)) for i in range(size)]
            values = values + lax.ppermute(values, axis, pairs)
        return values


    def copies(self, piece):
        return jnp.broadcast_to(piece, (self.depth, *piece.shape))

    def gather_z(self, piece):
        parts = [piece]
        for k in range(1, self.depth):
            shift = [((i // 2 + k) % self.depth * 2 + i % 2, i) for i in range(self.dp)]
            parts.append(lax.ppermute(piece, "dp", shift))
        return jnp.stack(parts)

    def both(self, near):
        return near, self.core_swap(near)

    def gather_xy(self, near):
        return [self.cross(values, False) for values in near]

    def gather_far(self, over):
        return self.cross(over[0], True)

    def gather_end(self, near, over, far):
        mine = [*over, far]
        return [*near, *mine, *[self.core_swap(values) for values in mine]]


    def gather_xy_joined(self, near):
        return self.cross(jnp.concatenate(near), False)

    def gather_far_joined(self, over):
        return self.cross(over[: self.depth], True)

    def gather_end_joined(self, near, over, far):
        return [*near, over, far, self.core_swap(over), self.core_swap(far)]

    def owner(self, z, dx, dy, dc):
        index_dp, index_shard = lax.axis_index("dp"), lax.axis_index("shard")
        x, y, c = index_dp % 2, index_shard // 2, index_shard % 2
        row = z * 2 + lax.rem(x + dx, 2)
        column = lax.rem(y + dy, 2) * 2 + lax.rem(c + dc, 2)
        return row, column

    def gathered_places(self, turned, joined):
        where = (2, 2, 4, 4, 3, 5) if joined else (2, 3, 5, 6, 4, 7)
        skip = self.depth if joined else 0
        core = lax.rem(lax.axis_index("shard"), 2)
        own = lax.axis_index("dp") // 2
        places = []
        for k in range(self.depth):
            z = lax.rem(own + k, self.depth) if turned else k
            for side in range(2):
                places.append((side, k, self.owner(z, 0, 0, side)))
                beyond = side * skip + k
                places.append((where[side], beyond, self.owner(z, 1 - core, core, side)))
                places.append((where[2 + side], beyond, self.owner(z, core, 1 - core, 1 - side)))
            places.append((where[4], k, self.owner(z, 1, 1, 0)))
            places.append((where[5], k, self.owner(z, 1, 1, 1)))
        return places

    def region(self, other):
        core = lax.rem(lax.axis_index("shard"), 2)
        role = 1 - core if other else core
        flip = 1 if other else 0
        depth = range(self.depth)
        blocks = [self.owner(k, 1 - role, role, (flip + side) % 2) for side in range(2) for k in depth]
        blocks += [self.owner(k, 1, 1, flip) for k in depth]
        return blocks + [self.owner(k, 0, 0, flip) for k in depth]


    def scatter_core(self, far):
        return self.core_swap(far)

    def scatter_far(self, near, other):
        corner = slice(2 * self.depth, 3 * self.depth)
        return self.cross(thin(wide(near[corner]) + wide(other[corner])), True)

    def scatter_xy(self, near, other, far):
        d = self.depth
        first = wide(near[:d]) + wide(other[:d]) + wide(far)
        second = wide(near[d : 2 * d]) + wide(other[d : 2 * d])
        return [self.cross(thin(second), False), self.cross(thin(first), False)][::-1]

    def scatter_home(self, over):
        return self.core_swap(over[1])

    def scatter_z(self, near, other, over, passed):
        d = self.depth
        home = slice(3 * d, 4 * d)
        here = wide(near[home]) + wide(other[home]) + wide(over[0]) + wide(passed)
        return self.z_exchange(thin(here))

    def scatter_end(self, sent):
        return jnp.sum(wide(sent), axis=0)


def tie(*values):
    return lax.optimization_barrier(values)


def block(ref, row, rows, column, columns):
    return ref.at[
        pl.ds(pl.multiple_of(row, rows), rows), pl.ds(pl.multiple_of(column, columns), columns)
    ]


def start_copies(pairs, sems):
    copies = [pltpu.make_async_copy(a, b, sems.at[n]) for n, (a, b) in enumerate(pairs)]
    for copy in copies:
        copy.start()
    return copies


def run_copies(pairs, sems):
    for copy in start_copies(pairs, sems):
        copy.wait()


def piece_loads(grid, refs, lane, target, lanes, across, offset, turned=True):
    rows = target.shape[0] // grid.dp
    pairs = []
    for i, place, (row, column) in grid.gathered_places(turned, len(refs) == 6):
        source = refs[i].at[place, :, pl.ds(lane, lanes)]
        pairs.append((source, block(target, row * rows, rows, column * across + offset, lanes)))
    return pairs


def block_stores(grid, source, lanes, near, far, lane):
    rows = source.shape[0] // grid.dp
    pairs = []
    for other in (1, 0):
        for n, (row, column) in enumerate(grid.region(other)):
            taken = block(source, row * rows, rows, column * lanes, lanes)
            pairs.append((taken, (near, far)[other].at[n, :, pl.ds(lane, lanes)]))
    return pairs


ANYWHERE = pl.BlockSpec(memory_space=pl.ANY)
SCALAR = pl.BlockSpec(memory_space=pltpu.SMEM)
HELD = pl.BlockSpec(memory_space=pltpu.VMEM)


def standardised(values):
    centred = values - jnp.mean(values, axis=-1, keepdims=True)
    inverse = lax.rsqrt(jnp.mean(centred * centred, axis=-1, keepdims=True) + NORM_EPSILON)
    return centred * inverse, inverse


def norm_back(grad, values, gain):
    n, inverse = standardised(values)
    scaled = grad * gain
    mean_scaled = jnp.mean(scaled, axis=-1, keepdims=True)
    mean_product = jnp.mean(scaled * n, axis=-1, keepdims=True)
    grad_values = inverse * (scaled - mean_scaled - n * mean_product)
    return (
        grad_values,
        jnp.sum(grad * n, axis=0, keepdims=True),
        jnp.sum(grad, axis=0, keepdims=True),
    )


def first_projection(grid, sets, cuts, tokens, norms):
    count, width = tokens.shape
    halves = len(sets)
    each = len(sets[0])
    across = sum(cuts)
    columns = across * grid.shard
    owners = grid.dp * grid.shard
    tile = width

    def kernel(x_ref, p_ref, *refs):
        sources, rest = refs[: halves * each], refs[halves * each :]
        turned_ref, joined_hbm, weight_hbm, weight, first, joined, sems, out_sems = rest
        pairs = []
        for n in range(halves):
            pieces = sources[n * each : (n + 1) * each]
            pairs += piece_loads(grid, pieces, 0, weight, cuts[n], across, sum(cuts[:n]))
        loads = start_copies(pairs, sems)

        @pl.loop(0, count, step=SEQ)
        def _(i):
            rows = pl.ds(pl.multiple_of(i, SEQ), SEQ)
            n, _ = standardised(wide(x_ref[rows, :]))
            value = thin(n * p_ref[0:1, :] + p_ref[1:2, :])
            first[rows, :] = value
            turned_ref[:, rows] = value.T

        for load in loads:
            load.wait()
        leaving = start_copies([(weight, weight_hbm)], out_sems)
        for n in range(columns // tile):
            own = slice(n * tile, (n + 1) * tile)
            joined[:, own] = thin(dot(first[...], weight[:, own]))
            pair = (joined.at[:, own], joined_hbm.at[:, own])
            leaving += start_copies([pair], out_sems.at[pl.ds(1 + n, 1)])
        for copy in leaving:
            copy.wait()

    return pl.pallas_call(
        kernel,
        out_shape=(
            shape_of((width, count), BF16),
            shape_of((count, columns), BF16),
            shape_of((width, columns), BF16),
        ),
        in_specs=[HELD, HELD] + [ANYWHERE] * (halves * each),
        out_specs=(HELD, ANYWHERE, ANYWHERE),
        scratch_shapes=[
            pltpu.VMEM((width, columns), BF16),
            pltpu.VMEM((count, width), BF16),
            pltpu.VMEM((count, columns), BF16),
            pltpu.SemaphoreType.DMA((halves * owners,)),
            pltpu.SemaphoreType.DMA((1 + columns // tile,)),
        ],
        compiler_params=limits(60),
        cost_estimate=cost(2 * count * width * columns, 4 * (width + count) * columns),
    )(tokens, norms, *[array for pieces in sets for array in pieces])


def attention(grid, pieces, lane, joined, seg_column, seg_row, tokens, norms):
    count, width = tokens.shape

    def kernel(
        j_ref, sc_ref, sr_ref, x_ref, p_ref, *refs,
    ):
        sources, rest = refs[: len(pieces)], refs[len(pieces) :]
        turned_ref, log_ref, res_ref, second_ref, second_turned_ref, mixed, weight, sems = rest
        lanes = width // grid.shard
        step = pl.program_id(0)

        @pl.when(step == 0)
        def _():
            start_copies(piece_loads(grid, sources, lane, weight, lanes, lanes, 0), sems)

        same = sc_ref[...] == sr_ref[0]
        left = lax.broadcasted_iota(jnp.int32, (SEQ, 2 * HD), 1) < HD
        for pair in range(HEADS // 2):
            a, b = pair * 2 * HD, (pair + 1) * 2 * HD
            query, key = j_ref[:, a:b], j_ref[:, width + a : width + b]
            value = j_ref[:, 2 * width + a : 2 * width + b]
            results = []
            for side in range(2):
                own_key = jnp.where(left == (side == 0), key, jnp.zeros_like(key))
                scores = jnp.where(same, dot(own_key, query, TRANSPOSED) * SCALING, MASK_FILL)
                top = jnp.max(scores, axis=0, keepdims=True)
                raised = jnp.exp(scores - top)
                total = jnp.sum(raised, axis=0, keepdims=True)
                head = 2 * pair + side
                log_ref[0, head : head + 1, :] = top + jnp.log(total)
                results.append(dot(thin(raised * (1.0 / total)), value, LEADING))
            mixed[:, a:b] = thin(jnp.where(left, results[0], results[1]))
        turned_ref[...] = mixed[...].T

        @pl.when(step == 0)
        def _():
            for n, (a, b) in enumerate(piece_loads(grid, sources, lane, weight, lanes, lanes, 0)):
                pltpu.make_async_copy(a, b, sems.at[n]).wait()

        residual = wide(x_ref[...]) + dot(mixed[...], weight[...])
        res_ref[...] = residual
        n, _ = standardised(residual)
        second = thin(n * p_ref[2:3, :] + p_ref[3:4, :])
        second_ref[...] = second
        second_turned_ref[...] = second.T

    blocks = count // SEQ

    def rows(columns):
        return pl.BlockSpec((SEQ, columns), lambda r: (r, 0))

    turned = pl.BlockSpec((width, SEQ), lambda r: (0, r))
    return pl.pallas_call(
        kernel,
        grid=(blocks,),
        out_shape=(
            shape_of((width, count), BF16),
            shape_of((blocks, HEADS, SEQ), F32),
            shape_of((count, width), F32),
            shape_of((count, width), BF16),
            shape_of((width, count), BF16),
        ),
        in_specs=[
            rows(3 * width),
            rows(1),
            pl.BlockSpec((1, 1, SEQ), lambda r: (r, 0, 0)),
            rows(width),
            entire(norms),
        ]
        + [ANYWHERE] * len(pieces),
        out_specs=(
            turned,
            pl.BlockSpec((1, HEADS, SEQ), lambda r: (r, 0, 0)),
            rows(width),
            rows(width),
            turned,
        ),
        scratch_shapes=[
            pltpu.VMEM((SEQ, width), BF16),
            pltpu.VMEM((width, width), BF16),
            pltpu.SemaphoreType.DMA((grid.dp * grid.shard,)),
        ],
        compiler_params=limits(60),
        cost_estimate=cost(
            4 * count * width * width + 16 * count * SEQ * width,
            20 * count * width,
            count * SEQ * HEADS,
        ),
    )(joined, seg_column, seg_row, tokens, norms, *pieces)


def gelu_and_slope(values):
    below = 0.5 * (1.0 + lax.erf(values * (1.0 / math.sqrt(2.0))))
    density = jnp.exp(-0.5 * values * values) * (1.0 / math.sqrt(2.0 * math.pi))
    return values * below, below + values * density


def feed_forward(grid, pieces, second, second_turned, cotangent, factor, sums, regions,
                 region_lane, region_lanes, up_lanes, down_lanes, turned):
    count, width = second.shape
    columns = up_lanes * grid.shard
    rows = width // grid.dp
    owners = grid.dp * grid.shard
    region = shape_of((4 * grid.depth, rows, region_lanes), BF16)
    used = len(pieces)

    def kernel(f_ref, s_hbm, st_hbm, c_hbm, *refs):
        sources, rest = refs[:used], refs[used:]
        if sums:
            out_in, back_in = rest[:2]
        (
            out_hbm, back_hbm, near, far, s_ref, st_ref, c_ref, up, down, out_sum, back_sum, hidden, grads,
            gu, gd, sems, sum_sems, row_sems,
        ) = rest[len(sums) + len(regions) :]
        up_sems, down_sems = sems.at[pl.ds(0, owners)], sems.at[pl.ds(owners, owners)]
        up_loads = start_copies([(s_hbm, s_ref)], row_sems.at[pl.ds(0, 1)])
        up_loads += start_copies(piece_loads(grid, sources, 0, up, up_lanes, up_lanes, 0, turned), up_sems)
        down_loads = start_copies([(c_hbm, c_ref)], row_sems.at[pl.ds(1, 1)])
        down_loads += start_copies(
            piece_loads(grid, sources, up_lanes, down, down_lanes, down_lanes, 0, turned), down_sems
        )
        if sums:
            arriving = start_copies([(out_in, out_sum), (back_in, back_sum)], sum_sems)
        turned_load = start_copies([(st_hbm, st_ref)], row_sems.at[pl.ds(2, 1)])
        for load in up_loads:
            load.wait()
        value, slope = gelu_and_slope(dot(s_ref[...], up[...]))
        for load in down_loads:
            load.wait()
        hidden[...] = thin(value)
        grads[...] = thin(dot(c_ref[...], down[...], TRANSPOSED) * slope)
        if sums:
            for copy in arriving:
                copy.wait()
            out_sum[...] += dot(hidden[...], down[...])
            back_sum[...] += dot(grads[...], up[...], TRANSPOSED)
        else:
            out_sum[...] = dot(hidden[...], down[...])
            back_sum[...] = dot(grads[...], up[...], TRANSPOSED)
        leaving = start_copies([(out_sum, out_hbm), (back_sum, back_hbm)], sum_sems)
        turned_load[0].wait()
        gu[...] = thin(dot(st_ref[...], grads[...]) * f_ref[0, 0])
        leaving += start_copies(block_stores(grid, gu, up_lanes, near, far, region_lane), up_sems)
        gd[...] = thin(dot(hidden[...], c_ref[...], LEADING) * f_ref[0, 0])
        leaving += start_copies(
            block_stores(grid, gd, down_lanes, near, far, region_lane + up_lanes), down_sems
        )
        for copy in leaving:
            copy.wait()

    aliases = {4 + used + n: n for n in range(len(sums))}
    aliases |= {4 + used + len(sums) + n: 2 + n for n in range(len(regions))}
    return pl.pallas_call(
        kernel,
        out_shape=(shape_of((count, width), F32),) * 2 + (region, region),
        in_specs=[SCALAR] + [ANYWHERE] * (3 + used + len(sums) + len(regions)),
        out_specs=(ANYWHERE,) * 4,
        scratch_shapes=[
            pltpu.VMEM((count, width), BF16),
            pltpu.VMEM((width, count), BF16),
            pltpu.VMEM((count, width), BF16),
            pltpu.VMEM((width, columns), BF16),
            pltpu.VMEM((columns, width), BF16),
            pltpu.VMEM((count, width), F32),
            pltpu.VMEM((count, width), F32),
            pltpu.VMEM((count, columns), BF16),
            pltpu.VMEM((count, columns), BF16),
            pltpu.VMEM((width, columns), BF16),
            pltpu.VMEM((columns, width), BF16),
            pltpu.SemaphoreType.DMA((2 * owners,)),
            pltpu.SemaphoreType.DMA((2,)),
            pltpu.SemaphoreType.DMA((3,)),
        ],
        input_output_aliases=aliases,
        compiler_params=limits(60),
        cost_estimate=cost(
            12 * count * width * columns,
            8 * width * columns + 22 * count * width,
            2 * count * columns,
        ),
    )(factor, second, second_turned, cotangent, *pieces, *sums, *regions)


def second_norm_back(grid, pieces, lane, sums, residual, cotangent, norms):
    out_sum, back_sum = sums
    count, width = residual.shape

    def kernel(o_ref, b_ref, res_ref, c_ref, p_ref, *refs):
        sources, rest = refs[: len(pieces)], refs[len(pieces) :]
        out_ref, grad_ref, ga_ref, gm_ref, terms_ref, weight, sems = rest
        lanes = width // grid.shard

        @pl.when(pl.program_id(0) == 0)
        def _():
            terms_ref[...] = jnp.zeros_like(terms_ref)
            run_copies(piece_loads(grid, sources, lane, weight, lanes, lanes, 0), sems)

        residual = res_ref[...]
        out_ref[...] = thin(residual + o_ref[...])
        part, gain, shift = norm_back(b_ref[...], residual, p_ref[2:3, :])
        terms_ref[0:1, :] += gain
        terms_ref[1:2, :] += shift
        grad = wide(c_ref[...]) + part
        grad_ref[...] = grad
        ga_ref[...] = thin(grad)
        gm_ref[...] = thin(dot(ga_ref[...], weight[...], TRANSPOSED))

    rows = pl.BlockSpec((SEQ, width), lambda r: (r, 0))
    return pl.pallas_call(
        kernel,
        grid=(count // SEQ,),
        out_shape=(
            shape_of((count, width), BF16),
            shape_of((count, width), F32),
            shape_of((count, width), BF16),
            shape_of((count, width), BF16),
            shape_of((2, width), F32),
        ),
        in_specs=[rows, rows, rows, rows, entire(norms)] + [ANYWHERE] * len(pieces),
        out_specs=(rows, rows, rows, rows, pl.BlockSpec((2, width), lambda r: (0, 0))),
        scratch_shapes=[
            pltpu.VMEM((width, width), BF16),
            pltpu.SemaphoreType.DMA((grid.dp * grid.shard,)),
        ],
        compiler_params=limits(60),
        cost_estimate=cost(2 * count * width * width, 24 * count * width),
    )(out_sum, back_sum, residual, cotangent, norms, *pieces)


def attention_back(first, blocks, joined, grad_mixed, logs, seg_column, seg_row):
    width = grad_mixed.shape[1]
    count = blocks * SEQ

    def kernel(j_ref, gm_ref, log_ref, sc_ref, sr_ref, gj_ref):
        same = sc_ref[...] == sr_ref[0]
        left = lax.broadcasted_iota(jnp.int32, (SEQ, 2 * HD), 1) < HD
        for pair in range(HEADS // 2):
            a, b = pair * 2 * HD, (pair + 1) * 2 * HD
            query, key = j_ref[:, a:b], j_ref[:, width + a : width + b]
            value, grad = j_ref[:, 2 * width + a : 2 * width + b], gm_ref[:, a:b]
            turned_key = key.T
            grad_query, results = [], []
            for side in range(2):
                chosen = left == (side == 0)
                own_key = jnp.where(chosen, key, jnp.zeros_like(key))
                own_value = jnp.where(chosen, value, jnp.zeros_like(value))
                scores = jnp.where(same, dot(own_key, query, TRANSPOSED) * SCALING, MASK_FILL)
                head = 2 * pair + side
                probs = jnp.exp(scores - log_ref[0, head : head + 1, :])
                grad_probs = dot(own_value, grad, TRANSPOSED)
                delta = jnp.sum(probs * grad_probs, axis=0, keepdims=True)
                grad_scores = thin(probs * (grad_probs - delta))
                grad_query.append(dot(turned_key[side * HD : (side + 1) * HD], grad_scores))
                results.append((dot(grad_scores, query) * SCALING, dot(thin(probs), grad)))
            gj_ref[:, a:b] = thin(jnp.concatenate(grad_query).T * SCALING)
            for n, (even, odd) in enumerate(zip(*results), 1):
                gj_ref[:, n * width + a : n * width + b] = thin(jnp.where(left, even, odd))

    def rows(columns):
        return pl.BlockSpec((SEQ, columns), lambda r: (r + first, 0))

    return pl.pallas_call(
        kernel,
        grid=(blocks,),
        out_shape=shape_of((count, 3 * width), BF16),
        in_specs=[
            rows(3 * width),
            rows(width),
            pl.BlockSpec((1, HEADS, SEQ), lambda r: (r + first, 0, 0)),
            rows(1),
            pl.BlockSpec((1, 1, SEQ), lambda r: (r + first, 0, 0)),
        ],
        out_specs=pl.BlockSpec((SEQ, 3 * width), lambda r: (r, 0)),
        compiler_params=limits(60),
        cost_estimate=cost(40 * count * SEQ * width, 14 * count * width, count * SEQ * HEADS),
    )(joined, grad_mixed, logs, seg_column, seg_row)


def first_norm_back(grad_joined, grad_residual, tokens, norms, weight):
    count, width = tokens.shape
    parts = len(grad_joined)
    blocks = count // SEQ // parts

    def kernel(*refs):
        gj_refs, (g_ref, x_ref, p_ref, w_ref, out_ref, terms_ref) = refs[:parts], refs[parts:]
        step = pl.program_id(0)

        @pl.when(step == 0)
        def _():
            terms_ref[...] = jnp.zeros_like(terms_ref)

        for n in range(parts):

            @pl.when(lax.div(step, blocks) == n)
            def _(n=n):
                grad_first = dot(gj_refs[n][...], w_ref[...], TRANSPOSED)
                part, gain, shift = norm_back(grad_first, wide(x_ref[...]), p_ref[0:1, :])
                terms_ref[0:1, :] += gain
                terms_ref[1:2, :] += shift
                out_ref[...] = g_ref[...] + part

    rows = pl.BlockSpec((SEQ, width), lambda r: (r, 0))

    def part_rows(n):
        return pl.BlockSpec(
            (SEQ, 3 * width), lambda r: (jnp.clip(r - n * blocks, 0, blocks - 1), 0)
        )

    return pl.pallas_call(
        kernel,
        grid=(count // SEQ,),
        out_shape=(shape_of((count, width), F32), shape_of((2, width), F32)),
        in_specs=[part_rows(n) for n in range(parts)] + [rows, rows, entire(norms), entire(weight)],
        out_specs=(rows, pl.BlockSpec((2, width), lambda r: (0, 0))),
        compiler_params=limits(60),
        cost_estimate=cost(6 * count * width * width, 16 * count * width + 6 * width * width),
    )(*grad_joined, grad_residual, tokens, norms, weight)


def weight_grad(grid, turned, grads, factor, lanes, across, offset, regions, region_lane, region_lanes):
    width, count = turned.shape
    parts = len(grads)
    share = count // parts
    columns = lanes * grid.shard
    region = shape_of((4 * grid.depth, width // grid.dp, region_lanes), BF16)

    def kernel(f_ref, t_ref, *refs):
        near, far, grad, whole, sems, load_sems = refs[parts + len(regions) :]
        pairs = []
        for n in range(parts):
            for s in range(grid.shard):
                source = refs[n].at[:, pl.ds(s * across + offset, lanes)]
                rows = pl.ds(n * share, share)
                pairs.append((source, grad.at[rows, pl.ds(s * lanes, lanes)]))
        run_copies(pairs, load_sems)
        whole[...] = thin(dot(t_ref[...], grad[...]) * f_ref[0, 0])
        run_copies(block_stores(grid, whole, lanes, near, far, region_lane), sems)

    return pl.pallas_call(
        kernel,
        out_shape=(region, region),
        in_specs=[SCALAR, HELD] + [ANYWHERE] * (parts + len(regions)),
        out_specs=(ANYWHERE,) * 2,
        scratch_shapes=[
            pltpu.VMEM((count, columns), BF16),
            pltpu.VMEM((width, columns), BF16),
            pltpu.SemaphoreType.DMA((grid.dp * grid.shard,)),
            pltpu.SemaphoreType.DMA((parts * grid.shard,)),
        ],
        input_output_aliases={2 + parts + n: n for n in range(len(regions))},
        compiler_params=limits(60),
        cost_estimate=cost(
            2 * count * width * columns, 2 * (width * count + (width + count) * columns)
        ),
    )(factor, turned, *grads, *regions)


def adam_update(master, moment, square, gradient, rate):
    new_moment = BETA_FIRST * moment + (1.0 - BETA_FIRST) * gradient
    new_square = BETA_SECOND * square + (1.0 - BETA_SECOND) * gradient * gradient
    bias_first = 1.0 - BETA_FIRST**STEP
    bias_second = 1.0 - BETA_SECOND**STEP
    update = new_moment / bias_first / (jnp.sqrt(new_square / bias_second) + ADAM_EPSILON)
    new_master = master - rate * (update + WEIGHT_DECAY * master)
    return (new_master, new_moment, new_square)


def local(
    grid,
    tokens,
    cotangent,
    segment_ids,
    group_counts,
    master_qkv,
    master_out,
    master_up,
    master_down,
    moment_qkv,
    moment_out,
    moment_up,
    moment_down,
    square_qkv,
    square_out,
    square_up,
    square_down,
    norm_params,
    norm_moment,
    norm_square,
):
    rows, out_lanes = master_up.shape[0], master_out.shape[1]
    qkv_lanes = master_qkv.shape[1]
    chunks = master_down.shape[0] // rows
    up_lanes = master_up.shape[1] // chunks
    down_lanes = master_down.shape[1]
    per_shard = grid.dp // grid.shard
    blocks = tokens.shape[0] // SEQ
    both_lanes = up_lanes + down_lanes

    up_cut = thin(master_up).reshape(rows, per_shard, chunks, up_lanes // per_shard)
    down_cut = thin(master_down).reshape(chunks, rows, down_lanes)
    cuts = (qkv_lanes - out_lanes, out_lanes)

    def large(*members):
        parts = []
        for n in members:
            parts += [up_cut[:, :, n].reshape(rows, up_lanes), down_cut[n]]
        return jnp.concatenate(parts, axis=1)

    counts = group_counts.astype(F32)
    own_count = jnp.sum(jnp.where(jnp.arange(counts.shape[0]) == lax.axis_index("dp"), counts, 0.0))
    factor = own_count * counts.shape[0] / jnp.sum(counts)
    factor_cell = factor.reshape(1, 1)
    seg_column = segment_ids[:, None]
    seg_row = segment_ids.reshape(blocks, 1, SEQ)

    piece = jnp.concatenate([thin(master_qkv[:, cuts[0] :]), thin(master_out)], axis=1)
    q0 = grid.gather_z(thin(master_qkv[:, : cuts[0]]))
    q0, piece = tie(grid.both(q0), piece)
    q0_over = grid.gather_xy(q0)
    q1 = grid.gather_z(piece)
    q0_over, q1, piece = tie(q0_over, grid.both(q1), large(0, 1))
    q1_over = grid.gather_xy(q1)
    q0_far = grid.gather_far(q0_over)
    m01 = grid.gather_z(piece)
    q1_over, q0_far, m01 = tie(q1_over, q0_far, m01)
    q0_pieces = grid.gather_end(q0, q0_over, q0_far)
    q1_far = grid.gather_far(q1_over)
    m01 = grid.both(m01)
    q1_far, m01 = tie(q1_far, m01)
    q1_pieces = grid.gather_end(q1, q1_over, q1_far)

    def halves(pair):
        lanes = [slice(n * both_lanes, (n + 1) * both_lanes) for n in range(2)]
        return [[values[:, :, own] for values in pair] for own in lanes]

    m0, m1 = halves(m01)

    q0_pieces, q1_pieces, m0, piece = tie(q0_pieces, q1_pieces, m0, large(2, 3))
    first_turned, joined, qkv_weight = first_projection(
        grid, [q0_pieces, q1_pieces], cuts, tokens, norm_params
    )
    m0_over = grid.gather_xy_joined(m0)
    m23 = grid.z_exchange(grid.copies(piece))

    joined, m0_over, m1 = tie(joined, m0_over, m1)
    mixed_turned, logs, residual, second, second_turned = attention(
        grid, q1_pieces, cuts[1], joined, seg_column, seg_row, tokens, norm_params
    )
    m0_far = grid.gather_far_joined(m0_over)
    m1_over = grid.gather_xy_joined(m1)
    second, m0_far, m1_over, m23 = tie(second, m0_far, m1_over, m23)
    m0_pieces = grid.gather_end_joined(m0, m0_over, m0_far)
    m2, m3 = halves(grid.both(m23))

    def chunk(weights, sums, regions, place, turned):
        out_sum, back_sum, near, far = feed_forward(
            grid, weights, second, second_turned, cotangent, factor_cell, sums, regions,
            place * both_lanes, 2 * both_lanes, up_lanes, down_lanes, turned,
        )
        return (out_sum, back_sum), (near, far)

    second, m0_pieces, m1_over, m2 = tie(second, m0_pieces, m1_over, m2)
    sums, r0 = chunk(m0_pieces, (), (), 0, True)
    m1_far = grid.gather_far_joined(m1_over)
    m2_over = grid.gather_xy_joined(m2)
    sums, m1_far, m2_over = tie(sums, m1_far, m2_over)
    m1_pieces = grid.gather_end_joined(m1, m1_over, m1_far)

    sums, m1_pieces, m2_over, m3 = tie(sums, m1_pieces, m2_over, m3)
    sums, r0 = chunk(m1_pieces, sums, r0, 1, True)
    m2_far = grid.gather_far_joined(m2_over)
    m3_over = grid.gather_xy_joined(m3)
    sums, m2_far, m3_over = tie(sums, m2_far, m3_over)
    m2_pieces = grid.gather_end_joined(m2, m2_over, m2_far)

    sums, m2_pieces, r0, m3_over = tie(sums, m2_pieces, r0, m3_over)
    sums, r1 = chunk(m2_pieces, sums, (), 0, False)
    r0_other = grid.scatter_core(r0[1])
    m3_far = grid.gather_far_joined(m3_over)
    sums, m3_far, r0_other = tie(sums, m3_far, r0_other)
    m3_pieces = grid.gather_end_joined(m3, m3_over, m3_far)

    sums, r0_other, m3_pieces = tie(sums, r0_other, m3_pieces)
    sums, r1 = chunk(m3_pieces, sums, r1, 1, False)
    r0_far = grid.scatter_far(r0[0], r0_other)

    sums, r0_far, r1 = tie(sums, r0_far, r1)
    block_out, grad_residual, grad_attention, grad_mixed, second_terms = second_norm_back(
        grid, q1_pieces, cuts[1], sums, residual, cotangent, norm_params
    )
    r0_over = grid.scatter_xy(r0[0], r0_other, r0_far)
    r1_other = grid.scatter_core(r1[1])
    q1 = weight_grad(
        grid, mixed_turned, [grad_attention], factor_cell, out_lanes, out_lanes, 0,
        (), cuts[1], cuts[1] + out_lanes,
    )

    grad_mixed, r0_over, r1_other, q1 = tie(grad_mixed, r0_over, r1_other, q1)
    grad_joined = [attention_back(0, blocks // 2, joined, grad_mixed, logs, seg_column, seg_row)]
    r1_far = grid.scatter_far(r1[0], r1_other)
    r0_passed = grid.scatter_home(r0_over)
    grad_mixed, grad_joined, r1_far, r0_passed = tie(grad_mixed, grad_joined, r1_far, r0_passed)
    grad_joined.append(
        attention_back(blocks // 2, blocks // 2, joined, grad_mixed, logs, seg_column, seg_row)
    )
    r1_over = grid.scatter_xy(r1[0], r1_other, r1_far)
    r0_sent = grid.scatter_z(r0[0], r0_other, r0_over, r0_passed)
    q0 = weight_grad(
        grid, first_turned, grad_joined, factor_cell, cuts[0], qkv_lanes, 0, (), 0, cuts[0]
    )
    grad_joined, q0, r1_over, r0_sent = tie(grad_joined, q0, r1_over, r0_sent)
    q0_other = grid.scatter_core(q0[1])
    r1_passed = grid.scatter_home(r1_over)
    q1 = weight_grad(
        grid, first_turned, grad_joined, factor_cell, cuts[1], qkv_lanes, cuts[0],
        q1, 0, cuts[1] + out_lanes,
    )

    grad_joined, q0_other, q1, r1_passed = tie(grad_joined, q0_other, q1, r1_passed)
    q0_far = grid.scatter_far(q0[0], q0_other)
    q1_other = grid.scatter_core(q1[1])
    q0_far, q1_other = tie(q0_far, q1_other)
    q0_over = grid.scatter_xy(q0[0], q0_other, q0_far)
    q1_far = grid.scatter_far(q1[0], q1_other)
    r1_sent = grid.scatter_z(r1[0], r1_other, r1_over, r1_passed)
    input_grad, first_terms = first_norm_back(
        grad_joined, grad_residual, tokens, norm_params, qkv_weight
    )
    first_terms, q0_over, q1_far = tie(first_terms, q0_over, q1_far)
    q0_passed = grid.scatter_home(q0_over)
    q1_over = grid.scatter_xy(q1[0], q1_other, q1_far)
    q0_sent = grid.scatter_z(q0[0], q0_other, q0_over, q0_passed)
    terms = jnp.concatenate([first_terms, second_terms]) * factor
    terms = grid.total(terms, "shard")
    q1_over, terms = tie(q1_over, terms)
    q1_passed = grid.scatter_home(q1_over)
    q1_sent = grid.scatter_z(q1[0], q1_other, q1_over, q1_passed)
    norm_grad = grid.total(terms, "dp")
    q0_total, q1_total = grid.scatter_end(q0_sent), grid.scatter_end(q1_sent)
    grad_qkv = jnp.concatenate([q0_total, q1_total[:, : cuts[1]]], axis=1)
    grad_out = q1_total[:, cuts[1] :]
    totals = [grid.scatter_end(r0_sent), grid.scatter_end(r1_sent)]

    def pieces_of(first, lanes):
        return [
            t[:, i * both_lanes + first : i * both_lanes + first + lanes]
            for t in totals
            for i in range(chunks // 2)
        ]

    grad_up = jnp.stack(
        [piece.reshape(rows, per_shard, -1) for piece in pieces_of(0, up_lanes)], axis=2
    ).reshape(master_up.shape)
    grad_down = jnp.concatenate(pieces_of(up_lanes, down_lanes))
    new_qkv, new_moment_qkv, new_square_qkv = adam_update(
        master_qkv, moment_qkv, square_qkv, grad_qkv, RATE_MATRIX
    )
    new_out, new_moment_out, new_square_out = adam_update(
        master_out, moment_out, square_out, grad_out, RATE_OUTPUT
    )
    new_up, new_moment_up, new_square_up = adam_update(
        master_up, moment_up, square_up, grad_up, RATE_MATRIX
    )
    new_down, new_moment_down, new_square_down = adam_update(
        master_down, moment_down, square_down, grad_down, RATE_MATRIX
    )
    new_norm, new_norm_moment, new_norm_square = adam_update(
        norm_params, norm_moment, norm_square, norm_grad, RATE_NORMS
    )
    return (
        block_out,
        input_grad,
        grad_qkv,
        grad_out,
        grad_up,
        grad_down,
        new_qkv,
        new_out,
        new_up,
        new_down,
        new_moment_qkv,
        new_moment_out,
        new_moment_up,
        new_moment_down,
        new_square_qkv,
        new_square_out,
        new_square_up,
        new_square_down,
        thin(new_qkv),
        thin(new_out),
        thin(new_up),
        thin(new_down),
        norm_grad,
        new_norm,
        new_norm_moment,
        new_norm_square,
    )


def solution(mesh):
    rows = P(("dp", "shard"), None)
    owned = P("dp", "shard")
    in_specs = (rows, rows, P(("dp", "shard")), P()) + (owned,) * 12 + (P(),) * 3
    out_specs = (rows, rows) + (owned,) * 20 + (P(),) * 4
    step = functools.partial(local, Grid(mesh.shape["dp"], mesh.shape["shard"]))
    return jax.shard_map(step, mesh=mesh, in_specs=in_specs, out_specs=out_specs, check_vma=False)
```

```python
import functools
import math

import jax
import jax.numpy as jnp
from jax import lax
from jax.experimental import pallas as pl
from jax.experimental.pallas import tpu as pltpu
from jax.sharding import PartitionSpec as P

HEADS = 16
HD = 64
SEQ = 256
STEP = 3

NORM_EPSILON = 1e-06
BETA_FIRST = 0.5
BETA_SECOND = 0.5
ADAM_EPSILON = 1e-08
RATE_MATRIX = 0.02
RATE_OUTPUT = 0.1
RATE_NORMS = 0.3
WEIGHT_DECAY = 0.01
MASK_FILL = -1000000000.0
SCALING = 1.0 / math.sqrt(HD)
PLAIN = (((1,), (0,)), ((), ()))
TRANSPOSED = (((1,), (1,)), ((), ()))
LEADING = (((0,), (0,)), ((), ()))

F32 = jnp.float32
BF16 = jnp.bfloat16
MIB = 2**20


def dot(left, right, dims=PLAIN):
    return lax.dot_general(left, right, dims, preferred_element_type=F32)


def wide(values):
    return values.astype(F32)


def thin(values):
    return values.astype(BF16)


def shape_of(dims, dtype):
    return jax.ShapeDtypeStruct(dims, dtype)


def limits(mib):
    return pltpu.CompilerParams(vmem_limit_bytes=mib * MIB)


def cost(flops, moved, transcendentals=0):
    return pl.CostEstimate(flops=flops, bytes_accessed=moved, transcendentals=transcendentals)


def entire(array):
    return pl.BlockSpec(array.shape, lambda *_: (0,) * array.ndim)


class Grid:
    def __init__(self, dp, shard):
        self.dp, self.shard, self.depth = dp, shard, dp // 2

    def core_swap(self, values):
        return lax.ppermute(values, "shard", [(i, i ^ 1) for i in range(self.shard)])

    def cross(self, values, turned):
        pairs = []
        for d in range(self.dp):
            for s in range(self.shard):
                along_x = (s % 2 == 0) != turned
                other = (d ^ 1, s) if along_x else (d, s ^ 2)
                pairs.append((d * self.shard + s, other[0] * self.shard + other[1]))
        return lax.ppermute(values, ("dp", "shard"), pairs)

    def z_exchange(self, values):
        groups = [[z * 2 + x for z in range(self.depth)] for x in range(2)]
        return lax.all_to_all(values, "dp", 0, 0, axis_index_groups=groups, tiled=True)

    def total(self, values, axis):
        size = self.shard if axis == "shard" else self.dp
        for bit in range((size - 1).bit_length()):
            pairs = [(i, i ^ (1 << bit)) for i in range(size)]
            values = values + lax.ppermute(values, axis, pairs)
        return values


    def copies(self, piece):
        return jnp.broadcast_to(piece, (self.depth, *piece.shape))

    def gather_z(self, piece):
        parts = [piece]
        for k in range(1, self.depth):
            shift = [((i // 2 + k) % self.depth * 2 + i % 2, i) for i in range(self.dp)]
            parts.append(lax.ppermute(piece, "dp", shift))
        return jnp.stack(parts)

    def both(self, near):
        return near, self.core_swap(near)

    def gather_xy(self, near):
        return [self.cross(values, False) for values in near]

    def gather_far(self, over):
        return self.cross(over[0], True)

    def gather_end(self, near, over, far):
        mine = [*over, far]
        return [*near, *mine, *[self.core_swap(values) for values in mine]]


    def gather_xy_joined(self, near):
        return self.cross(jnp.concatenate(near), False)

    def gather_far_joined(self, over):
        return self.cross(over[: self.depth], True)

    def gather_end_joined(self, near, over, far):
        return [*near, over, far, self.core_swap(over), self.core_swap(far)]

    def owner(self, z, dx, dy, dc):
        index_dp, index_shard = lax.axis_index("dp"), lax.axis_index("shard")
        x, y, c = index_dp % 2, index_shard // 2, index_shard % 2
        row = z * 2 + lax.rem(x + dx, 2)
        column = lax.rem(y + dy, 2) * 2 + lax.rem(c + dc, 2)
        return row, column

    def gathered_places(self, turned, joined):
        where = (2, 2, 4, 4, 3, 5) if joined else (2, 3, 5, 6, 4, 7)
        skip = self.depth if joined else 0
        core = lax.rem(lax.axis_index("shard"), 2)
        own = lax.axis_index("dp") // 2
        places = []
        for k in range(self.depth):
            z = lax.rem(own + k, self.depth) if turned else k
            for side in range(2):
                places.append((side, k, self.owner(z, 0, 0, side)))
                beyond = side * skip + k
                places.append((where[side], beyond, self.owner(z, 1 - core, core, side)))
                places.append((where[2 + side], beyond, self.owner(z, core, 1 - core, 1 - side)))
            places.append((where[4], k, self.owner(z, 1, 1, 0)))
            places.append((where[5], k, self.owner(z, 1, 1, 1)))
        return places

    def region(self, other):
        core = lax.rem(lax.axis_index("shard"), 2)
        role = 1 - core if other else core
        flip = 1 if other else 0
        depth = range(self.depth)
        blocks = [self.owner(k, 1 - role, role, (flip + side) % 2) for side in range(2) for k in depth]
        blocks += [self.owner(k, 1, 1, flip) for k in depth]
        return blocks + [self.owner(k, 0, 0, flip) for k in depth]


    def scatter_core(self, far):
        return self.core_swap(far)

    def scatter_far(self, near, other):
        corner = slice(2 * self.depth, 3 * self.depth)
        return self.cross(thin(wide(near[corner]) + wide(other[corner])), True)

    def scatter_xy(self, near, other, far):
        d = self.depth
        first = wide(near[:d]) + wide(other[:d]) + wide(far)
        second = wide(near[d : 2 * d]) + wide(other[d : 2 * d])
        return [self.cross(thin(second), False), self.cross(thin(first), False)][::-1]

    def scatter_home(self, over):
        return self.core_swap(over[1])

    def scatter_z(self, near, other, over, passed):
        d = self.depth
        home = slice(3 * d, 4 * d)
        here = wide(near[home]) + wide(other[home]) + wide(over[0]) + wide(passed)
        return self.z_exchange(thin(here))

    def scatter_end(self, sent):
        return jnp.sum(wide(sent), axis=0)


def tie(*values):
    return lax.optimization_barrier(values)


def block(ref, row, rows, column, columns):
    return ref.at[
        pl.ds(pl.multiple_of(row, rows), rows), pl.ds(pl.multiple_of(column, columns), columns)
    ]


def start_copies(pairs, sems):
    copies = [pltpu.make_async_copy(a, b, sems.at[n]) for n, (a, b) in enumerate(pairs)]
    for copy in copies:
        copy.start()
    return copies


def run_copies(pairs, sems):
    for copy in start_copies(pairs, sems):
        copy.wait()


def piece_loads(grid, refs, lane, target, lanes, across, offset, turned=True):
    rows = target.shape[0] // grid.dp
    pairs = []
    for i, place, (row, column) in grid.gathered_places(turned, len(refs) == 6):
        source = refs[i].at[place, :, pl.ds(lane, lanes)]
        pairs.append((source, block(target, row * rows, rows, column * across + offset, lanes)))
    return pairs


def block_stores(grid, source, lanes, near, far, lane):
    rows = source.shape[0] // grid.dp
    pairs = []
    for other in (1, 0):
        for n, (row, column) in enumerate(grid.region(other)):
            taken = block(source, row * rows, rows, column * lanes, lanes)
            pairs.append((taken, (near, far)[other].at[n, :, pl.ds(lane, lanes)]))
    return pairs


ANYWHERE = pl.BlockSpec(memory_space=pl.ANY)
SCALAR = pl.BlockSpec(memory_space=pltpu.SMEM)
HELD = pl.BlockSpec(memory_space=pltpu.VMEM)


def standardised(values):
    centred = values - jnp.mean(values, axis=-1, keepdims=True)
    inverse = lax.rsqrt(jnp.mean(centred * centred, axis=-1, keepdims=True) + NORM_EPSILON)
    return centred * inverse, inverse


def norm_back(grad, values, gain):
    n, inverse = standardised(values)
    scaled = grad * gain
    mean_scaled = jnp.mean(scaled, axis=-1, keepdims=True)
    mean_product = jnp.mean(scaled * n, axis=-1, keepdims=True)
    grad_values = inverse * (scaled - mean_scaled - n * mean_product)
    return (
        grad_values,
        jnp.sum(grad * n, axis=0, keepdims=True),
        jnp.sum(grad, axis=0, keepdims=True),
    )


def first_projection(grid, sets, cuts, tokens, norms):
    count, width = tokens.shape
    halves = len(sets)
    each = len(sets[0])
    across = sum(cuts)
    columns = across * grid.shard
    owners = grid.dp * grid.shard
    tile = width

    def kernel(x_ref, p_ref, *refs):
        sources, rest = refs[: halves * each], refs[halves * each :]
        turned_ref, joined_hbm, weight_hbm, weight, first, joined, sems, out_sems = rest
        pairs = []
        for n in range(halves):
            pieces = sources[n * each : (n + 1) * each]
            pairs += piece_loads(grid, pieces, 0, weight, cuts[n], across, sum(cuts[:n]))
        loads = start_copies(pairs, sems)

        @pl.loop(0, count, step=SEQ)
        def _(i):
            rows = pl.ds(pl.multiple_of(i, SEQ), SEQ)
            n, _ = standardised(wide(x_ref[rows, :]))
            value = thin(n * p_ref[0:1, :] + p_ref[1:2, :])
            first[rows, :] = value
            turned_ref[:, rows] = value.T

        for load in loads:
            load.wait()
        leaving = start_copies([(weight, weight_hbm)], out_sems)
        for n in range(columns // tile):
            own = slice(n * tile, (n + 1) * tile)
            joined[:, own] = thin(dot(first[...], weight[:, own]))
            pair = (joined.at[:, own], joined_hbm.at[:, own])
            leaving += start_copies([pair], out_sems.at[pl.ds(1 + n, 1)])
        for copy in leaving:
            copy.wait()

    return pl.pallas_call(
        kernel,
        out_shape=(
            shape_of((width, count), BF16),
            shape_of((count, columns), BF16),
            shape_of((width, columns), BF16),
        ),
        in_specs=[HELD, HELD] + [ANYWHERE] * (halves * each),
        out_specs=(HELD, ANYWHERE, ANYWHERE),
        scratch_shapes=[
            pltpu.VMEM((width, columns), BF16),
            pltpu.VMEM((count, width), BF16),
            pltpu.VMEM((count, columns), BF16),
            pltpu.SemaphoreType.DMA((halves * owners,)),
            pltpu.SemaphoreType.DMA((1 + columns // tile,)),
        ],
        compiler_params=limits(60),
        cost_estimate=cost(2 * count * width * columns, 4 * (width + count) * columns),
    )(tokens, norms, *[array for pieces in sets for array in pieces])


def attention(grid, pieces, lane, joined, seg_column, seg_row, tokens, norms):
    count, width = tokens.shape

    def kernel(
        j_ref, sc_ref, sr_ref, x_ref, p_ref, *refs,
    ):
        sources, rest = refs[: len(pieces)], refs[len(pieces) :]
        turned_ref, log_ref, res_ref, second_ref, second_turned_ref, mixed, weight, sems = rest
        lanes = width // grid.shard
        step = pl.program_id(0)

        @pl.when(step == 0)
        def _():
            start_copies(piece_loads(grid, sources, lane, weight, lanes, lanes, 0), sems)

        same = sc_ref[...] == sr_ref[0]
        left = lax.broadcasted_iota(jnp.int32, (SEQ, 2 * HD), 1) < HD
        for pair in range(HEADS // 2):
            a, b = pair * 2 * HD, (pair + 1) * 2 * HD
            query, key = j_ref[:, a:b], j_ref[:, width + a : width + b]
            value = j_ref[:, 2 * width + a : 2 * width + b]
            results = []
            for side in range(2):
                own_key = jnp.where(left == (side == 0), key, jnp.zeros_like(key))
                scores = jnp.where(same, dot(own_key, query, TRANSPOSED) * SCALING, MASK_FILL)
                top = jnp.max(scores, axis=0, keepdims=True)
                raised = jnp.exp(scores - top)
                total = jnp.sum(raised, axis=0, keepdims=True)
                head = 2 * pair + side
                log_ref[0, head : head + 1, :] = top + jnp.log(total)
                results.append(dot(thin(raised * (1.0 / total)), value, LEADING))
            mixed[:, a:b] = thin(jnp.where(left, results[0], results[1]))
        turned_ref[...] = mixed[...].T

        @pl.when(step == 0)
        def _():
            for n, (a, b) in enumerate(piece_loads(grid, sources, lane, weight, lanes, lanes, 0)):
                pltpu.make_async_copy(a, b, sems.at[n]).wait()

        residual = wide(x_ref[...]) + dot(mixed[...], weight[...])
        res_ref[...] = residual
        n, _ = standardised(residual)
        second = thin(n * p_ref[2:3, :] + p_ref[3:4, :])
        second_ref[...] = second
        second_turned_ref[...] = second.T

    blocks = count // SEQ

    def rows(columns):
        return pl.BlockSpec((SEQ, columns), lambda r: (r, 0))

    turned = pl.BlockSpec((width, SEQ), lambda r: (0, r))
    return pl.pallas_call(
        kernel,
        grid=(blocks,),
        out_shape=(
            shape_of((width, count), BF16),
            shape_of((blocks, HEADS, SEQ), F32),
            shape_of((count, width), F32),
            shape_of((count, width), BF16),
            shape_of((width, count), BF16),
        ),
        in_specs=[
            rows(3 * width),
            rows(1),
            pl.BlockSpec((1, 1, SEQ), lambda r: (r, 0, 0)),
            rows(width),
            entire(norms),
        ]
        + [ANYWHERE] * len(pieces),
        out_specs=(
            turned,
            pl.BlockSpec((1, HEADS, SEQ), lambda r: (r, 0, 0)),
            rows(width),
            rows(width),
            turned,
        ),
        scratch_shapes=[
            pltpu.VMEM((SEQ, width), BF16),
            pltpu.VMEM((width, width), BF16),
            pltpu.SemaphoreType.DMA((grid.dp * grid.shard,)),
        ],
        compiler_params=limits(60),
        cost_estimate=cost(
            4 * count * width * width + 16 * count * SEQ * width,
            20 * count * width,
            count * SEQ * HEADS,
        ),
    )(joined, seg_column, seg_row, tokens, norms, *pieces)


def gelu_and_slope(values):
    below = 0.5 * (1.0 + lax.erf(values * (1.0 / math.sqrt(2.0))))
    density = jnp.exp(-0.5 * values * values) * (1.0 / math.sqrt(2.0 * math.pi))
    return values * below, below + values * density


def feed_forward(grid, pieces, second, second_turned, cotangent, factor, sums, regions,
                 region_lane, region_lanes, up_lanes, down_lanes, turned):
    count, width = second.shape
    columns = up_lanes * grid.shard
    rows = width // grid.dp
    owners = grid.dp * grid.shard
    region = shape_of((4 * grid.depth, rows, region_lanes), BF16)
    used = len(pieces)

    def kernel(f_ref, s_hbm, st_hbm, c_hbm, *refs):
        sources, rest = refs[:used], refs[used:]
        if sums:
            out_in, back_in = rest[:2]
        (
            out_hbm, back_hbm, near, far, s_ref, st_ref, c_ref, up, down, out_sum, back_sum, hidden, grads,
            gu, gd, sems, sum_sems, row_sems,
        ) = rest[len(sums) + len(regions) :]
        up_sems, down_sems = sems.at[pl.ds(0, owners)], sems.at[pl.ds(owners, owners)]
        up_loads = start_copies([(s_hbm, s_ref)], row_sems.at[pl.ds(0, 1)])
        up_loads += start_copies(piece_loads(grid, sources, 0, up, up_lanes, up_lanes, 0, turned), up_sems)
        down_loads = start_copies([(c_hbm, c_ref)], row_sems.at[pl.ds(1, 1)])
        down_loads += start_copies(
            piece_loads(grid, sources, up_lanes, down, down_lanes, down_lanes, 0, turned), down_sems
        )
        if sums:
            arriving = start_copies([(out_in, out_sum), (back_in, back_sum)], sum_sems)
        turned_load = start_copies([(st_hbm, st_ref)], row_sems.at[pl.ds(2, 1)])
        for load in up_loads:
            load.wait()
        value, slope = gelu_and_slope(dot(s_ref[...], up[...]))
        for load in down_loads:
            load.wait()
        hidden[...] = thin(value)
        grads[...] = thin(dot(c_ref[...], down[...], TRANSPOSED) * slope)
        if sums:
            for copy in arriving:
                copy.wait()
            out_sum[...] += dot(hidden[...], down[...])
            back_sum[...] += dot(grads[...], up[...], TRANSPOSED)
        else:
            out_sum[...] = dot(hidden[...], down[...])
            back_sum[...] = dot(grads[...], up[...], TRANSPOSED)
        leaving = start_copies([(out_sum, out_hbm), (back_sum, back_hbm)], sum_sems)
        turned_load[0].wait()
        gu[...] = thin(dot(st_ref[...], grads[...]) * f_ref[0, 0])
        leaving += start_copies(block_stores(grid, gu, up_lanes, near, far, region_lane), up_sems)
        gd[...] = thin(dot(hidden[...], c_ref[...], LEADING) * f_ref[0, 0])
        leaving += start_copies(
            block_stores(grid, gd, down_lanes, near, far, region_lane + up_lanes), down_sems
        )
        for copy in leaving:
            copy.wait()

    aliases = {4 + used + n: n for n in range(len(sums))}
    aliases |= {4 + used + len(sums) + n: 2 + n for n in range(len(regions))}
    return pl.pallas_call(
        kernel,
        out_shape=(shape_of((count, width), F32),) * 2 + (region, region),
        in_specs=[SCALAR] + [ANYWHERE] * (3 + used + len(sums) + len(regions)),
        out_specs=(ANYWHERE,) * 4,
        scratch_shapes=[
            pltpu.VMEM((count, width), BF16),
            pltpu.VMEM((width, count), BF16),
            pltpu.VMEM((count, width), BF16),
            pltpu.VMEM((width, columns), BF16),
            pltpu.VMEM((columns, width), BF16),
            pltpu.VMEM((count, width), F32),
            pltpu.VMEM((count, width), F32),
            pltpu.VMEM((count, columns), BF16),
            pltpu.VMEM((count, columns), BF16),
            pltpu.VMEM((width, columns), BF16),
            pltpu.VMEM((columns, width), BF16),
            pltpu.SemaphoreType.DMA((2 * owners,)),
            pltpu.SemaphoreType.DMA((2,)),
            pltpu.SemaphoreType.DMA((3,)),
        ],
        input_output_aliases=aliases,
        compiler_params=limits(60),
        cost_estimate=cost(
            12 * count * width * columns,
            8 * width * columns + 22 * count * width,
            2 * count * columns,
        ),
    )(factor, second, second_turned, cotangent, *pieces, *sums, *regions)


def second_norm_back(grid, pieces, lane, sums, residual, cotangent, norms):
    out_sum, back_sum = sums
    count, width = residual.shape

    def kernel(o_ref, b_ref, res_ref, c_ref, p_ref, *refs):
        sources, rest = refs[: len(pieces)], refs[len(pieces) :]
        out_ref, grad_ref, ga_ref, gm_ref, terms_ref, weight, sems = rest
        lanes = width // grid.shard

        @pl.when(pl.program_id(0) == 0)
        def _():
            terms_ref[...] = jnp.zeros_like(terms_ref)
            run_copies(piece_loads(grid, sources, lane, weight, lanes, lanes, 0), sems)

        residual = res_ref[...]
        out_ref[...] = thin(residual + o_ref[...])
        part, gain, shift = norm_back(b_ref[...], residual, p_ref[2:3, :])
        terms_ref[0:1, :] += gain
        terms_ref[1:2, :] += shift
        grad = wide(c_ref[...]) + part
        grad_ref[...] = grad
        ga_ref[...] = thin(grad)
        gm_ref[...] = thin(dot(ga_ref[...], weight[...], TRANSPOSED))

    rows = pl.BlockSpec((SEQ, width), lambda r: (r, 0))
    return pl.pallas_call(
        kernel,
        grid=(count // SEQ,),
        out_shape=(
            shape_of((count, width), BF16),
            shape_of((count, width), F32),
            shape_of((count, width), BF16),
            shape_of((count, width), BF16),
            shape_of((2, width), F32),
        ),
        in_specs=[rows, rows, rows, rows, entire(norms)] + [ANYWHERE] * len(pieces),
        out_specs=(rows, rows, rows, rows, pl.BlockSpec((2, width), lambda r: (0, 0))),
        scratch_shapes=[
            pltpu.VMEM((width, width), BF16),
            pltpu.SemaphoreType.DMA((grid.dp * grid.shard,)),
        ],
        compiler_params=limits(60),
        cost_estimate=cost(2 * count * width * width, 24 * count * width),
    )(out_sum, back_sum, residual, cotangent, norms, *pieces)


def attention_back(first, blocks, joined, grad_mixed, logs, seg_column, seg_row):
    width = grad_mixed.shape[1]
    count = blocks * SEQ

    def kernel(j_ref, gm_ref, log_ref, sc_ref, sr_ref, gj_ref):
        same = sc_ref[...] == sr_ref[0]
        left = lax.broadcasted_iota(jnp.int32, (SEQ, 2 * HD), 1) < HD
        for pair in range(HEADS // 2):
            a, b = pair * 2 * HD, (pair + 1) * 2 * HD
            query, key = j_ref[:, a:b], j_ref[:, width + a : width + b]
            value, grad = j_ref[:, 2 * width + a : 2 * width + b], gm_ref[:, a:b]
            turned_key = key.T
            grad_query, results = [], []
            for side in range(2):
                chosen = left == (side == 0)
                own_key = jnp.where(chosen, key, jnp.zeros_like(key))
                own_value = jnp.where(chosen, value, jnp.zeros_like(value))
                scores = jnp.where(same, dot(own_key, query, TRANSPOSED) * SCALING, MASK_FILL)
                head = 2 * pair + side
                probs = jnp.exp(scores - log_ref[0, head : head + 1, :])
                grad_probs = dot(own_value, grad, TRANSPOSED)
                delta = jnp.sum(probs * grad_probs, axis=0, keepdims=True)
                grad_scores = thin(probs * (grad_probs - delta))
                grad_query.append(dot(turned_key[side * HD : (side + 1) * HD], grad_scores))
                results.append((dot(grad_scores, query) * SCALING, dot(thin(probs), grad)))
            gj_ref[:, a:b] = thin(jnp.concatenate(grad_query).T * SCALING)
            for n, (even, odd) in enumerate(zip(*results), 1):
                gj_ref[:, n * width + a : n * width + b] = thin(jnp.where(left, even, odd))

    def rows(columns):
        return pl.BlockSpec((SEQ, columns), lambda r: (r + first, 0))

    return pl.pallas_call(
        kernel,
        grid=(blocks,),
        out_shape=shape_of((count, 3 * width), BF16),
        in_specs=[
            rows(3 * width),
            rows(width),
            pl.BlockSpec((1, HEADS, SEQ), lambda r: (r + first, 0, 0)),
            rows(1),
            pl.BlockSpec((1, 1, SEQ), lambda r: (r + first, 0, 0)),
        ],
        out_specs=pl.BlockSpec((SEQ, 3 * width), lambda r: (r, 0)),
        compiler_params=limits(60),
        cost_estimate=cost(40 * count * SEQ * width, 14 * count * width, count * SEQ * HEADS),
    )(joined, grad_mixed, logs, seg_column, seg_row)


def first_norm_back(grad_joined, grad_residual, tokens, norms, weight):
    count, width = tokens.shape
    parts = len(grad_joined)
    blocks = count // SEQ // parts

    def kernel(*refs):
        gj_refs, (g_ref, x_ref, p_ref, w_ref, out_ref, terms_ref) = refs[:parts], refs[parts:]
        step = pl.program_id(0)

        @pl.when(step == 0)
        def _():
            terms_ref[...] = jnp.zeros_like(terms_ref)

        for n in range(parts):

            @pl.when(lax.div(step, blocks) == n)
            def _(n=n):
                grad_first = dot(gj_refs[n][...], w_ref[...], TRANSPOSED)
                part, gain, shift = norm_back(grad_first, wide(x_ref[...]), p_ref[0:1, :])
                terms_ref[0:1, :] += gain
                terms_ref[1:2, :] += shift
                out_ref[...] = g_ref[...] + part

    rows = pl.BlockSpec((SEQ, width), lambda r: (r, 0))

    def part_rows(n):
        return pl.BlockSpec(
            (SEQ, 3 * width), lambda r: (jnp.clip(r - n * blocks, 0, blocks - 1), 0)
        )

    return pl.pallas_call(
        kernel,
        grid=(count // SEQ,),
        out_shape=(shape_of((count, width), F32), shape_of((2, width), F32)),
        in_specs=[part_rows(n) for n in range(parts)] + [rows, rows, entire(norms), entire(weight)],
        out_specs=(rows, pl.BlockSpec((2, width), lambda r: (0, 0))),
        compiler_params=limits(60),
        cost_estimate=cost(6 * count * width * width, 16 * count * width + 6 * width * width),
    )(*grad_joined, grad_residual, tokens, norms, weight)


def weight_grad(grid, turned, grads, factor, lanes, across, offset, regions, region_lane, region_lanes):
    width, count = turned.shape
    parts = len(grads)
    share = count // parts
    columns = lanes * grid.shard
    region = shape_of((4 * grid.depth, width // grid.dp, region_lanes), BF16)

    def kernel(f_ref, t_hbm, *refs):
        near, far, turned_rows, grad, whole, sems, load_sems, row_sems = refs[parts + len(regions) :]
        loads = []
        for s in range(grid.shard):
            if s == 1:
                loads += start_copies([(t_hbm, turned_rows)], row_sems)
            pairs = []
            for n in range(parts):
                source = refs[n].at[:, pl.ds(s * across + offset, lanes)]
                pairs.append((source, grad.at[pl.ds(n * share, share), pl.ds(s * lanes, lanes)]))
            loads.append(start_copies(pairs, load_sems.at[pl.ds(s * parts, parts)]))
        loads = [loads[0], [loads[1]], *loads[2:]]
        for copy in loads[0] + loads[1] + loads[2]:
            copy.wait()
        half = columns // 2
        whole[:, :half] = thin(dot(turned_rows[...], grad[:, :half]) * f_ref[0, 0])
        for copies in loads[3:]:
            for copy in copies:
                copy.wait()
        whole[:, half:] = thin(dot(turned_rows[...], grad[:, half:]) * f_ref[0, 0])
        run_copies(block_stores(grid, whole, lanes, near, far, region_lane), sems)

    return pl.pallas_call(
        kernel,
        out_shape=(region, region),
        in_specs=[SCALAR] + [ANYWHERE] * (1 + parts + len(regions)),
        out_specs=(ANYWHERE,) * 2,
        scratch_shapes=[
            pltpu.VMEM((width, count), BF16),
            pltpu.VMEM((count, columns), BF16),
            pltpu.VMEM((width, columns), BF16),
            pltpu.SemaphoreType.DMA((grid.dp * grid.shard,)),
            pltpu.SemaphoreType.DMA((parts * grid.shard,)),
            pltpu.SemaphoreType.DMA((1,)),
        ],
        input_output_aliases={2 + parts + n: n for n in range(len(regions))},
        compiler_params=limits(60),
        cost_estimate=cost(
            2 * count * width * columns, 2 * (width * count + (width + count) * columns)
        ),
    )(factor, turned, *grads, *regions)


def adam_update(master, moment, square, gradient, rate):
    new_moment = BETA_FIRST * moment + (1.0 - BETA_FIRST) * gradient
    new_square = BETA_SECOND * square + (1.0 - BETA_SECOND) * gradient * gradient
    bias_first = 1.0 - BETA_FIRST**STEP
    bias_second = 1.0 - BETA_SECOND**STEP
    update = new_moment / bias_first / (jnp.sqrt(new_square / bias_second) + ADAM_EPSILON)
    new_master = master - rate * (update + WEIGHT_DECAY * master)
    return (new_master, new_moment, new_square)


def local(
    grid,
    tokens,
    cotangent,
    segment_ids,
    group_counts,
    master_qkv,
    master_out,
    master_up,
    master_down,
    moment_qkv,
    moment_out,
    moment_up,
    moment_down,
    square_qkv,
    square_out,
    square_up,
    square_down,
    norm_params,
    norm_moment,
    norm_square,
):
    rows, out_lanes = master_up.shape[0], master_out.shape[1]
    qkv_lanes = master_qkv.shape[1]
    chunks = master_down.shape[0] // rows
    up_lanes = master_up.shape[1] // chunks
    down_lanes = master_down.shape[1]
    per_shard = grid.dp // grid.shard
    blocks = tokens.shape[0] // SEQ
    both_lanes = up_lanes + down_lanes

    up_cut = thin(master_up).reshape(rows, per_shard, chunks, up_lanes // per_shard)
    down_cut = thin(master_down).reshape(chunks, rows, down_lanes)
    cuts = (qkv_lanes - out_lanes, out_lanes)

    def large(*members):
        parts = []
        for n in members:
            parts += [up_cut[:, :, n].reshape(rows, up_lanes), down_cut[n]]
        return jnp.concatenate(parts, axis=1)

    counts = group_counts.astype(F32)
    own_count = jnp.sum(jnp.where(jnp.arange(counts.shape[0]) == lax.axis_index("dp"), counts, 0.0))
    factor = own_count * counts.shape[0] / jnp.sum(counts)
    factor_cell = factor.reshape(1, 1)
    seg_column = segment_ids[:, None]
    seg_row = segment_ids.reshape(blocks, 1, SEQ)

    piece = jnp.concatenate([thin(master_qkv[:, cuts[0] :]), thin(master_out)], axis=1)
    q0 = grid.gather_z(thin(master_qkv[:, : cuts[0]]))
    q0, piece = tie(grid.both(q0), piece)
    q0_over = grid.gather_xy(q0)
    q1 = grid.gather_z(piece)
    q0_over, q1, piece = tie(q0_over, grid.both(q1), large(0, 1))
    q1_over = grid.gather_xy(q1)
    q0_far = grid.gather_far(q0_over)
    m01 = grid.gather_z(piece)
    q1_over, q0_far, m01, piece = tie(q1_over, q0_far, m01, large(2, 3))
    q0_pieces = grid.gather_end(q0, q0_over, q0_far)
    q1_far = grid.gather_far(q1_over)
    m01 = grid.both(m01)
    m23 = grid.z_exchange(grid.copies(piece))
    q1_far, m01 = tie(q1_far, m01)
    q1_pieces = grid.gather_end(q1, q1_over, q1_far)

    def halves(pair):
        lanes = [slice(n * both_lanes, (n + 1) * both_lanes) for n in range(2)]
        return [[values[:, :, own] for values in pair] for own in lanes]

    m0, m1 = halves(m01)

    q0_pieces, q1_pieces, m0 = tie(q0_pieces, q1_pieces, m0)
    first_turned, joined, qkv_weight = first_projection(
        grid, [q0_pieces, q1_pieces], cuts, tokens, norm_params
    )
    m0_over = grid.gather_xy_joined(m0)

    joined, m0_over, m1, m23 = tie(joined, m0_over, m1, m23)
    m2, m3 = halves(grid.both(m23))
    mixed_turned, logs, residual, second, second_turned = attention(
        grid, q1_pieces, cuts[1], joined, seg_column, seg_row, tokens, norm_params
    )
    m0_far = grid.gather_far_joined(m0_over)
    m1_over = grid.gather_xy_joined(m1)
    second, m0_far, m1_over, m2, m3 = tie(second, m0_far, m1_over, m2, m3)
    m0_pieces = grid.gather_end_joined(m0, m0_over, m0_far)

    def chunk(weights, sums, regions, place, turned):
        out_sum, back_sum, near, far = feed_forward(
            grid, weights, second, second_turned, cotangent, factor_cell, sums, regions,
            place * both_lanes, 2 * both_lanes, up_lanes, down_lanes, turned,
        )
        return (out_sum, back_sum), (near, far)

    second, m0_pieces, m1_over, m2 = tie(second, m0_pieces, m1_over, m2)
    sums, r0 = chunk(m0_pieces, (), (), 0, True)
    m1_far = grid.gather_far_joined(m1_over)
    m2_over = grid.gather_xy_joined(m2)
    sums, m1_far, m2_over = tie(sums, m1_far, m2_over)
    m1_pieces = grid.gather_end_joined(m1, m1_over, m1_far)

    sums, m1_pieces, m2_over, m3 = tie(sums, m1_pieces, m2_over, m3)
    sums, r0 = chunk(m1_pieces, sums, r0, 1, True)
    m2_far = grid.gather_far_joined(m2_over)
    m3_over = grid.gather_xy_joined(m3)
    sums, m2_far, m3_over = tie(sums, m2_far, m3_over)
    m2_pieces = grid.gather_end_joined(m2, m2_over, m2_far)

    sums, m2_pieces, r0, m3_over = tie(sums, m2_pieces, r0, m3_over)
    sums, r1 = chunk(m2_pieces, sums, (), 0, False)
    r0_other = grid.scatter_core(r0[1])
    m3_far = grid.gather_far_joined(m3_over)
    sums, m3_far, r0_other = tie(sums, m3_far, r0_other)
    m3_pieces = grid.gather_end_joined(m3, m3_over, m3_far)

    sums, r0_other, m3_pieces = tie(sums, r0_other, m3_pieces)
    sums, r1 = chunk(m3_pieces, sums, r1, 1, False)
    r0_far = grid.scatter_far(r0[0], r0_other)

    sums, r0_far, r1 = tie(sums, r0_far, r1)
    block_out, grad_residual, grad_attention, grad_mixed, second_terms = second_norm_back(
        grid, q1_pieces, cuts[1], sums, residual, cotangent, norm_params
    )
    r0_over = grid.scatter_xy(r0[0], r0_other, r0_far)
    r1_other = grid.scatter_core(r1[1])
    q1 = weight_grad(
        grid, mixed_turned, [grad_attention], factor_cell, out_lanes, out_lanes, 0,
        (), cuts[1], cuts[1] + out_lanes,
    )

    grad_mixed, r0_over, r1_other, q1 = tie(grad_mixed, r0_over, r1_other, q1)
    grad_joined = [attention_back(0, blocks // 2, joined, grad_mixed, logs, seg_column, seg_row)]
    r1_far = grid.scatter_far(r1[0], r1_other)
    r0_passed = grid.scatter_home(r0_over)
    grad_mixed, grad_joined, r1_far, r0_passed = tie(grad_mixed, grad_joined, r1_far, r0_passed)
    grad_joined.append(
        attention_back(blocks // 2, blocks // 2, joined, grad_mixed, logs, seg_column, seg_row)
    )
    r1_over = grid.scatter_xy(r1[0], r1_other, r1_far)
    r0_sent = grid.scatter_z(r0[0], r0_other, r0_over, r0_passed)
    q0 = weight_grad(
        grid, first_turned, grad_joined, factor_cell, cuts[0], qkv_lanes, 0, (), 0, cuts[0]
    )
    grad_joined, q0, r1_over, r0_sent = tie(grad_joined, q0, r1_over, r0_sent)
    q0_other = grid.scatter_core(q0[1])
    r1_passed = grid.scatter_home(r1_over)
    q1 = weight_grad(
        grid, first_turned, grad_joined, factor_cell, cuts[1], qkv_lanes, cuts[0],
        q1, 0, cuts[1] + out_lanes,
    )

    grad_joined, q0_other, q1, r1_passed = tie(grad_joined, q0_other, q1, r1_passed)
    q0_far = grid.scatter_far(q0[0], q0_other)
    q1_other = grid.scatter_core(q1[1])
    q0_far, q1_other = tie(q0_far, q1_other)
    q0_over = grid.scatter_xy(q0[0], q0_other, q0_far)
    q1_far = grid.scatter_far(q1[0], q1_other)
    r1_sent = grid.scatter_z(r1[0], r1_other, r1_over, r1_passed)
    input_grad, first_terms = first_norm_back(
        grad_joined, grad_residual, tokens, norm_params, qkv_weight
    )
    first_terms, q0_over, q1_far, r1_sent = tie(first_terms, q0_over, q1_far, r1_sent)
    q0_passed = grid.scatter_home(q0_over)
    q1_over = grid.scatter_xy(q1[0], q1_other, q1_far)
    q0_sent = grid.scatter_z(q0[0], q0_other, q0_over, q0_passed)
    terms = jnp.concatenate([first_terms, second_terms]) * factor
    terms = grid.total(terms, "shard")
    q1_over, q0_sent, terms = tie(q1_over, q0_sent, terms)
    q1_passed = grid.scatter_home(q1_over)
    q1_sent = grid.scatter_z(q1[0], q1_other, q1_over, q1_passed)
    norm_grad = grid.total(terms, "dp")
    q0_total, q1_total = grid.scatter_end(q0_sent), grid.scatter_end(q1_sent)
    grad_qkv = jnp.concatenate([q0_total, q1_total[:, : cuts[1]]], axis=1)
    grad_out = q1_total[:, cuts[1] :]
    totals = [grid.scatter_end(r0_sent), grid.scatter_end(r1_sent)]

    def pieces_of(first, lanes):
        return [
            t[:, i * both_lanes + first : i * both_lanes + first + lanes]
            for t in totals
            for i in range(chunks // 2)
        ]

    grad_up = jnp.stack(
        [piece.reshape(rows, per_shard, -1) for piece in pieces_of(0, up_lanes)], axis=2
    ).reshape(master_up.shape)
    grad_down = jnp.concatenate(pieces_of(up_lanes, down_lanes))
    new_qkv, new_moment_qkv, new_square_qkv = adam_update(
        master_qkv, moment_qkv, square_qkv, grad_qkv, RATE_MATRIX
    )
    new_out, new_moment_out, new_square_out = adam_update(
        master_out, moment_out, square_out, grad_out, RATE_OUTPUT
    )
    new_up, new_moment_up, new_square_up = adam_update(
        master_up, moment_up, square_up, grad_up, RATE_MATRIX
    )
    new_down, new_moment_down, new_square_down = adam_update(
        master_down, moment_down, square_down, grad_down, RATE_MATRIX
    )
    new_norm, new_norm_moment, new_norm_square = adam_update(
        norm_params, norm_moment, norm_square, norm_grad, RATE_NORMS
    )
    return (
        block_out,
        input_grad,
        grad_qkv,
        grad_out,
        grad_up,
        grad_down,
        new_qkv,
        new_out,
        new_up,
        new_down,
        new_moment_qkv,
        new_moment_out,
        new_moment_up,
        new_moment_down,
        new_square_qkv,
        new_square_out,
        new_square_up,
        new_square_down,
        thin(new_qkv),
        thin(new_out),
        thin(new_up),
        thin(new_down),
        norm_grad,
        new_norm,
        new_norm_moment,
        new_norm_square,
    )


def solution(mesh):
    rows = P(("dp", "shard"), None)
    owned = P("dp", "shard")
    in_specs = (rows, rows, P(("dp", "shard")), P()) + (owned,) * 12 + (P(),) * 3
    out_specs = (rows, rows) + (owned,) * 20 + (P(),) * 4
    step = functools.partial(local, Grid(mesh.shape["dp"], mesh.shape["shard"]))
    return jax.shard_map(step, mesh=mesh, in_specs=in_specs, out_specs=out_specs, check_vma=False)
```

```python
import functools
import math

import jax
import jax.numpy as jnp
from jax import lax
from jax.experimental import pallas as pl
from jax.experimental.pallas import tpu as pltpu
from jax.sharding import PartitionSpec as P

HEADS = 16
HD = 64
SEQ = 256
STEP = 3

NORM_EPSILON = 1e-06
BETA_FIRST = 0.5
BETA_SECOND = 0.5
ADAM_EPSILON = 1e-08
RATE_MATRIX = 0.02
RATE_OUTPUT = 0.1
RATE_NORMS = 0.3
WEIGHT_DECAY = 0.01
MASK_FILL = -1000000000.0
SCALING = 1.0 / math.sqrt(HD)
PLAIN = (((1,), (0,)), ((), ()))
TRANSPOSED = (((1,), (1,)), ((), ()))
LEADING = (((0,), (0,)), ((), ()))

F32 = jnp.float32
BF16 = jnp.bfloat16
MIB = 2**20


def dot(left, right, dims=PLAIN):
    return lax.dot_general(left, right, dims, preferred_element_type=F32)


def wide(values):
    return values.astype(F32)


def thin(values):
    return values.astype(BF16)


def shape_of(dims, dtype):
    return jax.ShapeDtypeStruct(dims, dtype)


def limits(mib):
    return pltpu.CompilerParams(vmem_limit_bytes=mib * MIB)


def cost(flops, moved, transcendentals=0):
    return pl.CostEstimate(flops=flops, bytes_accessed=moved, transcendentals=transcendentals)


def entire(array):
    return pl.BlockSpec(array.shape, lambda *_: (0,) * array.ndim)


class Grid:
    def __init__(self, dp, shard):
        self.dp, self.shard, self.depth = dp, shard, dp // 2

    def core_swap(self, values):
        return lax.ppermute(values, "shard", [(i, i ^ 1) for i in range(self.shard)])

    def cross(self, values, turned):
        pairs = []
        for d in range(self.dp):
            for s in range(self.shard):
                along_x = (s % 2 == 0) != turned
                other = (d ^ 1, s) if along_x else (d, s ^ 2)
                pairs.append((d * self.shard + s, other[0] * self.shard + other[1]))
        return lax.ppermute(values, ("dp", "shard"), pairs)

    def z_exchange(self, values):
        groups = [[z * 2 + x for z in range(self.depth)] for x in range(2)]
        return lax.all_to_all(values, "dp", 0, 0, axis_index_groups=groups, tiled=True)

    def total(self, values, axis):
        size = self.shard if axis == "shard" else self.dp
        for bit in range((size - 1).bit_length()):
            pairs = [(i, i ^ (1 << bit)) for i in range(size)]
            values = values + lax.ppermute(values, axis, pairs)
        return values


    def copies(self, piece):
        return jnp.broadcast_to(piece, (self.depth, *piece.shape))

    def gather_z(self, piece):
        parts = [piece]
        for k in range(1, self.depth):
            shift = [((i // 2 + k) % self.depth * 2 + i % 2, i) for i in range(self.dp)]
            parts.append(lax.ppermute(piece, "dp", shift))
        return jnp.stack(parts)

    def both(self, near):
        return near, self.core_swap(near)

    def gather_xy(self, near):
        return [self.cross(values, False) for values in near]

    def gather_far(self, over):
        return self.cross(over[0], True)

    def gather_end(self, near, over, far):
        mine = [*over, far]
        return [*near, *mine, *[self.core_swap(values) for values in mine]]


    def gather_xy_joined(self, near):
        return self.cross(jnp.concatenate(near), False)

    def gather_far_joined(self, over):
        return self.cross(over[: self.depth], True)

    def gather_end_joined(self, near, over, far):
        return [*near, over, far, self.core_swap(over), self.core_swap(far)]

    def owner(self, z, dx, dy, dc):
        index_dp, index_shard = lax.axis_index("dp"), lax.axis_index("shard")
        x, y, c = index_dp % 2, index_shard // 2, index_shard % 2
        row = z * 2 + lax.rem(x + dx, 2)
        column = lax.rem(y + dy, 2) * 2 + lax.rem(c + dc, 2)
        return row, column

    def gathered_places(self, turned, joined):
        where = (2, 2, 4, 4, 3, 5) if joined else (2, 3, 5, 6, 4, 7)
        skip = self.depth if joined else 0
        core = lax.rem(lax.axis_index("shard"), 2)
        own = lax.axis_index("dp") // 2
        places = []
        for k in range(self.depth):
            z = lax.rem(own + k, self.depth) if turned else k
            for side in range(2):
                places.append((side, k, self.owner(z, 0, 0, side)))
                beyond = side * skip + k
                places.append((where[side], beyond, self.owner(z, 1 - core, core, side)))
                places.append((where[2 + side], beyond, self.owner(z, core, 1 - core, 1 - side)))
            places.append((where[4], k, self.owner(z, 1, 1, 0)))
            places.append((where[5], k, self.owner(z, 1, 1, 1)))
        return places

    def region(self, other):
        core = lax.rem(lax.axis_index("shard"), 2)
        role = 1 - core if other else core
        flip = 1 if other else 0
        depth = range(self.depth)
        blocks = [self.owner(k, 1 - role, role, (flip + side) % 2) for side in range(2) for k in depth]
        blocks += [self.owner(k, 1, 1, flip) for k in depth]
        return blocks + [self.owner(k, 0, 0, flip) for k in depth]


    def scatter_core(self, far):
        return self.core_swap(far)

    def scatter_far(self, near, other):
        corner = slice(2 * self.depth, 3 * self.depth)
        return self.cross(thin(wide(near[corner]) + wide(other[corner])), True)

    def scatter_xy(self, near, other, far):
        d = self.depth
        first = wide(near[:d]) + wide(other[:d]) + wide(far)
        second = wide(near[d : 2 * d]) + wide(other[d : 2 * d])
        return [self.cross(thin(second), False), self.cross(thin(first), False)][::-1]

    def scatter_home(self, over):
        return self.core_swap(over[1])

    def scatter_z(self, near, other, over, passed):
        d = self.depth
        home = slice(3 * d, 4 * d)
        here = wide(near[home]) + wide(other[home]) + wide(over[0]) + wide(passed)
        return self.z_exchange(thin(here))

    def scatter_end(self, sent):
        return jnp.sum(wide(sent), axis=0)


def tie(*values):
    return lax.optimization_barrier(values)


def block(ref, row, rows, column, columns):
    return ref.at[
        pl.ds(pl.multiple_of(row, rows), rows), pl.ds(pl.multiple_of(column, columns), columns)
    ]


def start_copies(pairs, sems):
    copies = [pltpu.make_async_copy(a, b, sems.at[n]) for n, (a, b) in enumerate(pairs)]
    for copy in copies:
        copy.start()
    return copies


def run_copies(pairs, sems):
    for copy in start_copies(pairs, sems):
        copy.wait()


def piece_loads(grid, refs, lane, target, lanes, across, offset, turned=True):
    rows = target.shape[0] // grid.dp
    pairs = []
    for i, place, (row, column) in grid.gathered_places(turned, len(refs) == 6):
        source = refs[i].at[place, :, pl.ds(lane, lanes)]
        pairs.append((source, block(target, row * rows, rows, column * across + offset, lanes)))
    return pairs


def block_stores(grid, source, lanes, near, far, lane):
    rows = source.shape[0] // grid.dp
    pairs = []
    for other in (1, 0):
        for n, (row, column) in enumerate(grid.region(other)):
            taken = block(source, row * rows, rows, column * lanes, lanes)
            pairs.append((taken, (near, far)[other].at[n, :, pl.ds(lane, lanes)]))
    return pairs


ANYWHERE = pl.BlockSpec(memory_space=pl.ANY)
SCALAR = pl.BlockSpec(memory_space=pltpu.SMEM)
HELD = pl.BlockSpec(memory_space=pltpu.VMEM)


def standardised(values):
    centred = values - jnp.mean(values, axis=-1, keepdims=True)
    inverse = lax.rsqrt(jnp.mean(centred * centred, axis=-1, keepdims=True) + NORM_EPSILON)
    return centred * inverse, inverse


def norm_back(grad, values, gain):
    n, inverse = standardised(values)
    scaled = grad * gain
    mean_scaled = jnp.mean(scaled, axis=-1, keepdims=True)
    mean_product = jnp.mean(scaled * n, axis=-1, keepdims=True)
    grad_values = inverse * (scaled - mean_scaled - n * mean_product)
    return (
        grad_values,
        jnp.sum(grad * n, axis=0, keepdims=True),
        jnp.sum(grad, axis=0, keepdims=True),
    )


def first_projection(grid, sets, cuts, tokens, norms):
    count, width = tokens.shape
    halves = len(sets)
    each = len(sets[0])
    across = sum(cuts)
    columns = across * grid.shard
    owners = grid.dp * grid.shard
    tile = width

    def kernel(x_ref, p_ref, *refs):
        sources, rest = refs[: halves * each], refs[halves * each :]
        turned_ref, joined_hbm, weight_hbm, weight, first, joined, sems, out_sems = rest
        pairs = []
        for n in range(halves):
            pieces = sources[n * each : (n + 1) * each]
            pairs += piece_loads(grid, pieces, 0, weight, cuts[n], across, sum(cuts[:n]))
        loads = start_copies(pairs, sems)

        @pl.loop(0, count, step=SEQ)
        def _(i):
            rows = pl.ds(pl.multiple_of(i, SEQ), SEQ)
            n, _ = standardised(wide(x_ref[rows, :]))
            value = thin(n * p_ref[0:1, :] + p_ref[1:2, :])
            first[rows, :] = value
            turned_ref[:, rows] = value.T

        for load in loads:
            load.wait()
        leaving = start_copies([(weight, weight_hbm)], out_sems)
        for n in range(columns // tile):
            own = slice(n * tile, (n + 1) * tile)
            joined[:, own] = thin(dot(first[...], weight[:, own]))
            pair = (joined.at[:, own], joined_hbm.at[:, own])
            leaving += start_copies([pair], out_sems.at[pl.ds(1 + n, 1)])
        for copy in leaving:
            copy.wait()

    return pl.pallas_call(
        kernel,
        out_shape=(
            shape_of((width, count), BF16),
            shape_of((count, columns), BF16),
            shape_of((width, columns), BF16),
        ),
        in_specs=[HELD, HELD] + [ANYWHERE] * (halves * each),
        out_specs=(HELD, ANYWHERE, ANYWHERE),
        scratch_shapes=[
            pltpu.VMEM((width, columns), BF16),
            pltpu.VMEM((count, width), BF16),
            pltpu.VMEM((count, columns), BF16),
            pltpu.SemaphoreType.DMA((halves * owners,)),
            pltpu.SemaphoreType.DMA((1 + columns // tile,)),
        ],
        compiler_params=limits(60),
        cost_estimate=cost(2 * count * width * columns, 4 * (width + count) * columns),
    )(tokens, norms, *[array for pieces in sets for array in pieces])


def attention(grid, pieces, lane, joined, seg_column, seg_row, tokens, norms):
    count, width = tokens.shape

    def kernel(
        j_ref, sc_ref, sr_ref, x_ref, p_ref, *refs,
    ):
        sources, rest = refs[: len(pieces)], refs[len(pieces) :]
        turned_ref, log_ref, res_ref, second_ref, second_turned_ref, mixed, weight, sems = rest
        lanes = width // grid.shard
        step = pl.program_id(0)

        @pl.when(step == 0)
        def _():
            start_copies(piece_loads(grid, sources, lane, weight, lanes, lanes, 0), sems)

        same = sc_ref[...] == sr_ref[0]
        left = lax.broadcasted_iota(jnp.int32, (SEQ, 2 * HD), 1) < HD
        for pair in range(HEADS // 2):
            a, b = pair * 2 * HD, (pair + 1) * 2 * HD
            query, key = j_ref[:, a:b], j_ref[:, width + a : width + b]
            value = j_ref[:, 2 * width + a : 2 * width + b]
            results = []
            for side in range(2):
                own_key = jnp.where(left == (side == 0), key, jnp.zeros_like(key))
                scores = jnp.where(same, dot(own_key, query, TRANSPOSED) * SCALING, MASK_FILL)
                top = jnp.max(scores, axis=0, keepdims=True)
                raised = jnp.exp(scores - top)
                total = jnp.sum(raised, axis=0, keepdims=True)
                head = 2 * pair + side
                log_ref[0, head : head + 1, :] = top + jnp.log(total)
                results.append(dot(thin(raised * (1.0 / total)), value, LEADING))
            mixed[:, a:b] = thin(jnp.where(left, results[0], results[1]))
        turned_ref[...] = mixed[...].T

        @pl.when(step == 0)
        def _():
            for n, (a, b) in enumerate(piece_loads(grid, sources, lane, weight, lanes, lanes, 0)):
                pltpu.make_async_copy(a, b, sems.at[n]).wait()

        residual = wide(x_ref[...]) + dot(mixed[...], weight[...])
        res_ref[...] = residual
        n, _ = standardised(residual)
        second = thin(n * p_ref[2:3, :] + p_ref[3:4, :])
        second_ref[...] = second
        second_turned_ref[...] = second.T

    blocks = count // SEQ

    def rows(columns):
        return pl.BlockSpec((SEQ, columns), lambda r: (r, 0))

    turned = pl.BlockSpec((width, SEQ), lambda r: (0, r))
    return pl.pallas_call(
        kernel,
        grid=(blocks,),
        out_shape=(
            shape_of((width, count), BF16),
            shape_of((blocks, HEADS, SEQ), F32),
            shape_of((count, width), F32),
            shape_of((count, width), BF16),
            shape_of((width, count), BF16),
        ),
        in_specs=[
            rows(3 * width),
            rows(1),
            pl.BlockSpec((1, 1, SEQ), lambda r: (r, 0, 0)),
            rows(width),
            entire(norms),
        ]
        + [ANYWHERE] * len(pieces),
        out_specs=(
            turned,
            pl.BlockSpec((1, HEADS, SEQ), lambda r: (r, 0, 0)),
            rows(width),
            rows(width),
            turned,
        ),
        scratch_shapes=[
            pltpu.VMEM((SEQ, width), BF16),
            pltpu.VMEM((width, width), BF16),
            pltpu.SemaphoreType.DMA((grid.dp * grid.shard,)),
        ],
        compiler_params=limits(60),
        cost_estimate=cost(
            4 * count * width * width + 16 * count * SEQ * width,
            20 * count * width,
            count * SEQ * HEADS,
        ),
    )(joined, seg_column, seg_row, tokens, norms, *pieces)


def gelu_and_slope(values):
    below = 0.5 * (1.0 + lax.erf(values * (1.0 / math.sqrt(2.0))))
    density = jnp.exp(-0.5 * values * values) * (1.0 / math.sqrt(2.0 * math.pi))
    return values * below, below + values * density


def feed_forward(grid, pieces, second, second_turned, cotangent, factor, sums, regions,
                 region_lane, region_lanes, up_lanes, down_lanes, turned):
    count, width = second.shape
    columns = up_lanes * grid.shard
    rows = width // grid.dp
    owners = grid.dp * grid.shard
    region = shape_of((4 * grid.depth, rows, region_lanes), BF16)
    used = len(pieces)

    def kernel(f_ref, s_hbm, st_hbm, c_hbm, *refs):
        sources, rest = refs[:used], refs[used:]
        if sums:
            out_in, back_in = rest[:2]
        (
            out_hbm, back_hbm, near, far, s_ref, st_ref, c_ref, up, down, out_sum, back_sum, hidden, grads,
            gu, gd, sems, sum_sems, row_sems,
        ) = rest[len(sums) + len(regions) :]
        up_sems, down_sems = sems.at[pl.ds(0, owners)], sems.at[pl.ds(owners, owners)]
        up_loads = start_copies([(s_hbm, s_ref)], row_sems.at[pl.ds(0, 1)])
        up_loads += start_copies(piece_loads(grid, sources, 0, up, up_lanes, up_lanes, 0, turned), up_sems)
        down_loads = start_copies([(c_hbm, c_ref)], row_sems.at[pl.ds(1, 1)])
        down_loads += start_copies(
            piece_loads(grid, sources, up_lanes, down, down_lanes, down_lanes, 0, turned), down_sems
        )
        if sums:
            arriving = start_copies([(out_in, out_sum), (back_in, back_sum)], sum_sems)
        turned_load = start_copies([(st_hbm, st_ref)], row_sems.at[pl.ds(2, 1)])
        for load in up_loads:
            load.wait()
        value, slope = gelu_and_slope(dot(s_ref[...], up[...]))
        for load in down_loads:
            load.wait()
        hidden[...] = thin(value)
        grads[...] = thin(dot(c_ref[...], down[...], TRANSPOSED) * slope)
        if sums:
            for copy in arriving:
                copy.wait()
            out_sum[...] += dot(hidden[...], down[...])
            back_sum[...] += dot(grads[...], up[...], TRANSPOSED)
        else:
            out_sum[...] = dot(hidden[...], down[...])
            back_sum[...] = dot(grads[...], up[...], TRANSPOSED)
        leaving = start_copies([(out_sum, out_hbm), (back_sum, back_hbm)], sum_sems)
        turned_load[0].wait()
        gu[...] = thin(dot(st_ref[...], grads[...]) * f_ref[0, 0])
        leaving += start_copies(block_stores(grid, gu, up_lanes, near, far, region_lane), up_sems)
        gd[...] = thin(dot(hidden[...], c_ref[...], LEADING) * f_ref[0, 0])
        leaving += start_copies(
            block_stores(grid, gd, down_lanes, near, far, region_lane + up_lanes), down_sems
        )
        for copy in leaving:
            copy.wait()

    aliases = {4 + used + n: n for n in range(len(sums))}
    aliases |= {4 + used + len(sums) + n: 2 + n for n in range(len(regions))}
    return pl.pallas_call(
        kernel,
        out_shape=(shape_of((count, width), F32),) * 2 + (region, region),
        in_specs=[SCALAR] + [ANYWHERE] * (3 + used + len(sums) + len(regions)),
        out_specs=(ANYWHERE,) * 4,
        scratch_shapes=[
            pltpu.VMEM((count, width), BF16),
            pltpu.VMEM((width, count), BF16),
            pltpu.VMEM((count, width), BF16),
            pltpu.VMEM((width, columns), BF16),
            pltpu.VMEM((columns, width), BF16),
            pltpu.VMEM((count, width), F32),
            pltpu.VMEM((count, width), F32),
            pltpu.VMEM((count, columns), BF16),
            pltpu.VMEM((count, columns), BF16),
            pltpu.VMEM((width, columns), BF16),
            pltpu.VMEM((columns, width), BF16),
            pltpu.SemaphoreType.DMA((2 * owners,)),
            pltpu.SemaphoreType.DMA((2,)),
            pltpu.SemaphoreType.DMA((3,)),
        ],
        input_output_aliases=aliases,
        compiler_params=limits(60),
        cost_estimate=cost(
            12 * count * width * columns,
            8 * width * columns + 22 * count * width,
            2 * count * columns,
        ),
    )(factor, second, second_turned, cotangent, *pieces, *sums, *regions)


def second_norm_back(grid, pieces, lane, sums, residual, cotangent, norms):
    out_sum, back_sum = sums
    count, width = residual.shape

    def kernel(o_ref, b_ref, res_ref, c_ref, p_ref, *refs):
        sources, rest = refs[: len(pieces)], refs[len(pieces) :]
        out_ref, grad_ref, ga_ref, gm_ref, terms_ref, weight, sems = rest
        lanes = width // grid.shard

        @pl.when(pl.program_id(0) == 0)
        def _():
            terms_ref[...] = jnp.zeros_like(terms_ref)
            run_copies(piece_loads(grid, sources, lane, weight, lanes, lanes, 0), sems)

        residual = res_ref[...]
        out_ref[...] = thin(residual + o_ref[...])
        part, gain, shift = norm_back(b_ref[...], residual, p_ref[2:3, :])
        terms_ref[0:1, :] += gain
        terms_ref[1:2, :] += shift
        grad = wide(c_ref[...]) + part
        grad_ref[...] = grad
        ga_ref[...] = thin(grad)
        gm_ref[...] = thin(dot(ga_ref[...], weight[...], TRANSPOSED))

    rows = pl.BlockSpec((SEQ, width), lambda r: (r, 0))
    return pl.pallas_call(
        kernel,
        grid=(count // SEQ,),
        out_shape=(
            shape_of((count, width), BF16),
            shape_of((count, width), F32),
            shape_of((count, width), BF16),
            shape_of((count, width), BF16),
            shape_of((2, width), F32),
        ),
        in_specs=[rows, rows, rows, rows, entire(norms)] + [ANYWHERE] * len(pieces),
        out_specs=(rows, rows, rows, rows, pl.BlockSpec((2, width), lambda r: (0, 0))),
        scratch_shapes=[
            pltpu.VMEM((width, width), BF16),
            pltpu.SemaphoreType.DMA((grid.dp * grid.shard,)),
        ],
        compiler_params=limits(60),
        cost_estimate=cost(2 * count * width * width, 24 * count * width),
    )(out_sum, back_sum, residual, cotangent, norms, *pieces)


def attention_back(first, blocks, joined, grad_mixed, logs, seg_column, seg_row):
    width = grad_mixed.shape[1]
    count = blocks * SEQ

    def kernel(j_ref, gm_ref, log_ref, sc_ref, sr_ref, gj_ref):
        same = sc_ref[...] == sr_ref[0]
        left = lax.broadcasted_iota(jnp.int32, (SEQ, 2 * HD), 1) < HD
        for pair in range(HEADS // 2):
            a, b = pair * 2 * HD, (pair + 1) * 2 * HD
            query, key = j_ref[:, a:b], j_ref[:, width + a : width + b]
            value, grad = j_ref[:, 2 * width + a : 2 * width + b], gm_ref[:, a:b]
            turned_key = key.T
            grad_query, results = [], []
            for side in range(2):
                chosen = left == (side == 0)
                own_key = jnp.where(chosen, key, jnp.zeros_like(key))
                own_value = jnp.where(chosen, value, jnp.zeros_like(value))
                scores = jnp.where(same, dot(own_key, query, TRANSPOSED) * SCALING, MASK_FILL)
                head = 2 * pair + side
                probs = jnp.exp(scores - log_ref[0, head : head + 1, :])
                grad_probs = dot(own_value, grad, TRANSPOSED)
                delta = jnp.sum(probs * grad_probs, axis=0, keepdims=True)
                grad_scores = thin(probs * (grad_probs - delta))
                grad_query.append(dot(turned_key[side * HD : (side + 1) * HD], grad_scores))
                results.append((dot(grad_scores, query) * SCALING, dot(thin(probs), grad)))
            gj_ref[:, a:b] = thin(jnp.concatenate(grad_query).T * SCALING)
            for n, (even, odd) in enumerate(zip(*results), 1):
                gj_ref[:, n * width + a : n * width + b] = thin(jnp.where(left, even, odd))

    def rows(columns):
        return pl.BlockSpec((SEQ, columns), lambda r: (r + first, 0))

    return pl.pallas_call(
        kernel,
        grid=(blocks,),
        out_shape=shape_of((count, 3 * width), BF16),
        in_specs=[
            rows(3 * width),
            rows(width),
            pl.BlockSpec((1, HEADS, SEQ), lambda r: (r + first, 0, 0)),
            rows(1),
            pl.BlockSpec((1, 1, SEQ), lambda r: (r + first, 0, 0)),
        ],
        out_specs=pl.BlockSpec((SEQ, 3 * width), lambda r: (r, 0)),
        compiler_params=limits(60),
        cost_estimate=cost(40 * count * SEQ * width, 14 * count * width, count * SEQ * HEADS),
    )(joined, grad_mixed, logs, seg_column, seg_row)


def first_norm_back(grad_joined, grad_residual, tokens, norms, weight):
    count, width = tokens.shape
    parts = len(grad_joined)
    blocks = count // SEQ // parts

    def kernel(*refs):
        gj_refs, (g_ref, x_ref, p_ref, w_ref, out_ref, terms_ref) = refs[:parts], refs[parts:]
        step = pl.program_id(0)

        @pl.when(step == 0)
        def _():
            terms_ref[...] = jnp.zeros_like(terms_ref)

        for n in range(parts):

            @pl.when(lax.div(step, blocks) == n)
            def _(n=n):
                grad_first = dot(gj_refs[n][...], w_ref[...], TRANSPOSED)
                part, gain, shift = norm_back(grad_first, wide(x_ref[...]), p_ref[0:1, :])
                terms_ref[0:1, :] += gain
                terms_ref[1:2, :] += shift
                out_ref[...] = g_ref[...] + part

    rows = pl.BlockSpec((SEQ, width), lambda r: (r, 0))

    def part_rows(n):
        return pl.BlockSpec(
            (SEQ, 3 * width), lambda r: (jnp.clip(r - n * blocks, 0, blocks - 1), 0)
        )

    return pl.pallas_call(
        kernel,
        grid=(count // SEQ,),
        out_shape=(shape_of((count, width), F32), shape_of((2, width), F32)),
        in_specs=[part_rows(n) for n in range(parts)] + [rows, rows, entire(norms), entire(weight)],
        out_specs=(rows, pl.BlockSpec((2, width), lambda r: (0, 0))),
        compiler_params=limits(60),
        cost_estimate=cost(6 * count * width * width, 16 * count * width + 6 * width * width),
    )(*grad_joined, grad_residual, tokens, norms, weight)


def weight_grad(grid, turned, grads, factor, lanes, across, offset, regions, region_lane, region_lanes):
    width, count = turned.shape
    parts = len(grads)
    share = count // parts
    columns = lanes * grid.shard
    region = shape_of((4 * grid.depth, width // grid.dp, region_lanes), BF16)

    def kernel(f_ref, t_hbm, *refs):
        near, far, turned_rows, grad, whole, sems, load_sems, row_sems = refs[parts + len(regions) :]
        loads = []
        for s in range(grid.shard):
            if s == 1:
                loads += start_copies([(t_hbm, turned_rows)], row_sems)
            pairs = []
            for n in range(parts):
                source = refs[n].at[:, pl.ds(s * across + offset, lanes)]
                pairs.append((source, grad.at[pl.ds(n * share, share), pl.ds(s * lanes, lanes)]))
            loads.append(start_copies(pairs, load_sems.at[pl.ds(s * parts, parts)]))
        loads = [loads[0], [loads[1]], *loads[2:]]
        for copy in loads[0] + loads[1] + loads[2]:
            copy.wait()
        half = columns // 2
        whole[:, :half] = thin(dot(turned_rows[...], grad[:, :half]) * f_ref[0, 0])
        for copies in loads[3:]:
            for copy in copies:
                copy.wait()
        whole[:, half:] = thin(dot(turned_rows[...], grad[:, half:]) * f_ref[0, 0])
        run_copies(block_stores(grid, whole, lanes, near, far, region_lane), sems)

    return pl.pallas_call(
        kernel,
        out_shape=(region, region),
        in_specs=[SCALAR] + [ANYWHERE] * (1 + parts + len(regions)),
        out_specs=(ANYWHERE,) * 2,
        scratch_shapes=[
            pltpu.VMEM((width, count), BF16),
            pltpu.VMEM((count, columns), BF16),
            pltpu.VMEM((width, columns), BF16),
            pltpu.SemaphoreType.DMA((grid.dp * grid.shard,)),
            pltpu.SemaphoreType.DMA((parts * grid.shard,)),
            pltpu.SemaphoreType.DMA((1,)),
        ],
        input_output_aliases={2 + parts + n: n for n in range(len(regions))},
        compiler_params=limits(60),
        cost_estimate=cost(
            2 * count * width * columns, 2 * (width * count + (width + count) * columns)
        ),
    )(factor, turned, *grads, *regions)


def adam_update(master, moment, square, gradient, rate):
    new_moment = BETA_FIRST * moment + (1.0 - BETA_FIRST) * gradient
    new_square = BETA_SECOND * square + (1.0 - BETA_SECOND) * gradient * gradient
    bias_first = 1.0 - BETA_FIRST**STEP
    bias_second = 1.0 - BETA_SECOND**STEP
    update = new_moment / bias_first / (jnp.sqrt(new_square / bias_second) + ADAM_EPSILON)
    new_master = master - rate * (update + WEIGHT_DECAY * master)
    return (new_master, new_moment, new_square)


def local(
    grid,
    tokens,
    cotangent,
    segment_ids,
    group_counts,
    master_qkv,
    master_out,
    master_up,
    master_down,
    moment_qkv,
    moment_out,
    moment_up,
    moment_down,
    square_qkv,
    square_out,
    square_up,
    square_down,
    norm_params,
    norm_moment,
    norm_square,
):
    rows, out_lanes = master_up.shape[0], master_out.shape[1]
    qkv_lanes = master_qkv.shape[1]
    chunks = master_down.shape[0] // rows
    up_lanes = master_up.shape[1] // chunks
    down_lanes = master_down.shape[1]
    per_shard = grid.dp // grid.shard
    blocks = tokens.shape[0] // SEQ
    both_lanes = up_lanes + down_lanes

    up_cut = thin(master_up).reshape(rows, per_shard, chunks, up_lanes // per_shard)
    down_cut = thin(master_down).reshape(chunks, rows, down_lanes)
    cuts = (qkv_lanes - out_lanes, out_lanes)

    def large(*members):
        parts = []
        for n in members:
            parts += [up_cut[:, :, n].reshape(rows, up_lanes), down_cut[n]]
        return jnp.concatenate(parts, axis=1)

    counts = group_counts.astype(F32)
    own_count = jnp.sum(jnp.where(jnp.arange(counts.shape[0]) == lax.axis_index("dp"), counts, 0.0))
    factor = own_count * counts.shape[0] / jnp.sum(counts)
    factor_cell = factor.reshape(1, 1)
    seg_column = segment_ids[:, None]
    seg_row = segment_ids.reshape(blocks, 1, SEQ)

    piece = jnp.concatenate([thin(master_qkv[:, cuts[0] :]), thin(master_out)], axis=1)
    q0 = grid.gather_z(thin(master_qkv[:, : cuts[0]]))
    q0, piece = tie(grid.both(q0), piece)
    q0_over = grid.gather_xy(q0)
    q1 = grid.gather_z(piece)
    q0_over, q1, piece = tie(q0_over, grid.both(q1), large(0, 1))
    q1_over = grid.gather_xy(q1)
    q0_far = grid.gather_far(q0_over)
    m01 = grid.gather_z(piece)
    q1_over, q0_far, m01, piece = tie(q1_over, q0_far, m01, large(2, 3))
    q0_pieces = grid.gather_end(q0, q0_over, q0_far)
    q1_far = grid.gather_far(q1_over)
    m01 = grid.both(m01)
    m23 = grid.z_exchange(grid.copies(piece))
    q1_far, m01 = tie(q1_far, m01)
    q1_pieces = grid.gather_end(q1, q1_over, q1_far)

    def halves(pair):
        lanes = [slice(n * both_lanes, (n + 1) * both_lanes) for n in range(2)]
        return [[values[:, :, own] for values in pair] for own in lanes]

    m0, m1 = halves(m01)

    q0_pieces, q1_pieces, m0 = tie(q0_pieces, q1_pieces, m0)
    first_turned, joined, qkv_weight = first_projection(
        grid, [q0_pieces, q1_pieces], cuts, tokens, norm_params
    )
    m0_over = grid.gather_xy_joined(m0)

    joined, m0_over, m1, m23 = tie(joined, m0_over, m1, m23)
    m2, m3 = halves(grid.both(m23))
    mixed_turned, logs, residual, second, second_turned = attention(
        grid, q1_pieces, cuts[1], joined, seg_column, seg_row, tokens, norm_params
    )
    m0_far = grid.gather_far_joined(m0_over)
    m1_over = grid.gather_xy_joined(m1)
    second, m0_far, m1_over, m2, m3 = tie(second, m0_far, m1_over, m2, m3)
    m0_pieces = grid.gather_end_joined(m0, m0_over, m0_far)

    def chunk(weights, sums, regions, place, turned):
        out_sum, back_sum, near, far = feed_forward(
            grid, weights, second, second_turned, cotangent, factor_cell, sums, regions,
            place * both_lanes, 2 * both_lanes, up_lanes, down_lanes, turned,
        )
        return (out_sum, back_sum), (near, far)

    second, m0_pieces, m1_over, m2 = tie(second, m0_pieces, m1_over, m2)
    sums, r0 = chunk(m0_pieces, (), (), 0, True)
    m1_far = grid.gather_far_joined(m1_over)
    m2_over = grid.gather_xy_joined(m2)
    sums, m1_far, m2_over = tie(sums, m1_far, m2_over)
    m1_pieces = grid.gather_end_joined(m1, m1_over, m1_far)

    sums, m1_pieces, m2_over, m3 = tie(sums, m1_pieces, m2_over, m3)
    sums, r0 = chunk(m1_pieces, sums, r0, 1, True)
    m2_far = grid.gather_far_joined(m2_over)
    m3_over = grid.gather_xy_joined(m3)
    sums, m2_far, m3_over = tie(sums, m2_far, m3_over)
    m2_pieces = grid.gather_end_joined(m2, m2_over, m2_far)

    sums, m2_pieces, r0, m3_over = tie(sums, m2_pieces, r0, m3_over)
    sums, r1 = chunk(m2_pieces, sums, (), 0, False)
    r0_other = grid.scatter_core(r0[1])
    m3_far = grid.gather_far_joined(m3_over)
    sums, m3_far, r0_other = tie(sums, m3_far, r0_other)
    m3_pieces = grid.gather_end_joined(m3, m3_over, m3_far)

    sums, r0_other, m3_pieces = tie(sums, r0_other, m3_pieces)
    sums, r1 = chunk(m3_pieces, sums, r1, 1, False)
    r0_far = grid.scatter_far(r0[0], r0_other)

    sums, r0_far, r1 = tie(sums, r0_far, r1)
    block_out, grad_residual, grad_attention, grad_mixed, second_terms = second_norm_back(
        grid, q1_pieces, cuts[1], sums, residual, cotangent, norm_params
    )
    r0_over = grid.scatter_xy(r0[0], r0_other, r0_far)
    r1_other = grid.scatter_core(r1[1])
    q1 = weight_grad(
        grid, mixed_turned, [grad_attention], factor_cell, out_lanes, out_lanes, 0,
        (), cuts[1], cuts[1] + out_lanes,
    )

    grad_mixed, r0_over, r1_other, q1 = tie(grad_mixed, r0_over, r1_other, q1)
    grad_joined = [attention_back(0, blocks // 2, joined, grad_mixed, logs, seg_column, seg_row)]
    r1_far = grid.scatter_far(r1[0], r1_other)
    r0_passed = grid.scatter_home(r0_over)
    grad_mixed, grad_joined, r1_far, r0_passed = tie(grad_mixed, grad_joined, r1_far, r0_passed)
    grad_joined.append(
        attention_back(blocks // 2, blocks // 2, joined, grad_mixed, logs, seg_column, seg_row)
    )
    r1_over = grid.scatter_xy(r1[0], r1_other, r1_far)
    r0_sent = grid.scatter_z(r0[0], r0_other, r0_over, r0_passed)
    q0 = weight_grad(
        grid, first_turned, grad_joined, factor_cell, cuts[0], qkv_lanes, 0, (), 0, cuts[0]
    )
    grad_joined, q0, r1_over, r0_sent = tie(grad_joined, q0, r1_over, r0_sent)
    q0_other = grid.scatter_core(q0[1])
    r1_passed = grid.scatter_home(r1_over)
    q1 = weight_grad(
        grid, first_turned, grad_joined, factor_cell, cuts[1], qkv_lanes, cuts[0],
        q1, 0, cuts[1] + out_lanes,
    )

    grad_joined, q0_other, q1, r1_passed = tie(grad_joined, q0_other, q1, r1_passed)
    q0_far = grid.scatter_far(q0[0], q0_other)
    q1_other = grid.scatter_core(q1[1])
    q0_far, q1_other = tie(q0_far, q1_other)
    q0_over = grid.scatter_xy(q0[0], q0_other, q0_far)
    q1_far = grid.scatter_far(q1[0], q1_other)
    r1_sent = grid.scatter_z(r1[0], r1_other, r1_over, r1_passed)
    input_grad, first_terms = first_norm_back(
        grad_joined, grad_residual, tokens, norm_params, qkv_weight
    )
    first_terms, q0_over, q1_far, r1_sent = tie(first_terms, q0_over, q1_far, r1_sent)
    q0_passed = grid.scatter_home(q0_over)
    q1_over = grid.scatter_xy(q1[0], q1_other, q1_far)
    q0_sent = grid.scatter_z(q0[0], q0_other, q0_over, q0_passed)
    terms = jnp.concatenate([first_terms, second_terms]) * factor
    terms = grid.total(terms, "shard")
    q1_over, q0_sent, terms = tie(q1_over, q0_sent, terms)
    q1_passed = grid.scatter_home(q1_over)
    q1_passed, q0_sent, r0_sent, r1_sent = tie(q1_passed, q0_sent, r0_sent, r1_sent)
    q1_sent = grid.scatter_z(q1[0], q1_other, q1_over, q1_passed)
    q0_total, q1_total = grid.scatter_end(q0_sent), grid.scatter_end(q1_sent)
    grad_qkv = jnp.concatenate([q0_total, q1_total[:, : cuts[1]]], axis=1)
    grad_out = q1_total[:, cuts[1] :]
    totals = [grid.scatter_end(r0_sent), grid.scatter_end(r1_sent)]
    terms, totals = tie(terms, totals)
    norm_grad = grid.total(terms, "dp")

    def pieces_of(first, lanes):
        return [
            t[:, i * both_lanes + first : i * both_lanes + first + lanes]
            for t in totals
            for i in range(chunks // 2)
        ]

    grad_up = jnp.stack(
        [piece.reshape(rows, per_shard, -1) for piece in pieces_of(0, up_lanes)], axis=2
    ).reshape(master_up.shape)
    grad_down = jnp.concatenate(pieces_of(up_lanes, down_lanes))
    new_qkv, new_moment_qkv, new_square_qkv = adam_update(
        master_qkv, moment_qkv, square_qkv, grad_qkv, RATE_MATRIX
    )
    new_out, new_moment_out, new_square_out = adam_update(
        master_out, moment_out, square_out, grad_out, RATE_OUTPUT
    )
    new_up, new_moment_up, new_square_up = adam_update(
        master_up, moment_up, square_up, grad_up, RATE_MATRIX
    )
    new_down, new_moment_down, new_square_down = adam_update(
        master_down, moment_down, square_down, grad_down, RATE_MATRIX
    )
    new_norm, new_norm_moment, new_norm_square = adam_update(
        norm_params, norm_moment, norm_square, norm_grad, RATE_NORMS
    )
    return (
        block_out,
        input_grad,
        grad_qkv,
        grad_out,
        grad_up,
        grad_down,
        new_qkv,
        new_out,
        new_up,
        new_down,
        new_moment_qkv,
        new_moment_out,
        new_moment_up,
        new_moment_down,
        new_square_qkv,
        new_square_out,
        new_square_up,
        new_square_down,
        thin(new_qkv),
        thin(new_out),
        thin(new_up),
        thin(new_down),
        norm_grad,
        new_norm,
        new_norm_moment,
        new_norm_square,
    )


def solution(mesh):
    rows = P(("dp", "shard"), None)
    owned = P("dp", "shard")
    in_specs = (rows, rows, P(("dp", "shard")), P()) + (owned,) * 12 + (P(),) * 3
    out_specs = (rows, rows) + (owned,) * 20 + (P(),) * 4
    step = functools.partial(local, Grid(mesh.shape["dp"], mesh.shape["shard"]))
    return jax.shard_map(step, mesh=mesh, in_specs=in_specs, out_specs=out_specs, check_vma=False)
```

```python
import functools
import math

import jax
import jax.numpy as jnp
from jax import lax
from jax.experimental import pallas as pl
from jax.experimental.pallas import tpu as pltpu
from jax.sharding import PartitionSpec as P

HEADS = 16
HD = 64
SEQ = 256
STEP = 3

NORM_EPSILON = 1e-06
BETA_FIRST = 0.5
BETA_SECOND = 0.5
ADAM_EPSILON = 1e-08
RATE_MATRIX = 0.02
RATE_OUTPUT = 0.1
RATE_NORMS = 0.3
WEIGHT_DECAY = 0.01
MASK_FILL = -1000000000.0
SCALING = 1.0 / math.sqrt(HD)
PLAIN = (((1,), (0,)), ((), ()))
TRANSPOSED = (((1,), (1,)), ((), ()))
LEADING = (((0,), (0,)), ((), ()))

F32 = jnp.float32
BF16 = jnp.bfloat16
MIB = 2**20


def dot(left, right, dims=PLAIN):
    return lax.dot_general(left, right, dims, preferred_element_type=F32)


def wide(values):
    return values.astype(F32)


def thin(values):
    return values.astype(BF16)


def shape_of(dims, dtype):
    return jax.ShapeDtypeStruct(dims, dtype)


def limits(mib):
    return pltpu.CompilerParams(vmem_limit_bytes=mib * MIB)


def cost(flops, moved, transcendentals=0):
    return pl.CostEstimate(flops=flops, bytes_accessed=moved, transcendentals=transcendentals)


def entire(array):
    return pl.BlockSpec(array.shape, lambda *_: (0,) * array.ndim)


class Grid:
    def __init__(self, dp, shard):
        self.dp, self.shard, self.depth = dp, shard, dp // 2

    def core_swap(self, values):
        return lax.ppermute(values, "shard", [(i, i ^ 1) for i in range(self.shard)])

    def cross(self, values, turned):
        pairs = []
        for d in range(self.dp):
            for s in range(self.shard):
                along_x = (s % 2 == 0) != turned
                other = (d ^ 1, s) if along_x else (d, s ^ 2)
                pairs.append((d * self.shard + s, other[0] * self.shard + other[1]))
        return lax.ppermute(values, ("dp", "shard"), pairs)

    def z_exchange(self, values):
        groups = [[z * 2 + x for z in range(self.depth)] for x in range(2)]
        return lax.all_to_all(values, "dp", 0, 0, axis_index_groups=groups, tiled=True)

    def total(self, values, axis):
        size = self.shard if axis == "shard" else self.dp
        for bit in range((size - 1).bit_length()):
            pairs = [(i, i ^ (1 << bit)) for i in range(size)]
            values = values + lax.ppermute(values, axis, pairs)
        return values


    def copies(self, piece):
        return jnp.broadcast_to(piece, (self.depth, *piece.shape))

    def gather_z(self, piece):
        parts = [piece]
        for k in range(1, self.depth):
            shift = [((i // 2 + k) % self.depth * 2 + i % 2, i) for i in range(self.dp)]
            parts.append(lax.ppermute(piece, "dp", shift))
        return jnp.stack(parts)

    def both(self, near):
        return near, self.core_swap(near)

    def gather_xy(self, near):
        return [self.cross(values, False) for values in near]

    def gather_far(self, over):
        return self.cross(over[0], True)

    def gather_end(self, near, over, far):
        mine = [*over, far]
        return [*near, *mine, *[self.core_swap(values) for values in mine]]


    def gather_xy_joined(self, near):
        return self.cross(jnp.concatenate(near), False)

    def gather_far_joined(self, over):
        return self.cross(over[: self.depth], True)

    def gather_end_joined(self, near, over, far):
        return [*near, over, far, self.core_swap(over), self.core_swap(far)]

    def owner(self, z, dx, dy, dc):
        index_dp, index_shard = lax.axis_index("dp"), lax.axis_index("shard")
        x, y, c = index_dp % 2, index_shard // 2, index_shard % 2
        row = z * 2 + lax.rem(x + dx, 2)
        column = lax.rem(y + dy, 2) * 2 + lax.rem(c + dc, 2)
        return row, column

    def gathered_places(self, turned, joined):
        where = (2, 2, 4, 4, 3, 5) if joined else (2, 3, 5, 6, 4, 7)
        skip = self.depth if joined else 0
        core = lax.rem(lax.axis_index("shard"), 2)
        own = lax.axis_index("dp") // 2
        places = []
        for k in range(self.depth):
            z = lax.rem(own + k, self.depth) if turned else k
            for side in range(2):
                places.append((side, k, self.owner(z, 0, 0, side)))
                beyond = side * skip + k
                places.append((where[side], beyond, self.owner(z, 1 - core, core, side)))
                places.append((where[2 + side], beyond, self.owner(z, core, 1 - core, 1 - side)))
            places.append((where[4], k, self.owner(z, 1, 1, 0)))
            places.append((where[5], k, self.owner(z, 1, 1, 1)))
        return places

    def region(self, other):
        core = lax.rem(lax.axis_index("shard"), 2)
        role = 1 - core if other else core
        flip = 1 if other else 0
        depth = range(self.depth)
        blocks = [self.owner(k, 1 - role, role, (flip + side) % 2) for side in range(2) for k in depth]
        blocks += [self.owner(k, 1, 1, flip) for k in depth]
        return blocks + [self.owner(k, 0, 0, flip) for k in depth]


    def scatter_core(self, far):
        return self.core_swap(far)

    def scatter_far(self, near, other):
        corner = slice(2 * self.depth, 3 * self.depth)
        return self.cross(thin(wide(near[corner]) + wide(other[corner])), True)

    def scatter_xy(self, near, other, far):
        d = self.depth
        first = wide(near[:d]) + wide(other[:d]) + wide(far)
        second = wide(near[d : 2 * d]) + wide(other[d : 2 * d])
        return [self.cross(thin(second), False), self.cross(thin(first), False)][::-1]

    def scatter_home(self, over):
        return self.core_swap(over[1])

    def scatter_z(self, near, other, over, passed):
        d = self.depth
        home = slice(3 * d, 4 * d)
        here = wide(near[home]) + wide(other[home]) + wide(over[0]) + wide(passed)
        return self.z_exchange(thin(here))

    def scatter_end(self, sent):
        return jnp.sum(wide(sent), axis=0)


def tie(*values):
    return lax.optimization_barrier(values)


def block(ref, row, rows, column, columns):
    return ref.at[
        pl.ds(pl.multiple_of(row, rows), rows), pl.ds(pl.multiple_of(column, columns), columns)
    ]


def start_copies(pairs, sems):
    copies = [pltpu.make_async_copy(a, b, sems.at[n]) for n, (a, b) in enumerate(pairs)]
    for copy in copies:
        copy.start()
    return copies


def run_copies(pairs, sems):
    for copy in start_copies(pairs, sems):
        copy.wait()


def piece_loads(grid, refs, lane, target, lanes, across, offset, turned=True):
    rows = target.shape[0] // grid.dp
    pairs = []
    for i, place, (row, column) in grid.gathered_places(turned, len(refs) == 6):
        source = refs[i].at[place, :, pl.ds(lane, lanes)]
        start = pl.multiple_of(column * across + offset, math.gcd(across, offset, lanes))
        held = pl.ds(pl.multiple_of(row * rows, rows), rows)
        pairs.append((source, target.at[held, pl.ds(start, lanes)]))
    return pairs


def block_stores(grid, source, lanes, near, far, lane):
    rows = source.shape[0] // grid.dp
    pairs = []
    for other in (1, 0):
        for n, (row, column) in enumerate(grid.region(other)):
            taken = block(source, row * rows, rows, column * lanes, lanes)
            pairs.append((taken, (near, far)[other].at[n, :, pl.ds(lane, lanes)]))
    return pairs


ANYWHERE = pl.BlockSpec(memory_space=pl.ANY)
SCALAR = pl.BlockSpec(memory_space=pltpu.SMEM)
HELD = pl.BlockSpec(memory_space=pltpu.VMEM)


def standardised(values):
    centred = values - jnp.mean(values, axis=-1, keepdims=True)
    inverse = lax.rsqrt(jnp.mean(centred * centred, axis=-1, keepdims=True) + NORM_EPSILON)
    return centred * inverse, inverse


def norm_back(grad, values, gain):
    n, inverse = standardised(values)
    scaled = grad * gain
    mean_scaled = jnp.mean(scaled, axis=-1, keepdims=True)
    mean_product = jnp.mean(scaled * n, axis=-1, keepdims=True)
    grad_values = inverse * (scaled - mean_scaled - n * mean_product)
    return (
        grad_values,
        jnp.sum(grad * n, axis=0, keepdims=True),
        jnp.sum(grad, axis=0, keepdims=True),
    )


def first_projection(grid, sets, cuts, tokens, norms):
    count, width = tokens.shape
    halves = len(sets)
    each = len(sets[0])
    across = sum(cuts)
    columns = across * grid.shard
    owners = grid.dp * grid.shard
    tile = width

    def kernel(x_ref, p_ref, *refs):
        sources, rest = refs[: halves * each], refs[halves * each :]
        turned_ref, joined_hbm, weight_hbm, weight, first, joined, sems, out_sems = rest
        pairs = []
        for n in range(halves):
            pieces = sources[n * each : (n + 1) * each]
            pairs += piece_loads(grid, pieces, 0, weight, cuts[n], across, sum(cuts[:n]))
        loads = start_copies(pairs, sems)

        @pl.loop(0, count, step=SEQ)
        def _(i):
            rows = pl.ds(pl.multiple_of(i, SEQ), SEQ)
            n, _ = standardised(wide(x_ref[rows, :]))
            value = thin(n * p_ref[0:1, :] + p_ref[1:2, :])
            first[rows, :] = value
            turned_ref[:, rows] = value.T

        for load in loads:
            load.wait()
        leaving = start_copies([(weight, weight_hbm)], out_sems)
        for n in range(columns // tile):
            own = slice(n * tile, (n + 1) * tile)
            joined[:, own] = thin(dot(first[...], weight[:, own]))
            pair = (joined.at[:, own], joined_hbm.at[:, own])
            leaving += start_copies([pair], out_sems.at[pl.ds(1 + n, 1)])
        for copy in leaving:
            copy.wait()

    return pl.pallas_call(
        kernel,
        out_shape=(
            shape_of((width, count), BF16),
            shape_of((count, columns), BF16),
            shape_of((width, columns), BF16),
        ),
        in_specs=[HELD, HELD] + [ANYWHERE] * (halves * each),
        out_specs=(HELD, ANYWHERE, ANYWHERE),
        scratch_shapes=[
            pltpu.VMEM((width, columns), BF16),
            pltpu.VMEM((count, width), BF16),
            pltpu.VMEM((count, columns), BF16),
            pltpu.SemaphoreType.DMA((halves * owners,)),
            pltpu.SemaphoreType.DMA((1 + columns // tile,)),
        ],
        compiler_params=limits(60),
        cost_estimate=cost(2 * count * width * columns, 4 * (width + count) * columns),
    )(tokens, norms, *[array for pieces in sets for array in pieces])


def attention(grid, pieces, lane, joined, seg_column, seg_row, tokens, norms):
    count, width = tokens.shape

    def kernel(
        j_ref, sc_ref, sr_ref, x_ref, p_ref, *refs,
    ):
        sources, rest = refs[: len(pieces)], refs[len(pieces) :]
        turned_ref, log_ref, res_ref, second_ref, second_turned_ref, mixed, weight, sems = rest
        lanes = width // grid.shard
        step = pl.program_id(0)

        @pl.when(step == 0)
        def _():
            start_copies(piece_loads(grid, sources, lane, weight, lanes, lanes, 0), sems)

        same = sc_ref[...] == sr_ref[0]
        left = lax.broadcasted_iota(jnp.int32, (SEQ, 2 * HD), 1) < HD
        for pair in range(HEADS // 2):
            a, b = pair * 2 * HD, (pair + 1) * 2 * HD
            query, key = j_ref[:, a:b], j_ref[:, width + a : width + b]
            value = j_ref[:, 2 * width + a : 2 * width + b]
            results = []
            for side in range(2):
                own_key = jnp.where(left == (side == 0), key, jnp.zeros_like(key))
                scores = jnp.where(same, dot(own_key, query, TRANSPOSED) * SCALING, MASK_FILL)
                top = jnp.max(scores, axis=0, keepdims=True)
                raised = jnp.exp(scores - top)
                total = jnp.sum(raised, axis=0, keepdims=True)
                head = 2 * pair + side
                log_ref[0, head : head + 1, :] = top + jnp.log(total)
                results.append(dot(thin(raised * (1.0 / total)), value, LEADING))
            mixed[:, a:b] = thin(jnp.where(left, results[0], results[1]))
        turned_ref[...] = mixed[...].T

        @pl.when(step == 0)
        def _():
            for n, (a, b) in enumerate(piece_loads(grid, sources, lane, weight, lanes, lanes, 0)):
                pltpu.make_async_copy(a, b, sems.at[n]).wait()

        residual = wide(x_ref[...]) + dot(mixed[...], weight[...])
        res_ref[...] = residual
        n, _ = standardised(residual)
        second = thin(n * p_ref[2:3, :] + p_ref[3:4, :])
        second_ref[...] = second
        second_turned_ref[...] = second.T

    blocks = count // SEQ

    def rows(columns):
        return pl.BlockSpec((SEQ, columns), lambda r: (r, 0))

    turned = pl.BlockSpec((width, SEQ), lambda r: (0, r))
    return pl.pallas_call(
        kernel,
        grid=(blocks,),
        out_shape=(
            shape_of((width, count), BF16),
            shape_of((blocks, HEADS, SEQ), F32),
            shape_of((count, width), F32),
            shape_of((count, width), BF16),
            shape_of((width, count), BF16),
        ),
        in_specs=[
            rows(3 * width),
            rows(1),
            pl.BlockSpec((1, 1, SEQ), lambda r: (r, 0, 0)),
            rows(width),
            entire(norms),
        ]
        + [ANYWHERE] * len(pieces),
        out_specs=(
            turned,
            pl.BlockSpec((1, HEADS, SEQ), lambda r: (r, 0, 0)),
            rows(width),
            rows(width),
            turned,
        ),
        scratch_shapes=[
            pltpu.VMEM((SEQ, width), BF16),
            pltpu.VMEM((width, width), BF16),
            pltpu.SemaphoreType.DMA((grid.dp * grid.shard,)),
        ],
        compiler_params=limits(60),
        cost_estimate=cost(
            4 * count * width * width + 16 * count * SEQ * width,
            20 * count * width,
            count * SEQ * HEADS,
        ),
    )(joined, seg_column, seg_row, tokens, norms, *pieces)


def gelu_and_slope(values):
    below = 0.5 * (1.0 + lax.erf(values * (1.0 / math.sqrt(2.0))))
    density = jnp.exp(-0.5 * values * values) * (1.0 / math.sqrt(2.0 * math.pi))
    return values * below, below + values * density


def feed_forward(grid, pieces, second, second_turned, cotangent, factor, sums, regions,
                 region_lane, region_lanes, up_lanes, down_lanes, turned):
    count, width = second.shape
    columns = up_lanes * grid.shard
    rows = width // grid.dp
    owners = grid.dp * grid.shard
    region = shape_of((4 * grid.depth, rows, region_lanes), BF16)
    used = len(pieces)

    def kernel(f_ref, s_hbm, st_hbm, c_hbm, *refs):
        sources, rest = refs[:used], refs[used:]
        if sums:
            out_in, back_in = rest[:2]
        (
            out_hbm, back_hbm, near, far, s_ref, st_ref, c_ref, up, down, out_sum, back_sum, hidden, grads,
            gu, gd, sems, sum_sems, row_sems,
        ) = rest[len(sums) + len(regions) :]
        up_sems, down_sems = sems.at[pl.ds(0, owners)], sems.at[pl.ds(owners, owners)]
        up_loads = start_copies([(s_hbm, s_ref)], row_sems.at[pl.ds(0, 1)])
        up_loads += start_copies(piece_loads(grid, sources, 0, up, up_lanes, up_lanes, 0, turned), up_sems)
        down_loads = start_copies([(c_hbm, c_ref)], row_sems.at[pl.ds(1, 1)])
        down_loads += start_copies(
            piece_loads(grid, sources, up_lanes, down, down_lanes, down_lanes, 0, turned), down_sems
        )
        if sums:
            arriving = start_copies([(out_in, out_sum), (back_in, back_sum)], sum_sems)
        turned_load = start_copies([(st_hbm, st_ref)], row_sems.at[pl.ds(2, 1)])
        for load in up_loads:
            load.wait()
        value, slope = gelu_and_slope(dot(s_ref[...], up[...]))
        for load in down_loads:
            load.wait()
        hidden[...] = thin(value)
        grads[...] = thin(dot(c_ref[...], down[...], TRANSPOSED) * slope)
        if sums:
            for copy in arriving:
                copy.wait()
            out_sum[...] += dot(hidden[...], down[...])
            back_sum[...] += dot(grads[...], up[...], TRANSPOSED)
        else:
            out_sum[...] = dot(hidden[...], down[...])
            back_sum[...] = dot(grads[...], up[...], TRANSPOSED)
        leaving = start_copies([(out_sum, out_hbm), (back_sum, back_hbm)], sum_sems)
        turned_load[0].wait()
        gu[...] = thin(dot(st_ref[...], grads[...]) * f_ref[0, 0])
        leaving += start_copies(block_stores(grid, gu, up_lanes, near, far, region_lane), up_sems)
        gd[...] = thin(dot(hidden[...], c_ref[...], LEADING) * f_ref[0, 0])
        leaving += start_copies(
            block_stores(grid, gd, down_lanes, near, far, region_lane + up_lanes), down_sems
        )
        for copy in leaving:
            copy.wait()

    aliases = {4 + used + n: n for n in range(len(sums))}
    aliases |= {4 + used + len(sums) + n: 2 + n for n in range(len(regions))}
    return pl.pallas_call(
        kernel,
        out_shape=(shape_of((count, width), F32),) * 2 + (region, region),
        in_specs=[SCALAR] + [ANYWHERE] * (3 + used + len(sums) + len(regions)),
        out_specs=(ANYWHERE,) * 4,
        scratch_shapes=[
            pltpu.VMEM((count, width), BF16),
            pltpu.VMEM((width, count), BF16),
            pltpu.VMEM((count, width), BF16),
            pltpu.VMEM((width, columns), BF16),
            pltpu.VMEM((columns, width), BF16),
            pltpu.VMEM((count, width), F32),
            pltpu.VMEM((count, width), F32),
            pltpu.VMEM((count, columns), BF16),
            pltpu.VMEM((count, columns), BF16),
            pltpu.VMEM((width, columns), BF16),
            pltpu.VMEM((columns, width), BF16),
            pltpu.SemaphoreType.DMA((2 * owners,)),
            pltpu.SemaphoreType.DMA((2,)),
            pltpu.SemaphoreType.DMA((3,)),
        ],
        input_output_aliases=aliases,
        compiler_params=limits(60),
        cost_estimate=cost(
            12 * count * width * columns,
            8 * width * columns + 22 * count * width,
            2 * count * columns,
        ),
    )(factor, second, second_turned, cotangent, *pieces, *sums, *regions)


def second_norm_back(grid, pieces, lane, sums, residual, cotangent, norms):
    out_sum, back_sum = sums
    count, width = residual.shape

    def kernel(o_ref, b_ref, res_ref, c_ref, p_ref, *refs):
        sources, rest = refs[: len(pieces)], refs[len(pieces) :]
        out_ref, grad_ref, ga_ref, gm_ref, terms_ref, weight, sems = rest
        lanes = width // grid.shard

        @pl.when(pl.program_id(0) == 0)
        def _():
            terms_ref[...] = jnp.zeros_like(terms_ref)
            run_copies(piece_loads(grid, sources, lane, weight, lanes, lanes, 0), sems)

        residual = res_ref[...]
        out_ref[...] = thin(residual + o_ref[...])
        part, gain, shift = norm_back(b_ref[...], residual, p_ref[2:3, :])
        terms_ref[0:1, :] += gain
        terms_ref[1:2, :] += shift
        grad = wide(c_ref[...]) + part
        grad_ref[...] = grad
        ga_ref[...] = thin(grad)
        gm_ref[...] = thin(dot(ga_ref[...], weight[...], TRANSPOSED))

    rows = pl.BlockSpec((SEQ, width), lambda r: (r, 0))
    return pl.pallas_call(
        kernel,
        grid=(count // SEQ,),
        out_shape=(
            shape_of((count, width), BF16),
            shape_of((count, width), F32),
            shape_of((count, width), BF16),
            shape_of((count, width), BF16),
            shape_of((2, width), F32),
        ),
        in_specs=[rows, rows, rows, rows, entire(norms)] + [ANYWHERE] * len(pieces),
        out_specs=(rows, rows, rows, rows, pl.BlockSpec((2, width), lambda r: (0, 0))),
        scratch_shapes=[
            pltpu.VMEM((width, width), BF16),
            pltpu.SemaphoreType.DMA((grid.dp * grid.shard,)),
        ],
        compiler_params=limits(60),
        cost_estimate=cost(2 * count * width * width, 24 * count * width),
    )(out_sum, back_sum, residual, cotangent, norms, *pieces)


def attention_back(first, blocks, joined, grad_mixed, logs, seg_column, seg_row):
    width = grad_mixed.shape[1]
    count = blocks * SEQ

    def kernel(j_ref, gm_ref, log_ref, sc_ref, sr_ref, gj_ref):
        same = sc_ref[...] == sr_ref[0]
        left = lax.broadcasted_iota(jnp.int32, (SEQ, 2 * HD), 1) < HD
        for pair in range(HEADS // 2):
            a, b = pair * 2 * HD, (pair + 1) * 2 * HD
            query, key = j_ref[:, a:b], j_ref[:, width + a : width + b]
            value, grad = j_ref[:, 2 * width + a : 2 * width + b], gm_ref[:, a:b]
            turned_key = key.T
            grad_query, results = [], []
            for side in range(2):
                chosen = left == (side == 0)
                own_key = jnp.where(chosen, key, jnp.zeros_like(key))
                own_value = jnp.where(chosen, value, jnp.zeros_like(value))
                scores = jnp.where(same, dot(own_key, query, TRANSPOSED) * SCALING, MASK_FILL)
                head = 2 * pair + side
                probs = jnp.exp(scores - log_ref[0, head : head + 1, :])
                grad_probs = dot(own_value, grad, TRANSPOSED)
                delta = jnp.sum(probs * grad_probs, axis=0, keepdims=True)
                grad_scores = thin(probs * (grad_probs - delta))
                grad_query.append(dot(turned_key[side * HD : (side + 1) * HD], grad_scores))
                results.append((dot(grad_scores, query) * SCALING, dot(thin(probs), grad)))
            gj_ref[:, a:b] = thin(jnp.concatenate(grad_query).T * SCALING)
            for n, (even, odd) in enumerate(zip(*results), 1):
                gj_ref[:, n * width + a : n * width + b] = thin(jnp.where(left, even, odd))

    def rows(columns):
        return pl.BlockSpec((SEQ, columns), lambda r: (r + first, 0))

    return pl.pallas_call(
        kernel,
        grid=(blocks,),
        out_shape=shape_of((count, 3 * width), BF16),
        in_specs=[
            rows(3 * width),
            rows(width),
            pl.BlockSpec((1, HEADS, SEQ), lambda r: (r + first, 0, 0)),
            rows(1),
            pl.BlockSpec((1, 1, SEQ), lambda r: (r + first, 0, 0)),
        ],
        out_specs=pl.BlockSpec((SEQ, 3 * width), lambda r: (r, 0)),
        compiler_params=limits(60),
        cost_estimate=cost(40 * count * SEQ * width, 14 * count * width, count * SEQ * HEADS),
    )(joined, grad_mixed, logs, seg_column, seg_row)


def first_norm_back(grad_joined, grad_residual, tokens, norms, weight):
    count, width = tokens.shape
    parts = len(grad_joined)
    blocks = count // SEQ // parts

    def kernel(*refs):
        gj_refs, (g_ref, x_ref, p_ref, w_ref, out_ref, terms_ref) = refs[:parts], refs[parts:]
        step = pl.program_id(0)

        @pl.when(step == 0)
        def _():
            terms_ref[...] = jnp.zeros_like(terms_ref)

        for n in range(parts):

            @pl.when(lax.div(step, blocks) == n)
            def _(n=n):
                grad_first = dot(gj_refs[n][...], w_ref[...], TRANSPOSED)
                part, gain, shift = norm_back(grad_first, wide(x_ref[...]), p_ref[0:1, :])
                terms_ref[0:1, :] += gain
                terms_ref[1:2, :] += shift
                out_ref[...] = g_ref[...] + part

    rows = pl.BlockSpec((SEQ, width), lambda r: (r, 0))

    def part_rows(n):
        return pl.BlockSpec(
            (SEQ, 3 * width), lambda r: (jnp.clip(r - n * blocks, 0, blocks - 1), 0)
        )

    return pl.pallas_call(
        kernel,
        grid=(count // SEQ,),
        out_shape=(shape_of((count, width), F32), shape_of((2, width), F32)),
        in_specs=[part_rows(n) for n in range(parts)] + [rows, rows, entire(norms), entire(weight)],
        out_specs=(rows, pl.BlockSpec((2, width), lambda r: (0, 0))),
        compiler_params=limits(60),
        cost_estimate=cost(6 * count * width * width, 16 * count * width + 6 * width * width),
    )(*grad_joined, grad_residual, tokens, norms, weight)


def weight_grad(grid, turned, grads, factor, lanes, across, offset, regions, region_lane, region_lanes):
    width, count = turned.shape
    parts = len(grads)
    share = count // parts
    columns = lanes * grid.shard
    region = shape_of((4 * grid.depth, width // grid.dp, region_lanes), BF16)

    def kernel(f_ref, t_hbm, *refs):
        near, far, turned_rows, grad, whole, sems, load_sems, row_sems = refs[parts + len(regions) :]
        loads = []
        for s in range(grid.shard):
            if s == 1:
                loads += start_copies([(t_hbm, turned_rows)], row_sems)
            pairs = []
            for n in range(parts):
                source = refs[n].at[:, pl.ds(s * across + offset, lanes)]
                pairs.append((source, grad.at[pl.ds(n * share, share), pl.ds(s * lanes, lanes)]))
            loads.append(start_copies(pairs, load_sems.at[pl.ds(s * parts, parts)]))
        loads = [loads[0], [loads[1]], *loads[2:]]
        for copy in loads[0] + loads[1] + loads[2]:
            copy.wait()
        half = columns // 2
        whole[:, :half] = thin(dot(turned_rows[...], grad[:, :half]) * f_ref[0, 0])
        for copies in loads[3:]:
            for copy in copies:
                copy.wait()
        whole[:, half:] = thin(dot(turned_rows[...], grad[:, half:]) * f_ref[0, 0])
        run_copies(block_stores(grid, whole, lanes, near, far, region_lane), sems)

    return pl.pallas_call(
        kernel,
        out_shape=(region, region),
        in_specs=[SCALAR] + [ANYWHERE] * (1 + parts + len(regions)),
        out_specs=(ANYWHERE,) * 2,
        scratch_shapes=[
            pltpu.VMEM((width, count), BF16),
            pltpu.VMEM((count, columns), BF16),
            pltpu.VMEM((width, columns), BF16),
            pltpu.SemaphoreType.DMA((grid.dp * grid.shard,)),
            pltpu.SemaphoreType.DMA((parts * grid.shard,)),
            pltpu.SemaphoreType.DMA((1,)),
        ],
        input_output_aliases={2 + parts + n: n for n in range(len(regions))},
        compiler_params=limits(60),
        cost_estimate=cost(
            2 * count * width * columns, 2 * (width * count + (width + count) * columns)
        ),
    )(factor, turned, *grads, *regions)


def adam_update(master, moment, square, gradient, rate):
    new_moment = BETA_FIRST * moment + (1.0 - BETA_FIRST) * gradient
    new_square = BETA_SECOND * square + (1.0 - BETA_SECOND) * gradient * gradient
    bias_first = 1.0 - BETA_FIRST**STEP
    bias_second = 1.0 - BETA_SECOND**STEP
    update = new_moment / bias_first / (jnp.sqrt(new_square / bias_second) + ADAM_EPSILON)
    new_master = master - rate * (update + WEIGHT_DECAY * master)
    return (new_master, new_moment, new_square)


def local(
    grid,
    tokens,
    cotangent,
    segment_ids,
    group_counts,
    master_qkv,
    master_out,
    master_up,
    master_down,
    moment_qkv,
    moment_out,
    moment_up,
    moment_down,
    square_qkv,
    square_out,
    square_up,
    square_down,
    norm_params,
    norm_moment,
    norm_square,
):
    rows, out_lanes = master_up.shape[0], master_out.shape[1]
    qkv_lanes = master_qkv.shape[1]
    chunks = master_down.shape[0] // rows
    up_lanes = master_up.shape[1] // chunks
    down_lanes = master_down.shape[1]
    per_shard = grid.dp // grid.shard
    blocks = tokens.shape[0] // SEQ
    both_lanes = up_lanes + down_lanes

    up_cut = thin(master_up).reshape(rows, per_shard, chunks, up_lanes // per_shard)
    down_cut = thin(master_down).reshape(chunks, rows, down_lanes)
    cuts = (qkv_lanes - out_lanes, out_lanes)

    def large(*members):
        parts = []
        for n in members:
            parts += [up_cut[:, :, n].reshape(rows, up_lanes), down_cut[n]]
        return jnp.concatenate(parts, axis=1)

    counts = group_counts.astype(F32)
    own_count = jnp.sum(jnp.where(jnp.arange(counts.shape[0]) == lax.axis_index("dp"), counts, 0.0))
    factor = own_count * counts.shape[0] / jnp.sum(counts)
    factor_cell = factor.reshape(1, 1)
    seg_column = segment_ids[:, None]
    seg_row = segment_ids.reshape(blocks, 1, SEQ)

    piece = jnp.concatenate([thin(master_qkv[:, cuts[0] :]), thin(master_out)], axis=1)
    q0 = grid.gather_z(thin(master_qkv[:, : cuts[0]]))
    q0, piece = tie(grid.both(q0), piece)
    q0_over = grid.gather_xy(q0)
    q1 = grid.gather_z(piece)
    q0_over, q1, piece = tie(q0_over, grid.both(q1), large(0, 1))
    q1_over = grid.gather_xy(q1)
    q0_far = grid.gather_far(q0_over)
    m01 = grid.gather_z(piece)
    q1_over, q0_far, m01, piece, seg_column = tie(
        q1_over, q0_far, m01, grid.copies(large(2, 3)), seg_column
    )
    q0_pieces = grid.gather_end(q0, q0_over, q0_far)
    q1_far = grid.gather_far(q1_over)
    m01 = grid.both(m01)
    m23 = grid.z_exchange(piece)
    q1_far, m01 = tie(q1_far, m01)
    q1_pieces = grid.gather_end(q1, q1_over, q1_far)

    def halves(pair):
        lanes = [slice(n * both_lanes, (n + 1) * both_lanes) for n in range(2)]
        return [[values[:, :, own] for values in pair] for own in lanes]

    m0, m1 = halves(m01)

    q0_pieces, q1_pieces, m0 = tie(q0_pieces, q1_pieces, m0)
    first_turned, joined, qkv_weight = first_projection(
        grid, [q0_pieces, q1_pieces], cuts, tokens, norm_params
    )
    m0_over = grid.gather_xy_joined(m0)

    joined, m0_over, m1, m23 = tie(joined, m0_over, m1, m23)
    m2, m3 = halves(grid.both(m23))
    mixed_turned, logs, residual, second, second_turned = attention(
        grid, q1_pieces, cuts[1], joined, seg_column, seg_row, tokens, norm_params
    )
    m0_far = grid.gather_far_joined(m0_over)
    m1_over = grid.gather_xy_joined(m1)
    second, m0_far, m1_over, m2, m3 = tie(second, m0_far, m1_over, m2, m3)
    m0_pieces = grid.gather_end_joined(m0, m0_over, m0_far)

    def chunk(weights, sums, regions, place, turned):
        out_sum, back_sum, near, far = feed_forward(
            grid, weights, second, second_turned, cotangent, factor_cell, sums, regions,
            place * both_lanes, 2 * both_lanes, up_lanes, down_lanes, turned,
        )
        return (out_sum, back_sum), (near, far)

    second, m0_pieces, m1_over, m2 = tie(second, m0_pieces, m1_over, m2)
    sums, r0 = chunk(m0_pieces, (), (), 0, True)
    m1_far = grid.gather_far_joined(m1_over)
    m2_over = grid.gather_xy_joined(m2)
    sums, m1_far, m2_over = tie(sums, m1_far, m2_over)
    m1_pieces = grid.gather_end_joined(m1, m1_over, m1_far)

    sums, m1_pieces, m2_over, m3 = tie(sums, m1_pieces, m2_over, m3)
    sums, r0 = chunk(m1_pieces, sums, r0, 1, True)
    m2_far = grid.gather_far_joined(m2_over)
    m3_over = grid.gather_xy_joined(m3)
    sums, m2_far, m3_over = tie(sums, m2_far, m3_over)
    m2_pieces = grid.gather_end_joined(m2, m2_over, m2_far)

    sums, m2_pieces, r0, m3_over = tie(sums, m2_pieces, r0, m3_over)
    sums, r1 = chunk(m2_pieces, sums, (), 0, False)
    r0_other = grid.scatter_core(r0[1])
    m3_far = grid.gather_far_joined(m3_over)
    sums, m3_far, r0_other = tie(sums, m3_far, r0_other)
    m3_pieces = grid.gather_end_joined(m3, m3_over, m3_far)

    sums, r0_other, m3_pieces = tie(sums, r0_other, m3_pieces)
    sums, r1 = chunk(m3_pieces, sums, r1, 1, False)
    r0_far = grid.scatter_far(r0[0], r0_other)

    sums, r0_far, r1 = tie(sums, r0_far, r1)
    block_out, grad_residual, grad_attention, grad_mixed, second_terms = second_norm_back(
        grid, q1_pieces, cuts[1], sums, residual, cotangent, norm_params
    )
    r0_over = grid.scatter_xy(r0[0], r0_other, r0_far)
    r1_other = grid.scatter_core(r1[1])
    q1 = weight_grad(
        grid, mixed_turned, [grad_attention], factor_cell, out_lanes, out_lanes, 0,
        (), cuts[1], cuts[1] + out_lanes,
    )

    grad_mixed, r0_over, r1_other, q1 = tie(grad_mixed, r0_over, r1_other, q1)
    grad_joined = [attention_back(0, blocks // 2, joined, grad_mixed, logs, seg_column, seg_row)]
    r1_far = grid.scatter_far(r1[0], r1_other)
    r0_passed = grid.scatter_home(r0_over)
    grad_mixed, grad_joined, r1_far, r0_passed = tie(grad_mixed, grad_joined, r1_far, r0_passed)
    grad_joined.append(
        attention_back(blocks // 2, blocks // 2, joined, grad_mixed, logs, seg_column, seg_row)
    )
    r1_over = grid.scatter_xy(r1[0], r1_other, r1_far)
    r0_sent = grid.scatter_z(r0[0], r0_other, r0_over, r0_passed)
    q0 = weight_grad(
        grid, first_turned, grad_joined, factor_cell, cuts[0], qkv_lanes, 0, (), 0, cuts[0]
    )
    grad_joined, q0, r1_over, r0_sent = tie(grad_joined, q0, r1_over, r0_sent)
    q0_other = grid.scatter_core(q0[1])
    r1_passed = grid.scatter_home(r1_over)
    q1 = weight_grad(
        grid, first_turned, grad_joined, factor_cell, cuts[1], qkv_lanes, cuts[0],
        q1, 0, cuts[1] + out_lanes,
    )

    grad_joined, q0_other, q1, r1_passed = tie(grad_joined, q0_other, q1, r1_passed)
    q0_far = grid.scatter_far(q0[0], q0_other)
    q1_other = grid.scatter_core(q1[1])
    q0_far, q1_other = tie(q0_far, q1_other)
    q0_over = grid.scatter_xy(q0[0], q0_other, q0_far)
    q1_far = grid.scatter_far(q1[0], q1_other)
    r1_sent = grid.scatter_z(r1[0], r1_other, r1_over, r1_passed)
    input_grad, first_terms = first_norm_back(
        grad_joined, grad_residual, tokens, norm_params, qkv_weight
    )
    first_terms, q0_over, q1_far, r1_sent = tie(first_terms, q0_over, q1_far, r1_sent)
    q0_passed = grid.scatter_home(q0_over)
    q1_over = grid.scatter_xy(q1[0], q1_other, q1_far)
    q0_sent = grid.scatter_z(q0[0], q0_other, q0_over, q0_passed)
    terms = jnp.concatenate([first_terms, second_terms]) * factor
    terms = grid.total(terms, "shard")
    q1_over, q0_sent, terms = tie(q1_over, q0_sent, terms)
    q1_passed = grid.scatter_home(q1_over)
    q1_passed, q0_sent, r0_sent, r1_sent = tie(q1_passed, q0_sent, r0_sent, r1_sent)
    q1_sent = grid.scatter_z(q1[0], q1_other, q1_over, q1_passed)
    q0_total, q1_total = grid.scatter_end(q0_sent), grid.scatter_end(q1_sent)
    grad_qkv = jnp.concatenate([q0_total, q1_total[:, : cuts[1]]], axis=1)
    grad_out = q1_total[:, cuts[1] :]
    totals = [grid.scatter_end(r0_sent), grid.scatter_end(r1_sent)]
    terms, totals = tie(terms, totals)
    norm_grad = grid.total(terms, "dp")

    def pieces_of(first, lanes):
        return [
            t[:, i * both_lanes + first : i * both_lanes + first + lanes]
            for t in totals
            for i in range(chunks // 2)
        ]

    grad_up = jnp.stack(
        [piece.reshape(rows, per_shard, -1) for piece in pieces_of(0, up_lanes)], axis=2
    ).reshape(master_up.shape)
    grad_down = jnp.concatenate(pieces_of(up_lanes, down_lanes))
    new_qkv, new_moment_qkv, new_square_qkv = adam_update(
        master_qkv, moment_qkv, square_qkv, grad_qkv, RATE_MATRIX
    )
    new_out, new_moment_out, new_square_out = adam_update(
        master_out, moment_out, square_out, grad_out, RATE_OUTPUT
    )
    new_up, new_moment_up, new_square_up = adam_update(
        master_up, moment_up, square_up, grad_up, RATE_MATRIX
    )
    new_down, new_moment_down, new_square_down = adam_update(
        master_down, moment_down, square_down, grad_down, RATE_MATRIX
    )
    new_norm, new_norm_moment, new_norm_square = adam_update(
        norm_params, norm_moment, norm_square, norm_grad, RATE_NORMS
    )
    return (
        block_out,
        input_grad,
        grad_qkv,
        grad_out,
        grad_up,
        grad_down,
        new_qkv,
        new_out,
        new_up,
        new_down,
        new_moment_qkv,
        new_moment_out,
        new_moment_up,
        new_moment_down,
        new_square_qkv,
        new_square_out,
        new_square_up,
        new_square_down,
        thin(new_qkv),
        thin(new_out),
        thin(new_up),
        thin(new_down),
        norm_grad,
        new_norm,
        new_norm_moment,
        new_norm_square,
    )


def solution(mesh):
    rows = P(("dp", "shard"), None)
    owned = P("dp", "shard")
    in_specs = (rows, rows, P(("dp", "shard")), P()) + (owned,) * 12 + (P(),) * 3
    out_specs = (rows, rows) + (owned,) * 20 + (P(),) * 4
    step = functools.partial(local, Grid(mesh.shape["dp"], mesh.shape["shard"]))
    return jax.shard_map(step, mesh=mesh, in_specs=in_specs, out_specs=out_specs, check_vma=False)
```
